256 devices in a mesh: ens: 4 (over z_lo, core), tile: 64 (over y, x, z_hi).
Axes of the slice: x: 4, y: 4, z: 8 (z_hi: 4, z_lo: 2; z = z_hi * 2 + z_lo), core: 2. Of those that a mesh axis runs over, the one named last changes fastest.
Arguments:
- inputs: bfloat16 [8, 12, 1024, 384], P('ens', None, 'tile'), may hold values from -6 to 6
- target: float32 [77, 12, 1024], P(None, None, 'tile'), may hold values from -6 to 6
- land_sea: int32 [12, 1024], P(None, 'tile'), may hold values from 0 to 1, as said below
- kernel: float32 [7, 7, 384], replicated, may hold values from -0.875 to 0.875
- norm_gain: float32 [384], replicated, may hold values from 0.5 to 1.5
- w_expand: bfloat16 [384, 1536], replicated, may hold values from -0.3125 to 0.3125
- w_reduce: bfloat16 [1536, 384], replicated, may hold values from -0.15625 to 0.15625
- head_weight: bfloat16 [384, 77], replicated, may hold values from -0.3125 to 0.3125
Outputs:
- grad_inputs: float32 [8, 12, 1024, 384], P('ens', None, 'tile')
- grad_kernel: float32 [7, 7, 384], replicated
- grad_gain: float32 [384], replicated
- grad_expand: float32 [384, 1536], replicated
- grad_reduce: float32 [1536, 384], replicated
- grad_head: float32 [384, 77], replicated
The draws below stay inside these ranges and needn't reach their ends.
Inputs may be any that keep to these rules, and one draw needn't show every extreme that they name: `land_sea`: number the tiles of 16 longitude cells k = 0 to 63 from west to east. Tile k holds between min(48 + 96 * k // 63, 144) and that bound plus 192 // 8 - 1 ocean cells, never more than 144; the easternmost tile holds exactly 144.
All inputs are finite; a program needn't handle non-finite values.
Results may differ from the reference program's by a relative error of at most 0.011.
Values may be sent and summed in bfloat16 or wider, within the bound.
A program may use at most 64 MiB of HBM per device.

```python
import jax
import jax.numpy as jnp
from jax import lax

D = 384
FFN = 1536
C_OUT = 77
KSIZE = 7
NLAT = 12
TLON = 16
MEMBERS = 8
NLON = 1024


def draw_land_sea(key, part):
    key = jax.random.fold_in(key, 7)
    tile_count = NLON // TLON
    tile_cells = NLAT * TLON
    rank_key, count_key = jax.random.split(key)
    position = jnp.arange(tile_count, dtype=jnp.int32)
    low_bound = tile_cells // 4 + tile_cells // 2 * position // max(tile_count - 1, 1)
    surplus = jax.random.randint(count_key, (tile_count,), 0, tile_cells // 8)
    ocean_counts = jnp.minimum(low_bound + surplus, 3 * tile_cells // 4)
    ocean_counts = jnp.where(position == tile_count - 1, 3 * tile_cells // 4, ocean_counts)
    scores = jax.random.randint(rank_key, (tile_count, tile_cells), 0, 1 << 30)
    ranking = jnp.argsort(jnp.argsort(scores, axis=1, stable=True), axis=1, stable=True)
    ocean_cells = (ranking < ocean_counts[:, None]).astype(jnp.int32)
    return ocean_cells.reshape(tile_count, NLAT, TLON).transpose(1, 0, 2).reshape(NLAT, NLON)


def block_scale(rng, dims, pieces, low, largest):
    def one(axis_at, shards_of):
        heights = jax.random.uniform(jax.random.fold_in(jax.random.fold_in(rng, 6), axis_at), (shards_of,), jnp.float32, low / len(pieces), largest / len(pieces))
        return jnp.repeat(jnp.exp(heights), dims[axis_at] // shards_of).reshape((-1,) + (1,) * (len(dims) - axis_at - 1))

    loudness = one(*pieces[0])
    for cut in pieces[1:]:
        loudness = loudness * one(*cut)
    return loudness


def scatter_about(key, shape, width, reach, cuts=(), kind=jnp.bfloat16):
    array = width * jax.random.normal(key, shape, jnp.float32)
    if cuts:
        array = array * block_scale(key, shape, cuts, -0.22, 0.18)
    return jnp.clip(array, -reach, reach).astype(kind)


def setup_inputs(seed: int = 0) -> dict:
    key_of = jax.random.split(jax.random.key(seed), 9)
    inputs = scatter_about(key_of[0], (MEMBERS, NLAT, NLON, D), 1.0, 6.0, ((0, 4), (2, 64)))
    target = scatter_about(key_of[1], (C_OUT, NLAT, NLON), 1.0, 6.0, ((2, 64),), jnp.float32)
    land_sea = draw_land_sea(jax.random.fold_in(key_of[8], 71), 0)
    kernel = scatter_about(key_of[3], (KSIZE, KSIZE, D), (KSIZE * KSIZE) ** -0.5, 0.875, (), jnp.float32)
    norm_gain = jnp.clip(1.0 + 0.1 * jax.random.normal(key_of[4], (D,), jnp.float32), 0.5, 1.5)
    w_expand = scatter_about(key_of[5], (D, FFN), D ** -0.5, 0.3125)
    w_reduce = scatter_about(key_of[6], (FFN, D), FFN ** -0.5, 0.15625)
    head_weight = scatter_about(key_of[7], (D, C_OUT), D ** -0.5, 0.3125)
    return dict(inputs=inputs, target=target, land_sea=land_sea, kernel=kernel, norm_gain=norm_gain, w_expand=w_expand, w_reduce=w_reduce, head_weight=head_weight)


FAIR_WEIGHT = 0.95
SMOOTHING = 0.5
NORM_EPS = 1e-06

def local_gradient(offset):
    return offset / jnp.sqrt(offset * offset + SMOOTHING * SMOOTHING)

def correlate(member_field, kernel):
    extent = kernel.shape[0]
    margin = extent // 2
    height, breadth = (member_field.shape[0], member_field.shape[1])
    padded_field = jnp.pad(member_field, ((margin, margin), (0, 0), (0, 0)))
    padded_field = jnp.concatenate([padded_field[:, breadth - margin:], padded_field, padded_field[:, :margin]], axis=1)
    result = jnp.zeros(member_field.shape, jnp.float32)
    for lat_step in range(extent):
        for lon_step in range(extent):
            result = result + padded_field[lat_step:lat_step + height, lon_step:lon_step + breadth] * kernel[lat_step, lon_step]
    return (result, padded_field)

def forward_member(member_input, kernel, norm_gain, w_expand, w_reduce, head_weight):
    channels = member_input.shape[-1]
    member_field = member_input.astype(jnp.float32)
    mixed_field, padded_field = correlate(member_field, kernel)
    rows_flat = mixed_field.reshape(-1, channels)
    centre = rows_flat - lax.optimization_barrier(jnp.mean(rows_flat, axis=-1, keepdims=True))
    reciprocal = lax.rsqrt(lax.optimization_barrier(jnp.mean(centre * centre, axis=-1, keepdims=True)) + NORM_EPS)
    standard_deviation = centre * reciprocal
    normalized = (standard_deviation * norm_gain).astype(jnp.bfloat16)
    prior_field = jnp.dot(normalized, w_expand, preferred_element_type=jnp.float32)
    hidden_state = jax.nn.gelu(prior_field).astype(jnp.bfloat16)
    summed = member_field.reshape(-1, channels) + jnp.dot(hidden_state, w_reduce, preferred_element_type=jnp.float32)
    block_result = summed.astype(jnp.bfloat16)
    prediction = jnp.dot(block_result, head_weight, preferred_element_type=jnp.float32)
    return (prediction, (padded_field, reciprocal, standard_deviation, normalized, prior_field, hidden_state, block_result))

def reference(inputs, target, land_sea, kernel, norm_gain, w_expand, w_reduce, head_weight):
    ensemble_members = inputs.shape[0]
    height, breadth, channels = (inputs.shape[1], inputs.shape[2], inputs.shape[3])
    output_fields = head_weight.shape[1]
    extent = kernel.shape[0]
    ocean_mask = land_sea.astype(jnp.float32).reshape(-1)
    observed_rows = jnp.transpose(target, (1, 2, 0)).reshape(-1, output_fields)

    def predict_fields(member_input):
        return forward_member(member_input, kernel, norm_gain, w_expand, w_reduce, head_weight)[0]
    predictions = lax.map(predict_fields, inputs)

    def member_gradient(prediction):
        ensemble_spread = lax.optimization_barrier(jnp.sum(local_gradient(prediction[None] - predictions), axis=0))
        self_term = local_gradient(prediction - observed_rows) / ensemble_members
        return (self_term - FAIR_WEIGHT / (ensemble_members * (ensemble_members - 1)) * ensemble_spread) * ocean_mask[:, None]
    local_gradients = lax.map(member_gradient, predictions)

    def member_back(running, member_item):
        g_kernel, g_gain, g_expand, g_reduce, g_head = running
        member_input, member_slopes = member_item
        _, saved_state = forward_member(member_input, kernel, norm_gain, w_expand, w_reduce, head_weight)
        padded_field, reciprocal, standard_deviation, normalized, prior_field, hidden_state, block_result = saved_state
        slopes_b = member_slopes.astype(jnp.bfloat16)
        g_head = g_head + jnp.dot(block_result.T, slopes_b, preferred_element_type=jnp.float32)
        d_block = jnp.dot(slopes_b, head_weight.T, preferred_element_type=jnp.float32)
        d_block_b = d_block.astype(jnp.bfloat16)
        g_reduce = g_reduce + jnp.dot(hidden_state.T, d_block_b, preferred_element_type=jnp.float32)
        d_hidden = jnp.dot(d_block_b, w_reduce.T, preferred_element_type=jnp.float32)
        _, pullback = jax.vjp(jax.nn.gelu, prior_field)
        d_before = pullback(d_hidden)[0].astype(jnp.bfloat16)
        g_expand = g_expand + jnp.dot(normalized.T, d_before, preferred_element_type=jnp.float32)
        d_normed = jnp.dot(d_before, w_expand.T, preferred_element_type=jnp.float32)
        g_gain = g_gain + lax.optimization_barrier(jnp.sum(d_normed * standard_deviation, axis=0))
        scaled = d_normed * norm_gain
        d_mixed = reciprocal * (scaled - lax.optimization_barrier(jnp.mean(scaled, axis=-1, keepdims=True)) - standard_deviation * lax.optimization_barrier(jnp.mean(scaled * standard_deviation, axis=-1, keepdims=True)))
        d_mixed = d_mixed.reshape(height, breadth, channels)
        kernel_terms = jnp.stack([jnp.stack([lax.optimization_barrier(jnp.sum(d_mixed * padded_field[lat_step:lat_step + height, lon_step:lon_step + breadth], axis=(0, 1))) for lon_step in range(extent)]) for lat_step in range(extent)])
        g_kernel = g_kernel + kernel_terms
        backward_field, _ = correlate(d_mixed, kernel[::-1, ::-1])
        grad_member = d_block.reshape(height, breadth, channels) + backward_field
        return ((g_kernel, g_gain, g_expand, g_reduce, g_head), grad_member)
    start = (jnp.zeros(kernel.shape, jnp.float32), jnp.zeros(norm_gain.shape, jnp.float32), jnp.zeros(w_expand.shape, jnp.float32), jnp.zeros(w_reduce.shape, jnp.float32), jnp.zeros(head_weight.shape, jnp.float32))
    running, grad_inputs = lax.scan(member_back, start, (inputs, local_gradients))
    g_kernel, g_gain, g_expand, g_reduce, g_head = running
    ocean_total = jnp.sum(ocean_mask)
    return (grad_inputs, g_kernel / ocean_total, g_gain / ocean_total, g_expand / ocean_total, g_reduce / ocean_total, g_head / ocean_total)
```

```python
import jax
import jax.numpy as jnp
from jax import lax
from jax.experimental import pallas as pl
from jax.experimental.pallas import tpu as pltpu
from jax.sharding import PartitionSpec as P

FAIR_WEIGHT = 0.95
SMOOTHING = 0.5
NORM_EPS = 1e-06
D = 384
FFN = 1536
LANES = 3
BLOCK = 512
BLOCKS = FFN // BLOCK
MEMBERS = 8
HALF = 2560
COUNT_BITS = 8
F32 = jnp.float32
BF16 = jnp.bfloat16


def grid_of(mesh):
    tiles = mesh.shape["tile"]
    side = 4 if tiles == 64 else 2
    return side, side, tiles // (side * side)


def dot(a, b, dims):
    return lax.dot_general(a, b, (dims, ((), ())), preferred_element_type=F32)


NN = ((1,), (0,))
NT = ((1,), (1,))
TN = ((0,), (0,))


class Place:
    def __init__(self, sizes):
        self.nx, self.ny, self.nzh = sizes
        self.nz = 2 * self.nzh
        self.tiles = self.nx * self.ny * self.nzh
        self.ens = lax.axis_index("ens")
        self.tile = lax.axis_index("tile")
        self.core = lax.rem(self.ens, 2)
        self.zl = lax.div(self.ens, 2)
        self.zh = lax.rem(self.tile, self.nzh)
        self.x = lax.rem(lax.div(self.tile, self.nzh), self.nx)
        self.y = lax.div(self.tile, self.nzh * self.nx)
        self.z = self.zh * 2 + self.zl

    def at(self, x, y, z, core):
        return (lax.rem(z, 2) * 2 + core, (y * self.nx + x) * self.nzh + lax.div(z, 2))

    def along_x(self, d):
        return self.at(lax.rem(self.x + d, self.nx), self.y, self.z, self.core)

    def along_y(self, d):
        return self.at(self.x, lax.rem(self.y + d, self.ny), self.z, self.core)

    def along_z(self, d):
        return self.at(self.x, self.y, lax.rem(self.z + d, self.nz), self.core)

    def other_core(self):
        return self.at(self.x, self.y, self.z, 1 - self.core)

    def along_tile(self, d):
        return (self.ens, lax.rem(self.tile + d + self.tiles, self.tiles))

    def along_ens(self, d):
        return (lax.rem(self.ens + d, 4), self.tile)

    def everyone(self):
        peers = [self.along_tile(1), self.along_tile(-1)]
        peers += [self.along_ens(d) for d in range(1, 4)]
        peers += [self.along_x(d) for d in range(1, self.nx)]
        peers += [self.along_y(d) for d in range(1, self.ny)]
        peers += [self.along_z(d) for d in range(1, self.nz)]
        return peers


def remote(src, dst, send, recv, to):
    return pltpu.make_async_remote_copy(
        src_ref=src,
        dst_ref=dst,
        send_sem=send,
        recv_sem=recv,
        device_id=to,
        device_id_type=pl.DeviceIdType.MESH,
    )


def chunks_of(rows, devices):
    tiles = rows // 16
    for each in range(1, tiles + 1):
        if tiles % each == 0 and tiles // each <= devices:
            return tiles // each, each * 16


class Reduce:
    def __init__(self, place, refs, out):
        self.p = place
        self.g, self.rc, self.s1, self.r1, self.s2, self.r2, self.sz, self.rz, self.oz, self.o, sems = refs
        self.out = out
        n = place.nx
        self.n, self.nz = n, place.nz
        self.c_rows = HALF // 2
        self.p_rows = self.c_rows // n
        self.q_rows = self.p_rows // n
        self.owners, self.z_rows = chunks_of(2 * self.q_rows, self.nz)
        self.send, self.recv = sems
        self.slots = 0
        self.pending = []

    def slot(self):
        self.slots += 1
        return self.slots - 1

    def copy(self, src, dst, to):
        s = self.slot()
        return remote(src, dst, self.send.at[s], self.recv.at[s], to)

    def first(self, h):
        return self.p.x if h == 0 else self.p.y

    def second(self, h):
        return self.p.y if h == 0 else self.p.x

    def to_first(self, h, d):
        return self.p.along_x(d) if h == 0 else self.p.along_y(d)

    def to_second(self, h, d):
        return self.p.along_y(d) if h == 0 else self.p.along_x(d)

    def rows(self, start, count):
        return pl.ds(pl.multiple_of(start, 16), count)

    def start_core(self):
        other = 1 - self.p.core
        self.core_copies = [
            self.copy(
                self.g.at[h, self.rows(other * self.c_rows, self.c_rows)], self.rc.at[h], self.p.other_core()
            )
            for h in range(2)
        ]
        for copy in self.core_copies:
            copy.start()

    def add(self, out, out_at, terms, count, step):
        def body(i, _):
            at = i * step
            total = None
            for ref, start in terms:
                part = ref[self.rows(start + at, step), :].astype(F32)
                total = part if total is None else total + part
            out[self.rows(out_at + at, step), :] = total.astype(BF16)
            return 0

        lax.fori_loop(0, count // step, body, 0)

    def core_to_first(self):
        mine = self.p.core * self.c_rows
        self.first_copies = []
        for h in range(2):
            self.core_copies[h].wait_recv()
            self.add(self.s1.at[h], 0, [(self.g.at[h], mine), (self.rc.at[h], 0)], self.c_rows, 160)
            for d in range(1, self.n):
                target = lax.rem(self.first(h) + d, self.n)
                copy = self.copy(
                    self.s1.at[h, self.rows(target * self.p_rows, self.p_rows)],
                    self.r1.at[h, d - 1],
                    self.to_first(h, d),
                )
                copy.start()
                self.first_copies.append(copy)

    def first_to_second(self):
        self.second_copies = []
        per = self.n - 1
        for h in range(2):
            for d in range(per):
                self.first_copies[h * per + d].wait_recv()
            terms = [(self.s1.at[h], self.first(h) * self.p_rows)]
            terms += [(self.r1.at[h, d], 0) for d in range(per)]
            self.add(self.s2.at[h], 0, terms, self.p_rows, 80)
            for d in range(1, self.n):
                target = lax.rem(self.second(h) + d, self.n)
                copy = self.copy(
                    self.s2.at[h, self.rows(target * self.q_rows, self.q_rows)],
                    self.r2.at[h, d - 1],
                    self.to_second(h, d),
                )
                copy.start()
                self.second_copies.append(copy)

    def second_to_z(self):
        per = self.n - 1
        for h in range(2):
            for d in range(per):
                self.second_copies[h * per + d].wait_recv()
            terms = [(self.s2.at[h], self.second(h) * self.q_rows)]
            terms += [(self.r2.at[h, d], 0) for d in range(per)]
            self.add(self.sz, h * self.q_rows, terms, self.q_rows, 80)
        self.z_copies = []
        for d in range(1, self.nz):
            target = lax.rem(self.p.z + d, self.nz)
            copy = self.copy(
                self.sz.at[self.rows(lax.rem(target, self.owners) * self.z_rows, self.z_rows)],
                self.rz.at[d - 1],
                self.p.along_z(d),
            )
            self.z_copies.append(copy)
            pl.when(target < self.owners)(copy.start)

    def z_to_gather(self):
        is_owner = self.p.z < self.owners
        at = lax.rem(self.p.z, self.owners) * self.z_rows
        base = self.slots
        self.slots += self.nz
        self.gather_copies = [
            remote(
                self.oz.at[self.rows(at, self.z_rows)],
                self.oz.at[self.rows(at, self.z_rows)],
                self.send.at[base + d],
                self.recv.at[base + self.p.z],
                self.p.along_z(d),
            )
            for d in range(1, self.nz)
        ]
        self.gather_waits = [
            remote(
                self.oz.at[pl.ds(k * self.z_rows, self.z_rows)],
                self.oz.at[pl.ds(k * self.z_rows, self.z_rows)],
                self.send.at[base],
                self.recv.at[base + k],
                self.p.along_z(1),
            )
            for k in range(self.owners)
        ]

        @pl.when(is_owner)
        def _():
            for copy in self.z_copies:
                copy.wait_recv()
            terms = [(self.sz, at)] + [(self.rz.at[d], 0) for d in range(self.nz - 1)]
            self.add(self.oz, at, terms, self.z_rows, self.z_rows)
            for copy in self.gather_copies:
                copy.start()

    def shard(self, h):
        return self.p.core * self.c_rows + self.first(h) * self.p_rows + self.second(h) * self.q_rows

    def gather_to_second(self):
        for k in range(self.owners):
            pl.when(self.p.z != k)(self.gather_waits[k].wait_recv)
        self.back_second = []
        for h in range(2):
            at = self.shard(h)
            for d in range(1, self.n):
                copy = self.copy(
                    self.oz.at[pl.ds(h * self.q_rows, self.q_rows)],
                    self.o.at[h, self.rows(at, self.q_rows)],
                    self.to_second(h, d),
                )
                copy.start()
                self.back_second.append(copy)
        for h in range(2):
            self.o[h, self.rows(self.shard(h), self.q_rows), :] = self.oz[
                h * self.q_rows : (h + 1) * self.q_rows, :
            ]

    def second_to_first(self):
        per = self.n - 1
        self.back_first = []
        for h in range(2):
            for d in range(per):
                self.back_second[h * per + d].wait_recv()
            at = self.p.core * self.c_rows + self.first(h) * self.p_rows
            for d in range(1, self.n):
                copy = self.copy(
                    self.o.at[h, self.rows(at, self.p_rows)],
                    self.o.at[h, self.rows(at, self.p_rows)],
                    self.to_first(h, d),
                )
                copy.start()
                self.back_first.append(copy)

    def first_to_core(self):
        per = self.n - 1
        self.back_core = []
        self.local = []
        for h in range(2):
            for d in range(per):
                self.back_first[h * per + d].wait_recv()
            at = self.rows(self.p.core * self.c_rows, self.c_rows)
            copy = self.copy(self.o.at[h, at], self.out.at[h, at], self.p.other_core())
            copy.start()
            self.back_core.append(copy)
            keep = pltpu.make_async_copy(self.o.at[h, at], self.out.at[h, at], self.send.at[self.slot()])
            keep.start()
            self.local.append(keep)

    def finish(self):
        for copy in self.back_core:
            copy.wait_recv()
        for copy in self.local:
            copy.wait()
        for copy in self.core_copies + self.first_copies + self.second_copies:
            copy.wait_send()
        for d in range(1, self.nz):
            target = lax.rem(self.p.z + d, self.nz)
            pl.when(target < self.owners)(self.z_copies[d - 1].wait_send)

        @pl.when(self.p.z < self.owners)
        def _():
            for copy in self.gather_copies:
                copy.wait_send()

        for copy in self.back_second + self.back_first + self.back_core:
            copy.wait_send()


def reduce_scratch(sizes):
    n, _, nzh = sizes
    nz = 2 * nzh
    c_rows = HALF // 2
    p_rows = c_rows // n
    q_rows = p_rows // n
    _, z_rows = chunks_of(2 * q_rows, nz)
    slots = 2 + 4 * (n - 1) + nz - 1 + nz + 4 * (n - 1) + 4
    return [
        pltpu.VMEM((2, HALF, 128), BF16),
        pltpu.VMEM((2, c_rows, 128), BF16),
        pltpu.VMEM((2, c_rows, 128), BF16),
        pltpu.VMEM((2, n - 1, p_rows, 128), BF16),
        pltpu.VMEM((2, p_rows, 128), BF16),
        pltpu.VMEM((2, n - 1, q_rows, 128), BF16),
        pltpu.VMEM((2 * q_rows, 128), BF16),
        pltpu.VMEM((nz - 1, z_rows, 128), BF16),
        pltpu.VMEM((2 * q_rows, 128), BF16),
        pltpu.VMEM((2, HALF, 128), BF16),
        (pltpu.SemaphoreType.DMA((slots,)), pltpu.SemaphoreType.DMA((slots,))),
    ]


def slope_of(offset):
    return offset * lax.rsqrt(offset * offset + SMOOTHING * SMOOTHING)


def put_main(batch, flat, value):
    count = value.shape[0]
    if flat < HALF:
        take = min(count, HALF - flat)
        batch[0, flat : flat + take, :] = value[:take].astype(BF16)
        if take < count:
            put_main(batch, HALF, value[take:])
        return
    for at in range(0, count, 64):
        shard = (flat - HALF + at) // 64
        batch[1, shard * 80 : shard * 80 + 64, :] = value[at : at + 64].astype(BF16)


def put_small(batch, index, value):
    batch[1, index * 80 + 64 : index * 80 + 80, :] = value.astype(BF16)


def work(sizes, *refs):
    (
        x_hbm, target_hbm, sea_hbm, kernel_hbm, gain_hbm, expand_hbm, reduce_hbm, head_hbm,
        out1, out2, direct_out,
        xb, tg, sea, taps, gain, we, wr, head,
        ext, dext, hs, hr, hs2, hr2, mixed, standard, recip, normed, before, slope, hidden, hidden_t, normed_t,
        block, head_t, fall, d_block, d_block_b, d_before, d_norm, gk,
        in_sems, halo_send, halo_recv, ens_send, ens_recv,
        *reduce_refs,
    ) = refs
    place = Place(sizes)
    pieces = len(reduce_refs) // 2
    first_refs = reduce_refs[: pieces - 2] + [tuple(reduce_refs[pieces - 2 : pieces])]
    second_refs = reduce_refs[pieces : 2 * pieces - 2] + [tuple(reduce_refs[2 * pieces - 2 :])]
    batch1 = Reduce(place, first_refs, out1)
    batch2 = Reduce(place, second_refs, out2)

    loads = [
        pltpu.make_async_copy(x_hbm.at[0, 0:8], xb.at[0:8], in_sems.at[0]),
        pltpu.make_async_copy(x_hbm.at[1, 0:8], xb.at[8:16], in_sems.at[1]),
        pltpu.make_async_copy(x_hbm.at[0, 8:12], xb.at[16:20], in_sems.at[2]),
        pltpu.make_async_copy(x_hbm.at[1, 8:12], xb.at[20:24], in_sems.at[3]),
    ]
    tap_loads = [
        pltpu.make_async_copy(kernel_hbm.at[:, :, l * 128 : (l + 1) * 128], taps.at[l], in_sems.at[4 + l])
        for l in range(LANES)
    ]
    later = [
        pltpu.make_async_copy(gain_hbm, gain, in_sems.at[7]),
        pltpu.make_async_copy(head_hbm, head, in_sems.at[8]),
        pltpu.make_async_copy(expand_hbm, we, in_sems.at[9]),
        pltpu.make_async_copy(reduce_hbm, wr, in_sems.at[10]),
        pltpu.make_async_copy(target_hbm, tg, in_sems.at[11]),
        pltpu.make_async_copy(sea_hbm, sea, in_sems.at[12]),
    ]
    for copy in loads + tap_loads + later:
        copy.start()

    barrier = pltpu.get_barrier_semaphore()
    peers = place.everyone()
    for peer in peers:
        pl.semaphore_signal(barrier, inc=1, device_id=peer, device_id_type=pl.DeviceIdType.MESH)

    def clear(i, _):
        l, m = lax.div(i, 2), lax.rem(i, 2)
        for ref in (ext, dext):
            ref[l, m, 0:3] = jnp.zeros((3, 32, 128), F32)
            ref[l, m, 15:18] = jnp.zeros((3, 32, 128), F32)
        return 0

    lax.fori_loop(0, 2 * LANES, clear, 0)
    gk[...] = jnp.zeros_like(gk)
    for copy in loads:
        copy.wait()
    for l in range(LANES):
        lanes = slice(l * 128, (l + 1) * 128)
        for m in range(2):
            ext[l, m, 3:11, 8:24, :] = xb[m * 8 : m * 8 + 8, :, lanes].astype(F32)
            ext[l, m, 11:15, 8:24, :] = xb[16 + m * 4 : 20 + m * 4, :, lanes].astype(F32)

    def pack(field, out):
        for side, col in ((0, 8), (1, 21)):
            for m in range(2):
                for j in range(3):
                    for l in range(LANES):
                        out[side, m * 3 + j, :, l * 128 : (l + 1) * 128] = field[l, m, 2:18, col + j, :].astype(BF16)

    def unpack(field, got):
        for side, col in ((0, 5), (1, 24)):
            for m in range(2):
                for j in range(3):
                    for l in range(LANES):
                        field[l, m, 2:18, col + j, :] = got[side, m * 3 + j, :, l * 128 : (l + 1) * 128].astype(F32)

    def halo(out, got, at):
        copies = [
            remote(out.at[0], got.at[1], halo_send.at[at], halo_recv.at[at], place.along_tile(-1)),
            remote(out.at[1], got.at[0], halo_send.at[at + 1], halo_recv.at[at + 1], place.along_tile(1)),
        ]
        for copy in copies:
            copy.start()
        return copies

    pack(ext, hs)
    pl.semaphore_wait(barrier, len(peers))
    halo1 = halo(hs, hr, 0)

    for copy in tap_loads + later:
        copy.wait()
    head_f = head[...].astype(F32).T
    head_t[...] = jnp.concatenate([head_f, jnp.zeros((80 - head_f.shape[0], D), F32)], axis=0).astype(BF16)
    for copy in halo1:
        copy.wait_recv()
    unpack(ext, hr)

    def correlate(field, l, m, flip):
        total = jnp.zeros((12, 16, 128), F32)
        for j in range(7):
            shifted = field[l, m, :, 5 + j : 21 + j, :]
            for i in range(7):
                tap = taps[l, 6 - i, 6 - j : 7 - j, :] if flip else taps[l, i, j : j + 1, :]
                total = total + shifted[i : i + 12] * tap
        return total

    def mix(i, _):
        l, m = lax.div(i, 2), lax.rem(i, 2)
        total = correlate(ext, l, m, False)
        mixed[l, pl.ds(m * 8, 8)] = total[:8]
        mixed[l, pl.ds(16 + m * 4, 4)] = total[8:]
        return 0

    lax.fori_loop(0, 2 * LANES, mix, 0)

    def norm(i, _):
        rows = pl.ds(pl.multiple_of(i * 64, 64), 64)
        parts = [mixed[l, pl.ds(i * 4, 4)].reshape(64, 128) for l in range(LANES)]
        mean = jnp.sum(parts[0] + parts[1] + parts[2], axis=-1, keepdims=True) / D
        centre = [part - mean for part in parts]
        square = centre[0] * centre[0] + centre[1] * centre[1] + centre[2] * centre[2]
        scale = lax.rsqrt(jnp.sum(square, axis=-1, keepdims=True) / D + NORM_EPS)
        recip[rows, :] = jnp.broadcast_to(scale, (64, 128))
        for l in range(LANES):
            lanes = slice(l * 128, (l + 1) * 128)
            value = centre[l] * scale
            standard[rows, lanes] = value
            normed[rows, lanes] = (value * gain[:, lanes]).astype(BF16)
        return 0

    lax.fori_loop(0, 6, norm, 0)

    total = xb[...].reshape(D, D).astype(F32)
    for b in range(BLOCKS):
        columns = slice(b * BLOCK, (b + 1) * BLOCK)
        before[...] = dot(normed[...], we[:, columns], NN)

        def gelu(i, _):
            rows = pl.ds(pl.multiple_of(i * 32, 32), 32)
            v = before[rows, :]
            square = v * v
            scale = 0.7978845608028654
            t = jnp.tanh(v * (scale + (scale * 0.044715) * square))
            half = 0.5 + 0.5 * t
            hidden[rows, columns] = (v * half).astype(BF16)
            slope[rows, columns] = half + (0.5 * v) * (1.0 - t * t) * (scale + (scale * 3 * 0.044715) * square)
            return 0

        lax.fori_loop(0, 12, gelu, 0)
        total = total + dot(hidden[:, columns], wr[columns, :], NN)
    block[...] = total.astype(BF16)

    own = dot(head_t[...], block[...], NT)
    fall[place.ens] = own
    ens_copies = [
        remote(fall.at[place.ens], fall.at[place.ens], ens_send.at[d], ens_recv.at[place.ens], place.along_ens(d))
        for d in range(1, 4)
    ]
    ens_waits = [
        remote(
            fall.at[lax.rem(place.ens + d, 4)],
            fall.at[lax.rem(place.ens + d, 4)],
            ens_send.at[0],
            ens_recv.at[lax.rem(place.ens + d, 4)],
            place.along_ens(d),
        )
        for d in range(1, 4)
    ]
    for copy in ens_copies:
        copy.start()
    normed_t[...] = normed[...].T
    for b in range(BLOCKS):
        hidden_t[b * BLOCK : (b + 1) * BLOCK, :] = hidden[:, b * BLOCK : (b + 1) * BLOCK].T
    for copy in ens_waits:
        copy.wait_recv()

    spread = jnp.zeros((80, D), F32)
    for s in range(4):
        theirs = fall[s]
        swapped = jnp.concatenate(
            [theirs[:, 128:256], theirs[:, 0:128], pltpu.roll(theirs[:, 256:384], 64, 1)], axis=1
        )
        spread = spread + slope_of(own - theirs) + slope_of(own - swapped)
    observed = jnp.concatenate([tg[:, 0:128], tg[:, 0:128], tg[:, 128:256]], axis=1)
    ocean = jnp.concatenate([sea[:, 0:128], sea[:, 0:128], sea[:, 128:256]], axis=1)[0:1]
    slopes = slope_of(own - observed) / MEMBERS - FAIR_WEIGHT / (MEMBERS * (MEMBERS - 1)) * spread
    slopes_b = (slopes * ocean).astype(BF16)

    grad_head = dot(slopes_b, block[...], NN)
    for r in range(5):
        for l in range(LANES):
            put_small(batch1.g, r * 3 + l, grad_head[r * 16 : r * 16 + 16, l * 128 : (l + 1) * 128])
    for index in range(15, 32):
        put_small(batch1.g, index, jnp.zeros((16, 128), F32))
    back = dot(slopes_b, head_t[...], TN)
    d_block[...] = back
    d_block_b[...] = back.astype(BF16)
    grad_reduce = dot(hidden_t[...], d_block_b[...], NN)
    for l in range(LANES):
        put_main(batch1.g, l * FFN, grad_reduce[:, l * 128 : (l + 1) * 128])
    batch1.start_core()

    d_normed = jnp.zeros((D, D), F32)
    for b in range(BLOCKS):
        columns = slice(b * BLOCK, (b + 1) * BLOCK)
        before[...] = dot(d_block_b[...], wr[columns, :], NT)

        def gate(i, _):
            rows = pl.ds(pl.multiple_of(i * 32, 32), 32)
            d_before[rows, :] = (before[rows, :] * slope[rows, columns]).astype(BF16)
            return 0

        lax.fori_loop(0, 12, gate, 0)
        grad_expand = dot(normed_t[...], d_before[...], NN)
        for l in range(BLOCK // 128):
            put_main(batch2.g, (b * (BLOCK // 128) + l) * D, grad_expand[:, l * 128 : (l + 1) * 128])
        d_normed = d_normed + dot(d_before[...], we[:, columns], NT)
        if b == 1:
            batch1.core_to_first()
    d_norm[...] = d_normed

    gk[0, 7:8, :] = jnp.zeros((1, 128), F32)

    def unnorm(i, _):
        rows = pl.ds(pl.multiple_of(i * 64, 64), 64)
        value = [d_norm[rows, l * 128 : (l + 1) * 128] for l in range(LANES)]
        std = [standard[rows, l * 128 : (l + 1) * 128] for l in range(LANES)]
        for l in range(LANES):
            gk[l, 7:8, :] += jnp.sum(value[l] * std[l], axis=0, keepdims=True)
        scaled = [value[l] * gain[:, l * 128 : (l + 1) * 128] for l in range(LANES)]
        mean = jnp.sum(scaled[0] + scaled[1] + scaled[2], axis=-1, keepdims=True) / D
        along = jnp.sum(scaled[0] * std[0] + scaled[1] * std[1] + scaled[2] * std[2], axis=-1, keepdims=True) / D
        for l in range(LANES):
            mixed[l, pl.ds(i * 4, 4)] = (recip[rows, :] * (scaled[l] - mean - std[l] * along)).reshape(4, 16, 128)
        return 0

    lax.fori_loop(0, 6, unnorm, 0)
    for l in range(LANES):
        for m in range(2):
            dext[l, m, 3:11, 8:24, :] = mixed[l, m * 8 : m * 8 + 8]
            dext[l, m, 11:15, 8:24, :] = mixed[l, 16 + m * 4 : 20 + m * 4]
    pack(dext, hs2)
    halo2 = halo(hs2, hr2, 2)
    batch1.first_to_second()

    def kernel_grad(l, _):
        for j in range(7):
            near = [ext[l, m, :, 5 + j : 21 + j, :] for m in range(2)]
            for i in range(7):
                part = jnp.zeros((16, 128), F32)
                for m in range(2):
                    part = part + jnp.sum(dext[l, m, 3:15, 8:24, :] * near[m][i : i + 12], axis=0)
                gk[l, i * 8 + j : i * 8 + j + 1, :] = jnp.sum(part, axis=0, keepdims=True)
        return 0

    lax.fori_loop(0, LANES, kernel_grad, 0)
    count = jnp.sum(sea[0:1, 0:192]).astype(jnp.int32)
    lane = lax.broadcasted_iota(jnp.int32, (1, 128), 1)
    bits = lax.bitwise_and(lax.shift_right_logical(jnp.broadcast_to(count, (1, 128)), jnp.minimum(lane, 31)), 1)
    gk[0, 15:16, :] = jnp.where(lane < COUNT_BITS, bits, 0).astype(F32)
    for r in range(4):
        for l in range(LANES):
            put_small(batch2.g, r * 3 + l, gk[l, r * 16 : r * 16 + 16, :])
    for index in range(12, 32):
        put_small(batch2.g, index, jnp.zeros((16, 128), F32))
    batch2.start_core()
    batch1.second_to_z()

    for copy in halo2:
        copy.wait_recv()
    unpack(dext, hr2)

    def mix_back(i, _):
        l, m = lax.div(i, 2), lax.rem(i, 2)
        mixed_back = correlate(dext, l, m, True)
        mixed[l, pl.ds(m * 8, 8)] = mixed_back[:8]
        mixed[l, pl.ds(16 + m * 4, 4)] = mixed_back[8:]
        return 0

    lax.fori_loop(0, 2, mix_back, 0)
    batch2.core_to_first()
    batch1.z_to_gather()
    lax.fori_loop(2, 4, mix_back, 0)
    batch1.gather_to_second()
    lax.fori_loop(4, 6, mix_back, 0)
    batch2.first_to_second()
    batch1.second_to_first()
    for l in range(LANES):
        lanes = slice(l * 128, (l + 1) * 128)
        mixed[l] = mixed[l] + d_block[:, lanes].reshape(24, 16, 128)
    direct = []
    for l in range(LANES):
        for m in range(2):
            lanes = slice(l * 128, (l + 1) * 128)
            at = (l * 2 + m) * 2
            direct.append(
                pltpu.make_async_copy(
                    mixed.at[l, m * 8 : m * 8 + 8], direct_out.at[m, 0:8, :, lanes], in_sems.at[at]
                )
            )
            direct.append(
                pltpu.make_async_copy(
                    mixed.at[l, 16 + m * 4 : 20 + m * 4], direct_out.at[m, 8:12, :, lanes], in_sems.at[at + 1]
                )
            )
    for copy in direct:
        copy.start()
    batch2.second_to_z()
    batch1.first_to_core()
    batch2.z_to_gather()
    batch2.gather_to_second()
    batch2.second_to_first()
    batch2.first_to_core()
    for copy in halo1 + halo2 + ens_copies:
        copy.wait_send()
    for copy in direct:
        copy.wait()
    batch1.finish()
    batch2.finish()


def finish(o1, o2, direct, g_inputs, g_kernel, g_gain, g_expand, g_reduce, g_head):
    def small(o, index):
        return o[1, index * 80 + 64 : index * 80 + 80, :].astype(F32)

    g_inputs[...] = direct[...]
    rows = [[small(o2, r * 3 + l) for l in range(LANES)] for r in range(4)]
    weight = lax.broadcasted_iota(jnp.int32, (1, 128), 1)
    weight = jnp.where(weight < COUNT_BITS, lax.shift_left(1, jnp.minimum(weight, 15)), 0).astype(F32)
    total = jnp.sum(rows[0][0][15:16] * weight, axis=-1, keepdims=True) / 4
    scale = 1.0 / total
    for l in range(LANES):
        lanes = slice(l * 128, (l + 1) * 128)
        for i in range(7):
            at = (i % 2) * 8
            g_kernel[i, :, lanes] = rows[i // 2][l][at : at + 7] * scale
        g_gain[:, lanes] = rows[0][l][7:8] * scale
    head = jnp.concatenate(
        [jnp.concatenate([small(o1, r * 3 + l) for l in range(LANES)], axis=1) for r in range(5)], axis=0
    )
    g_head[...] = (head * scale).T[:, : g_head.shape[1]]

    def main(o, flat, count):
        if flat < HALF:
            take = min(count, HALF - flat)
            yield 0, o[0, flat : flat + take, :]
            for at, rows in main(o, HALF, count - take) if take < count else ():
                yield take + at, rows
            return
        for at in range(0, count, 64):
            shard = (flat - HALF + at) // 64
            yield at, o[1, shard * 80 : shard * 80 + 64, :]

    for l in range(LANES):
        for at, rows in main(o1, l * FFN, FFN):
            g_reduce[at : at + rows.shape[0], l * 128 : (l + 1) * 128] = rows.astype(F32) * scale
    for l in range(FFN // 128):
        for at, rows in main(o2, l * D, D):
            g_expand[at : at + rows.shape[0], l * 128 : (l + 1) * 128] = rows.astype(F32) * scale


def on_device(sizes, inputs, target, land_sea, kernel, norm_gain, w_expand, w_reduce, head_weight):
    outputs = target.shape[0]
    observed = target.reshape(outputs, 192)
    observed = jnp.concatenate([observed, observed[:, 128:192]], axis=1)
    observed = jnp.pad(observed, ((0, 80 - outputs), (0, 0)))
    ocean = land_sea.reshape(1, 192).astype(F32)
    ocean = jnp.concatenate([ocean, ocean[:, 128:192]], axis=1)
    ocean = jnp.broadcast_to(ocean, (8, 256))
    anywhere = pl.BlockSpec(memory_space=pl.ANY)
    vmem = pltpu.VMEM
    scratch = [
        vmem((24, 16, D), BF16),
        vmem((80, 256), F32),
        vmem((8, 256), F32),
        vmem((LANES, 7, 7, 128), F32),
        vmem((1, D), F32),
        vmem((D, FFN), BF16),
        vmem((FFN, D), BF16),
        vmem((D, outputs), BF16),
        vmem((LANES, 2, 18, 32, 128), F32),
        vmem((LANES, 2, 18, 32, 128), F32),
        vmem((2, 6, 16, D), BF16),
        vmem((2, 6, 16, D), BF16),
        vmem((2, 6, 16, D), BF16),
        vmem((2, 6, 16, D), BF16),
        vmem((LANES, 24, 16, 128), F32),
        vmem((D, D), F32),
        vmem((D, 128), F32),
        vmem((D, D), BF16),
        vmem((D, BLOCK), F32),
        vmem((D, FFN), F32),
        vmem((D, FFN), BF16),
        vmem((FFN, D), BF16),
        vmem((D, D), BF16),
        vmem((D, D), BF16),
        vmem((80, D), BF16),
        vmem((4, 80, D), F32),
        vmem((D, D), F32),
        vmem((D, D), BF16),
        vmem((D, BLOCK), BF16),
        vmem((D, D), F32),
        vmem((LANES, 64, 128), F32),
        pltpu.SemaphoreType.DMA((13,)),
        pltpu.SemaphoreType.DMA((4,)),
        pltpu.SemaphoreType.DMA((4,)),
        pltpu.SemaphoreType.DMA((4,)),
        pltpu.SemaphoreType.DMA((4,)),
    ]
    batch = reduce_scratch(sizes)
    batch = batch[:-1] + list(batch[-1])
    scratch += batch + batch
    o1, o2, direct = pl.pallas_call(
        lambda *refs: work(sizes, *refs),
        out_shape=(
            jax.ShapeDtypeStruct((2, HALF, 128), BF16),
            jax.ShapeDtypeStruct((2, HALF, 128), BF16),
            jax.ShapeDtypeStruct(inputs.shape, F32),
        ),
        in_specs=[anywhere] * 8,
        out_specs=(anywhere,) * 3,
        scratch_shapes=scratch,
        compiler_params=pltpu.CompilerParams(
            collective_id=0, has_side_effects=True, vmem_limit_bytes=48 * 1024 * 1024
        ),
        name="block_pass",
    )(inputs, observed, ocean, kernel, norm_gain.reshape(1, D), w_expand, w_reduce, head_weight)
    g_inputs, g_kernel, g_gain, g_expand, g_reduce, g_head = pl.pallas_call(
        finish,
        out_shape=(
            jax.ShapeDtypeStruct(inputs.shape, F32),
            jax.ShapeDtypeStruct(kernel.shape, F32),
            jax.ShapeDtypeStruct((1, D), F32),
            jax.ShapeDtypeStruct(w_expand.shape, F32),
            jax.ShapeDtypeStruct(w_reduce.shape, F32),
            jax.ShapeDtypeStruct(head_weight.shape, F32),
        ),
        compiler_params=pltpu.CompilerParams(vmem_limit_bytes=32 * 1024 * 1024),
        name="finish",
    )(o1, o2, direct)
    return g_inputs, g_kernel, g_gain.reshape(D), g_expand, g_reduce, g_head


def solution(mesh):
    sizes = grid_of(mesh)
    return jax.shard_map(
        lambda *arrays: on_device(sizes, *arrays),
        mesh=mesh,
        in_specs=(
            P("ens", None, "tile", None),
            P(None, None, "tile"),
            P(None, "tile"),
            P(),
            P(),
            P(),
            P(),
            P(),
        ),
        out_specs=(P("ens", None, "tile", None), P(), P(), P(), P(), P()),
        check_vma=False,
    )
```

```python
import jax
import jax.numpy as jnp
from jax import lax
from jax.experimental import pallas as pl
from jax.experimental.pallas import tpu as pltpu
from jax.sharding import PartitionSpec as P

FAIR_WEIGHT = 0.95
SMOOTHING = 0.5
NORM_EPS = 1e-06
D = 384
FFN = 1536
LANES = 3
BLOCK = 512
BLOCKS = FFN // BLOCK
MEMBERS = 8
HALF = 2560
COUNT_BITS = 8
FEW = 96
F32 = jnp.float32
BF16 = jnp.bfloat16


def grid_of(mesh):
    tiles = mesh.shape["tile"]
    side = 4 if tiles == 64 else 2
    return side, side, tiles // (side * side)


def dot(a, b, dims):
    return lax.dot_general(a, b, (dims, ((), ())), preferred_element_type=F32)


NN = ((1,), (0,))
NT = ((1,), (1,))
TN = ((0,), (0,))


class Place:
    def __init__(self, sizes):
        self.nx, self.ny, self.nzh = sizes
        self.nz = 2 * self.nzh
        self.tiles = self.nx * self.ny * self.nzh
        self.ens = lax.axis_index("ens")
        self.tile = lax.axis_index("tile")
        self.core = lax.rem(self.ens, 2)
        self.zl = lax.div(self.ens, 2)
        self.zh = lax.rem(self.tile, self.nzh)
        self.x = lax.rem(lax.div(self.tile, self.nzh), self.nx)
        self.y = lax.div(self.tile, self.nzh * self.nx)
        self.z = self.zh * 2 + self.zl

    def at(self, x, y, z, core):
        return (lax.rem(z, 2) * 2 + core, (y * self.nx + x) * self.nzh + lax.div(z, 2))

    def along_x(self, d):
        return self.at(lax.rem(self.x + d, self.nx), self.y, self.z, self.core)

    def along_y(self, d):
        return self.at(self.x, lax.rem(self.y + d, self.ny), self.z, self.core)

    def along_z(self, d):
        return self.at(self.x, self.y, lax.rem(self.z + d, self.nz), self.core)

    def other_core(self):
        return self.at(self.x, self.y, self.z, 1 - self.core)

    def along_tile(self, d):
        return (self.ens, lax.rem(self.tile + d + self.tiles, self.tiles))

    def along_ens(self, d):
        return (lax.rem(self.ens + d, 4), self.tile)

    def everyone(self):
        peers = [self.along_tile(1), self.along_tile(-1)]
        peers += [self.along_ens(d) for d in range(1, 4)]
        peers += [self.along_x(d) for d in range(1, self.nx)]
        peers += [self.along_y(d) for d in range(1, self.ny)]
        peers += [self.along_z(d) for d in range(1, self.nz)]
        return peers


def remote(src, dst, send, recv, to):
    return pltpu.make_async_remote_copy(
        src_ref=src,
        dst_ref=dst,
        send_sem=send,
        recv_sem=recv,
        device_id=to,
        device_id_type=pl.DeviceIdType.MESH,
    )


def chunks_of(rows, devices):
    tiles = rows // 16
    for each in range(1, tiles + 1):
        if tiles % each == 0 and tiles // each <= devices:
            return tiles // each, each * 16


class Reduce:
    def __init__(self, place, refs, out):
        self.p = place
        self.g, self.rc, self.s1, self.r1, self.s2, self.r2, self.sz, self.rz, self.oz, sems = refs
        self.out = out
        n = place.nx
        self.n, self.nz = n, place.nz
        self.c_rows = HALF // 2
        self.p_rows = self.c_rows // n
        self.q_rows = self.p_rows // n
        self.owners, self.z_rows = chunks_of(2 * self.q_rows, self.nz)
        self.send, self.recv = sems
        self.slots = 0
        self.pending = []

    def slot(self):
        self.slots += 1
        return self.slots - 1

    def copy(self, src, dst, to):
        s = self.slot()
        return remote(src, dst, self.send.at[s], self.recv.at[s], to)

    def first(self, h):
        return self.p.x if h == 0 else self.p.y

    def second(self, h):
        return self.p.y if h == 0 else self.p.x

    def to_first(self, h, d):
        return self.p.along_x(d) if h == 0 else self.p.along_y(d)

    def to_second(self, h, d):
        return self.p.along_y(d) if h == 0 else self.p.along_x(d)

    def rows(self, start, count):
        return pl.ds(pl.multiple_of(start, 16), count)

    def pieces(self, h):
        return [lax.rem(self.first(h) + d, self.n) * self.p_rows for d in (*range(1, self.n), 0)]

    def start_core(self):
        other = 1 - self.p.core
        self.core_copies = [[], []]
        for k in range(self.n):
            for h in range(2):
                at = self.pieces(h)[k]
                copy = self.copy(
                    self.g.at[h, self.rows(other * self.c_rows + at, self.p_rows)],
                    self.rc.at[h, self.rows(at, self.p_rows)],
                    self.p.other_core(),
                )
                copy.start()
                self.core_copies[h].append(copy)

    def add(self, out, out_at, terms, count, step):
        def body(i, _):
            at = i * step
            total = None
            for ref, start in terms:
                part = ref[self.rows(start + at, step), :].astype(F32)
                total = part if total is None else total + part
            out[self.rows(out_at + at, step), :] = total.astype(BF16)
            return 0

        lax.fori_loop(0, count // step, body, 0)

    def core_to_first(self):
        mine = self.p.core * self.c_rows
        self.first_copies = [[], []]
        for k in range(self.n):
            for h in range(2):
                at = self.pieces(h)[k]
                self.core_copies[h][k].wait_recv()
                self.add(self.s1.at[h], at, [(self.g.at[h], mine + at), (self.rc.at[h], at)], self.p_rows, 80)
                if k == self.n - 1:
                    continue
                copy = self.copy(
                    self.s1.at[h, self.rows(at, self.p_rows)], self.r1.at[h, k], self.to_first(h, k + 1)
                )
                copy.start()
                self.first_copies[h].append(copy)

    def first_to_second(self):
        self.second_copies = []
        per = self.n - 1
        for h in range(2):
            for copy in self.first_copies[h]:
                copy.wait_recv()
            terms = [(self.s1.at[h], self.first(h) * self.p_rows)]
            terms += [(self.r1.at[h, d], 0) for d in range(per)]
            self.add(self.s2.at[h], 0, terms, self.p_rows, 80)
            for d in range(1, self.n):
                target = lax.rem(self.second(h) + d, self.n)
                copy = self.copy(
                    self.s2.at[h, self.rows(target * self.q_rows, self.q_rows)],
                    self.r2.at[h, d - 1],
                    self.to_second(h, d),
                )
                copy.start()
                self.second_copies.append(copy)

    def second_to_z(self):
        per = self.n - 1
        for h in range(2):
            for d in range(per):
                self.second_copies[h * per + d].wait_recv()
            terms = [(self.s2.at[h], self.second(h) * self.q_rows)]
            terms += [(self.r2.at[h, d], 0) for d in range(per)]
            self.add(self.sz, h * self.q_rows, terms, self.q_rows, 80)
        self.z_copies = []
        for d in range(1, self.nz):
            target = lax.rem(self.p.z + d, self.nz)
            copy = self.copy(
                self.sz.at[self.rows(lax.rem(target, self.owners) * self.z_rows, self.z_rows)],
                self.rz.at[d - 1],
                self.p.along_z(d),
            )
            self.z_copies.append(copy)
            pl.when(target < self.owners)(copy.start)

    def z_to_gather(self):
        is_owner = self.p.z < self.owners
        at = lax.rem(self.p.z, self.owners) * self.z_rows
        base = self.slots
        self.slots += self.nz
        self.gather_copies = [
            remote(
                self.oz.at[self.rows(at, self.z_rows)],
                self.oz.at[self.rows(at, self.z_rows)],
                self.send.at[base + d],
                self.recv.at[base + self.p.z],
                self.p.along_z(d),
            )
            for d in range(1, self.nz)
        ]
        self.gather_waits = [
            remote(
                self.oz.at[pl.ds(k * self.z_rows, self.z_rows)],
                self.oz.at[pl.ds(k * self.z_rows, self.z_rows)],
                self.send.at[base],
                self.recv.at[base + k],
                self.p.along_z(1),
            )
            for k in range(self.owners)
        ]

        @pl.when(is_owner)
        def _():
            for copy in self.z_copies:
                copy.wait_recv()
            terms = [(self.sz, at)] + [(self.rz.at[d], 0) for d in range(self.nz - 1)]
            self.add(self.oz, at, terms, self.z_rows, self.z_rows)
            for copy in self.gather_copies:
                copy.start()

    def shard(self, h):
        return self.p.core * self.c_rows + self.first(h) * self.p_rows + self.second(h) * self.q_rows

    def gather_to_second(self):
        for k in range(self.owners):
            pl.when(self.p.z != k)(self.gather_waits[k].wait_recv)
        self.back_second = []
        self.kept = []
        for h in range(2):
            at = self.rows(self.shard(h), self.q_rows)
            mine = self.oz.at[pl.ds(h * self.q_rows, self.q_rows)]
            for d in range(1, self.n):
                copy = self.copy(mine, self.out.at[h, at], self.to_second(h, d))
                copy.start()
                self.back_second.append(copy)
            keep = pltpu.make_async_copy(mine, self.out.at[h, at], self.send.at[self.slot()])
            keep.start()
            self.kept.append(keep)

    def piece(self, h, at):
        return self.out.at[h, self.rows(self.p.core * self.c_rows + at, self.p_rows)]

    def second_to_first(self):
        per = self.n - 1
        self.back_first = []
        self.back_core = []
        for h in range(2):
            for d in range(per):
                self.back_second[h * per + d].wait_recv()
            self.kept[h].wait()
            mine = self.piece(h, self.first(h) * self.p_rows)
            for d in range(1, self.n):
                copy = self.copy(mine, mine, self.to_first(h, d))
                copy.start()
                self.back_first.append(copy)
            copy = self.copy(mine, mine, self.p.other_core())
            copy.start()
            self.back_core.append(copy)

    def first_to_core(self):
        per = self.n - 1
        for d in sorted(range(1, self.n), key=lambda d: min(d, self.n - d)):
            for h in range(2):
                self.back_first[h * per + d - 1].wait_recv()
                came = self.piece(h, lax.rem(self.first(h) + self.n - d, self.n) * self.p_rows)
                copy = self.copy(came, came, self.p.other_core())
                copy.start()
                self.back_core.append(copy)

    def finish(self):
        for copy in self.back_core:
            copy.wait_recv()
        for copy in sum(self.core_copies + self.first_copies, []) + self.second_copies:
            copy.wait_send()
        for d in range(1, self.nz):
            target = lax.rem(self.p.z + d, self.nz)
            pl.when(target < self.owners)(self.z_copies[d - 1].wait_send)

        @pl.when(self.p.z < self.owners)
        def _():
            for copy in self.gather_copies:
                copy.wait_send()

        for copy in self.back_second + self.back_first + self.back_core:
            copy.wait_send()


class Few:
    def __init__(self, place, refs, out):
        self.p = place
        self.g, self.rc, self.sx, self.sy, self.sz, self.o, self.send, self.recv = refs
        self.out = out
        self.slots = 0
        self.copies = []

    def copy(self, src, dst, to):
        s = self.slots
        self.slots += 1
        copy = remote(src, dst, self.send.at[s], self.recv.at[s], to)
        copy.start()
        self.copies.append(copy)
        return copy

    def start(self):
        self.got = [self.copy(self.g.at[1 - self.p.core], self.rc, self.p.other_core())]

    def spread(self, value, slots, at, along, size):
        for copy in self.got:
            copy.wait_recv()
        slots[at] = value().astype(BF16)
        self.got = [self.copy(slots.at[at], slots.at[at], along(d)) for d in range(1, size)]

    def total(self, slots, size):
        value = slots[0].astype(F32)
        for s in range(1, size):
            value = value + slots[s].astype(F32)
        return value

    def to_x(self):
        p = self.p
        self.spread(lambda: self.g[p.core].astype(F32) + self.rc[...].astype(F32), self.sx, p.x, p.along_x, p.nx)

    def to_y(self):
        p = self.p
        self.spread(lambda: self.total(self.sx, p.nx), self.sy, p.y, p.along_y, p.ny)

    def to_z(self):
        p = self.p
        self.spread(lambda: self.total(self.sy, p.ny), self.sz, p.z, p.along_z, p.nz)

    def to_core(self):
        for copy in self.got:
            copy.wait_recv()
        self.o[...] = self.total(self.sz, self.p.nz).astype(BF16)
        self.keep = pltpu.make_async_copy(self.o, self.out.at[self.p.core], self.send.at[self.slots])
        self.slots += 1
        self.keep.start()
        self.got = [self.copy(self.o, self.out.at[self.p.core], self.p.other_core())]

    def finish(self):
        self.got[0].wait_recv()
        self.keep.wait()
        for copy in self.copies:
            copy.wait_send()


def reduce_scratch(sizes):
    n, _, nzh = sizes
    nz = 2 * nzh
    c_rows = HALF // 2
    p_rows = c_rows // n
    q_rows = p_rows // n
    _, z_rows = chunks_of(2 * q_rows, nz)
    slots = 2 * n + 4 * (n - 1) + nz - 1 + nz + 2 * (n - 1) + 2 + 2 * (n - 1) + 2 * n
    return [
        pltpu.VMEM((2, HALF, 128), BF16),
        pltpu.VMEM((2, c_rows, 128), BF16),
        pltpu.VMEM((2, c_rows, 128), BF16),
        pltpu.VMEM((2, n - 1, p_rows, 128), BF16),
        pltpu.VMEM((2, p_rows, 128), BF16),
        pltpu.VMEM((2, n - 1, q_rows, 128), BF16),
        pltpu.VMEM((2 * q_rows, 128), BF16),
        pltpu.VMEM((nz - 1, z_rows, 128), BF16),
        pltpu.VMEM((2 * q_rows, 128), BF16),
        (pltpu.SemaphoreType.DMA((slots,)), pltpu.SemaphoreType.DMA((slots,))),
    ]


def slope_of(offset):
    return offset * lax.rsqrt(offset * offset + SMOOTHING * SMOOTHING)


def put_main(batch, flat, value):
    count = value.shape[0]
    if flat < HALF:
        take = min(count, HALF - flat)
        batch[0, flat : flat + take, :] = value[:take].astype(BF16)
        if take < count:
            put_main(batch, HALF, value[take:])
        return
    for at in range(0, count, 64):
        shard = (flat - HALF + at) // 64
        batch[1, shard * 80 : shard * 80 + 64, :] = value[at : at + 64].astype(BF16)


def put_small(batch, index, value):
    batch[1, index * 80 + 64 : index * 80 + 80, :] = value.astype(BF16)


def put_few(batch, index, value):
    batch[index // 6, index % 6 * 16 : index % 6 * 16 + 16, :] = value.astype(BF16)


def work(sizes, *refs):
    (
        x_hbm, target_hbm, sea_hbm, kernel_hbm, gain_hbm, expand_hbm, reduce_hbm, head_hbm,
        out1, out2, out3, direct_out,
        xb, target, tall, tg, sea, taps, gain, we, wr, head,
        ext, dext, rim, hs, hr, hs2, hr2, mixed, standard, recip, normed, before, slope, hidden, hidden_t, normed_t,
        block, head_t, fall, d_block, d_block_b, d_before, d_norm, gk,
        in_sems, halo_send, halo_recv, ens_send, ens_recv,
        *rest,
    ) = refs
    place = Place(sizes)
    few = Few(place, rest[-8:], out3)
    pieces = (len(rest) - 8) // 2
    batch1, batch2 = (
        Reduce(place, [*mine[:-2], mine[-2:]], out)
        for mine, out in ((rest[:pieces], out1), (rest[pieces : 2 * pieces], out2))
    )

    loads = [
        pltpu.make_async_copy(x_hbm.at[0, 0:8], xb.at[0:8], in_sems.at[0]),
        pltpu.make_async_copy(x_hbm.at[1, 0:8], xb.at[8:16], in_sems.at[1]),
        pltpu.make_async_copy(x_hbm.at[0, 8:12], xb.at[16:20], in_sems.at[2]),
        pltpu.make_async_copy(x_hbm.at[1, 8:12], xb.at[20:24], in_sems.at[3]),
    ]
    tap_loads = [
        pltpu.make_async_copy(kernel_hbm.at[:, :, l * 128 : (l + 1) * 128], taps.at[l], in_sems.at[4 + l])
        for l in range(LANES)
    ]
    later = [
        pltpu.make_async_copy(gain_hbm, gain, in_sems.at[7]),
        pltpu.make_async_copy(head_hbm, head, in_sems.at[8]),
        pltpu.make_async_copy(expand_hbm, we, in_sems.at[9]),
        pltpu.make_async_copy(reduce_hbm, wr, in_sems.at[10]),
        pltpu.make_async_copy(target_hbm, target, in_sems.at[11]),
        pltpu.make_async_copy(sea_hbm, sea, in_sems.at[12]),
    ]
    for copy in loads + tap_loads + later:
        copy.start()

    barrier = pltpu.get_barrier_semaphore()
    peers = place.everyone()
    for peer in peers:
        pl.semaphore_signal(barrier, inc=1, device_id=peer, device_id_type=pl.DeviceIdType.MESH)

    def clear(i, _):
        l, m = lax.div(i, 2), lax.rem(i, 2)
        for ref in (ext, dext):
            ref[l, m, 0:3] = jnp.zeros((3, 32, 128), F32)
            ref[l, m, 15:18] = jnp.zeros((3, 32, 128), F32)
        return 0

    lax.fori_loop(0, 2 * LANES, clear, 0)
    gk[...] = jnp.zeros_like(gk)
    rim[...] = jnp.zeros_like(rim)
    for copy in loads:
        copy.wait()
    for l in range(LANES):
        lanes = slice(l * 128, (l + 1) * 128)
        for m in range(2):
            ext[l, m, 3:11, 8:24, :] = xb[m * 8 : m * 8 + 8, :, lanes].astype(F32)
            ext[l, m, 11:15, 8:24, :] = xb[16 + m * 4 : 20 + m * 4, :, lanes].astype(F32)

    def pack(field, out):
        for side, col in ((0, 8), (1, 21)):
            for m in range(2):
                for j in range(3):
                    for l in range(LANES):
                        rows = slice((m * 3 + j) * 12, (m * 3 + j) * 12 + 12)
                        rim[side, rows, l * 128 : (l + 1) * 128] = field[l, m, 3:15, col + j, :]
        out[...] = rim[...].astype(BF16)

    def unpack(field, got):
        rim[...] = got[...].astype(F32)
        for side, col in ((0, 5), (1, 24)):
            for m in range(2):
                for j in range(3):
                    for l in range(LANES):
                        rows = slice((m * 3 + j) * 12, (m * 3 + j) * 12 + 12)
                        field[l, m, 3:15, col + j, :] = rim[side, rows, l * 128 : (l + 1) * 128]

    def halo(out, got, at):
        copies = [
            remote(out.at[0], got.at[1], halo_send.at[at], halo_recv.at[at], place.along_tile(-1)),
            remote(out.at[1], got.at[0], halo_send.at[at + 1], halo_recv.at[at + 1], place.along_tile(1)),
        ]
        for copy in copies:
            copy.start()
        return copies

    pack(ext, hs)
    pl.semaphore_wait(barrier, len(peers))
    halo1 = halo(hs, hr, 0)

    for copy in tap_loads + later:
        copy.wait()
    outputs = head.shape[0]
    head_t[...] = jnp.concatenate([head[...].astype(F32), jnp.zeros((80 - outputs, D), F32)], axis=0).astype(BF16)
    diagonal = lax.broadcasted_iota(jnp.int32, (16, 16), 0) == lax.broadcasted_iota(jnp.int32, (16, 16), 1)
    tall[...] = jnp.zeros_like(tall)
    for a in range(12):
        water = jnp.broadcast_to(sea[a : a + 1, :].astype(F32), (16, 16))
        water = jnp.sum(jnp.where(diagonal, water, 0.0), axis=1, keepdims=True)
        for at in (a * 16,) if a < 8 else (a * 16, a * 16 + 64):
            tall[at : at + 16, 0:outputs] = target[a]
            tall[at : at + 16, outputs : outputs + 1] = water
    tg[...] = tall[...].T[0:80]
    for copy in halo1:
        copy.wait_recv()
    unpack(ext, hr)

    def correlate(field, l, m, flip):
        total = jnp.zeros((12, 16, 128), F32)
        for j in range(7):
            shifted = field[l, m, :, 5 + j : 21 + j, :]
            for i in range(7):
                tap = taps[l, 6 - i, 6 - j : 7 - j, :] if flip else taps[l, i, j : j + 1, :]
                total = total + shifted[i : i + 12] * tap
        return total

    def mix(i, _):
        l, m = lax.div(i, 2), lax.rem(i, 2)
        total = correlate(ext, l, m, False)
        mixed[l, pl.ds(m * 8, 8)] = total[:8]
        mixed[l, pl.ds(16 + m * 4, 4)] = total[8:]
        return 0

    lax.fori_loop(0, 2 * LANES, mix, 0)

    gain_row = gain[...].reshape(1, D)

    def norm(i, _):
        rows = pl.ds(pl.multiple_of(i * 64, 64), 64)
        parts = [mixed[l, pl.ds(i * 4, 4)].reshape(64, 128) for l in range(LANES)]
        mean = jnp.sum(parts[0] + parts[1] + parts[2], axis=-1, keepdims=True) / D
        centre = [part - mean for part in parts]
        square = centre[0] * centre[0] + centre[1] * centre[1] + centre[2] * centre[2]
        scale = lax.rsqrt(jnp.sum(square, axis=-1, keepdims=True) / D + NORM_EPS)
        recip[rows, :] = jnp.broadcast_to(scale, (64, 128))
        for l in range(LANES):
            lanes = slice(l * 128, (l + 1) * 128)
            value = centre[l] * scale
            standard[rows, lanes] = value
            normed[rows, lanes] = (value * gain_row[:, lanes]).astype(BF16)
        return 0

    lax.fori_loop(0, 6, norm, 0)

    total = xb[...].reshape(D, D).astype(F32)
    for b in range(BLOCKS):
        columns = slice(b * BLOCK, (b + 1) * BLOCK)
        before[...] = dot(normed[...], we[:, columns], NN)

        def gelu(i, _):
            rows = pl.ds(pl.multiple_of(i * 32, 32), 32)
            v = before[rows, :]
            square = v * v
            scale = 0.7978845608028654
            t = jnp.tanh(v * (scale + (scale * 0.044715) * square))
            half = 0.5 + 0.5 * t
            hidden[rows, columns] = (v * half).astype(BF16)
            slope[rows, columns] = half + (0.5 * v) * (1.0 - t * t) * (scale + (scale * 3 * 0.044715) * square)
            return 0

        lax.fori_loop(0, 12, gelu, 0)
        total = total + dot(hidden[:, columns], wr[columns, :], NN)
    block[...] = total.astype(BF16)

    own = dot(head_t[...], block[...], NT)
    fall[0] = own
    far = place.along_ens(2)
    far_copies = [
        remote(fall.at[0, pl.ds(r, 40)], fall.at[2, pl.ds(r, 40)], ens_send.at[k], ens_recv.at[k], far)
        for k, r in enumerate((0, 40))
    ]
    near_copy = remote(fall.at[0], fall.at[1], ens_send.at[2], ens_recv.at[2], place.other_core())
    relays = [
        remote(fall.at[2, pl.ds(r, 40)], fall.at[3, pl.ds(r, 40)], ens_send.at[3 + k], ens_recv.at[3 + k], place.other_core())
        for k, r in enumerate((0, 40))
    ]
    for copy in [*far_copies, near_copy]:
        copy.start()
    normed_t[...] = normed[...].T
    for b in range(BLOCKS):
        hidden_t[b * BLOCK : (b + 1) * BLOCK, :] = hidden[:, b * BLOCK : (b + 1) * BLOCK].T
    for came, relay in zip(far_copies, relays):
        came.wait_recv()
        relay.start()
    near_copy.wait_recv()

    spread = jnp.zeros((80, D), F32)
    for s in range(4):
        if s == 3:
            for copy in relays:
                copy.wait_recv()
        theirs = fall[s]
        swapped = jnp.concatenate(
            [theirs[:, 128:256], theirs[:, 0:128], pltpu.roll(theirs[:, 256:384], 64, 1)], axis=1
        )
        spread = spread + slope_of(own - theirs) + slope_of(own - swapped)
    observed = jnp.concatenate([tg[:, 0:128], tg[:, 0:128], tg[:, 128:256]], axis=1)
    ocean = observed[outputs : outputs + 1]
    slopes = slope_of(own - observed) / MEMBERS - FAIR_WEIGHT / (MEMBERS * (MEMBERS - 1)) * spread
    slopes_b = (slopes * ocean).astype(BF16)

    grad_head = dot(slopes_b, block[...], NN)
    for r in range(5):
        for l in range(LANES):
            put_small(batch1.g, r * 3 + l, grad_head[r * 16 : r * 16 + 16, l * 128 : (l + 1) * 128])
    for index in range(32):
        if index >= 15:
            put_small(batch1.g, index, jnp.zeros((16, 128), F32))
        put_small(batch2.g, index, jnp.zeros((16, 128), F32))
    back = dot(slopes_b, head_t[...], TN)
    d_block[...] = back
    d_block_b[...] = back.astype(BF16)
    grad_reduce = dot(hidden_t[...], d_block_b[...], NN)
    for l in range(LANES):
        put_main(batch1.g, l * FFN, grad_reduce[:, l * 128 : (l + 1) * 128])
    batch1.start_core()

    d_normed = jnp.zeros((D, D), F32)
    for b in range(BLOCKS):
        columns = slice(b * BLOCK, (b + 1) * BLOCK)
        before[...] = dot(d_block_b[...], wr[columns, :], NT)

        def gate(i, _):
            rows = pl.ds(pl.multiple_of(i * 32, 32), 32)
            d_before[rows, :] = (before[rows, :] * slope[rows, columns]).astype(BF16)
            return 0

        lax.fori_loop(0, 12, gate, 0)
        grad_expand = dot(normed_t[...], d_before[...], NN)
        for l in range(BLOCK // 128):
            put_main(batch2.g, (b * (BLOCK // 128) + l) * D, grad_expand[:, l * 128 : (l + 1) * 128])
        d_normed = d_normed + dot(d_before[...], we[:, columns], NT)
        if b == 1:
            batch1.core_to_first()
    batch2.start_core()
    d_norm[...] = d_normed

    gk[0, 7:8, :] = jnp.zeros((1, 128), F32)

    def unnorm(i, _):
        rows = pl.ds(pl.multiple_of(i * 64, 64), 64)
        value = [d_norm[rows, l * 128 : (l + 1) * 128] for l in range(LANES)]
        std = [standard[rows, l * 128 : (l + 1) * 128] for l in range(LANES)]
        for l in range(LANES):
            gk[l, 7:8, :] += jnp.sum(value[l] * std[l], axis=0, keepdims=True)
        scaled = [value[l] * gain_row[:, l * 128 : (l + 1) * 128] for l in range(LANES)]
        mean = jnp.sum(scaled[0] + scaled[1] + scaled[2], axis=-1, keepdims=True) / D
        along = jnp.sum(scaled[0] * std[0] + scaled[1] * std[1] + scaled[2] * std[2], axis=-1, keepdims=True) / D
        for l in range(LANES):
            mixed[l, pl.ds(i * 4, 4)] = (recip[rows, :] * (scaled[l] - mean - std[l] * along)).reshape(4, 16, 128)
        return 0

    lax.fori_loop(0, 6, unnorm, 0)
    for l in range(LANES):
        for m in range(2):
            dext[l, m, 3:11, 8:24, :] = mixed[l, m * 8 : m * 8 + 8]
            dext[l, m, 11:15, 8:24, :] = mixed[l, 16 + m * 4 : 20 + m * 4]
    pack(dext, hs2)
    halo2 = halo(hs2, hr2, 2)

    def kernel_grad(l, _):
        for j in range(7):
            near = [ext[l, m, :, 5 + j : 21 + j, :] for m in range(2)]
            for i in range(7):
                part = jnp.zeros((16, 128), F32)
                for m in range(2):
                    part = part + jnp.sum(dext[l, m, 3:15, 8:24, :] * near[m][i : i + 12], axis=0)
                gk[l, i * 8 + j : i * 8 + j + 1, :] = jnp.sum(part, axis=0, keepdims=True)
        return 0

    lax.fori_loop(0, 2, kernel_grad, 0)
    batch2.core_to_first()
    lax.fori_loop(2, 3, kernel_grad, 0)
    count = jnp.sum(sea[...].astype(F32)).astype(jnp.int32)
    lane = lax.broadcasted_iota(jnp.int32, (1, 128), 1)
    bits = lax.bitwise_and(lax.shift_right_logical(jnp.broadcast_to(count, (1, 128)), jnp.minimum(lane, 31)), 1)
    gk[0, 15:16, :] = jnp.where(lane < COUNT_BITS, bits, 0).astype(F32)
    for r in range(4):
        for l in range(LANES):
            put_few(few.g, r * 3 + l, gk[l, r * 16 : r * 16 + 16, :])
    few.start()
    batch1.first_to_second()
    few.to_x()
    for copy in halo2:
        copy.wait_recv()
    unpack(dext, hr2)

    def mix_back(i, _):
        l, m = lax.div(i, 2), lax.rem(i, 2)
        mixed_back = correlate(dext, l, m, True)
        mixed[l, pl.ds(m * 8, 8)] = mixed_back[:8]
        mixed[l, pl.ds(16 + m * 4, 4)] = mixed_back[8:]
        return 0

    lax.fori_loop(0, 4, mix_back, 0)
    batch1.second_to_z()
    few.to_y()
    batch2.first_to_second()
    lax.fori_loop(4, 6, mix_back, 0)
    for l in range(LANES):
        lanes = slice(l * 128, (l + 1) * 128)
        mixed[l] = mixed[l] + d_block[:, lanes].reshape(24, 16, 128)
    direct = []
    for l in range(LANES):
        for m in range(2):
            lanes = slice(l * 128, (l + 1) * 128)
            at = (l * 2 + m) * 2
            direct.append(
                pltpu.make_async_copy(
                    mixed.at[l, m * 8 : m * 8 + 8], direct_out.at[m, 0:8, :, lanes], in_sems.at[at]
                )
            )
            direct.append(
                pltpu.make_async_copy(
                    mixed.at[l, 16 + m * 4 : 20 + m * 4], direct_out.at[m, 8:12, :, lanes], in_sems.at[at + 1]
                )
            )
    for copy in direct:
        copy.start()
    batch2.second_to_z()
    batch1.z_to_gather()
    few.to_z()
    batch2.z_to_gather()
    batch1.gather_to_second()
    few.to_core()
    batch1.second_to_first()
    batch2.gather_to_second()
    batch2.second_to_first()
    batch1.first_to_core()
    batch2.first_to_core()
    for copy in halo1 + halo2 + far_copies + [near_copy] + relays:
        copy.wait_send()
    for copy in direct:
        copy.wait()
    few.finish()
    batch1.finish()
    batch2.finish()


def finish(o1, o2, o3, direct, g_inputs, g_kernel, g_gain, g_expand, g_reduce, g_head):
    def small(o, index):
        return o[1, index * 80 + 64 : index * 80 + 80, :].astype(F32)

    g_inputs[...] = direct[...]
    def few(index):
        return o3[index // 6, index % 6 * 16 : index % 6 * 16 + 16, :].astype(F32)

    rows = [[few(r * 3 + l) for l in range(LANES)] for r in range(4)]
    weight = lax.broadcasted_iota(jnp.int32, (1, 128), 1)
    weight = jnp.where(weight < COUNT_BITS, lax.shift_left(1, jnp.minimum(weight, 15)), 0).astype(F32)
    total = jnp.sum(rows[0][0][15:16] * weight, axis=-1, keepdims=True) / 4
    scale = 1.0 / total
    for l in range(LANES):
        lanes = slice(l * 128, (l + 1) * 128)
        for i in range(7):
            at = (i % 2) * 8
            g_kernel[i, :, lanes] = rows[i // 2][l][at : at + 7] * scale
        g_gain[lanes] = (rows[0][l][7:8] * scale).reshape(128)
    head = jnp.concatenate(
        [jnp.concatenate([small(o1, r * 3 + l) for l in range(LANES)], axis=1) for r in range(5)], axis=0
    )
    g_head[...] = (head * scale)[: g_head.shape[0]]

    def main(o, flat, count):
        if flat < HALF:
            take = min(count, HALF - flat)
            yield 0, o[0, flat : flat + take, :]
            for at, rows in main(o, HALF, count - take) if take < count else ():
                yield take + at, rows
            return
        for at in range(0, count, 64):
            shard = (flat - HALF + at) // 64
            yield at, o[1, shard * 80 : shard * 80 + 64, :]

    for l in range(LANES):
        for at, rows in main(o1, l * FFN, FFN):
            g_reduce[at : at + rows.shape[0], l * 128 : (l + 1) * 128] = rows.astype(F32) * scale
    for l in range(FFN // 128):
        for at, rows in main(o2, l * D, D):
            g_expand[at : at + rows.shape[0], l * 128 : (l + 1) * 128] = rows.astype(F32) * scale


def on_device(sizes, inputs, target, land_sea, kernel, norm_gain, w_expand, w_reduce, head_weight):
    outputs = target.shape[0]
    by_cell = jnp.transpose(target, (1, 2, 0))
    head_rows = head_weight.T
    anywhere = pl.BlockSpec(memory_space=pl.ANY)
    in_hbm = pl.BlockSpec(memory_space=pltpu.HBM)
    vmem = pltpu.VMEM
    scratch = [
        vmem((24, 16, D), BF16),
        vmem((12, 16, outputs), F32),
        vmem((256, 128), F32),
        vmem((80, 256), F32),
        vmem((12, 16), jnp.int32),
        vmem((LANES, 7, 7, 128), F32),
        vmem((D,), F32),
        vmem((D, FFN), BF16),
        vmem((FFN, D), BF16),
        vmem((outputs, D), BF16),
        vmem((LANES, 2, 18, 32, 128), F32),
        vmem((LANES, 2, 18, 32, 128), F32),
        vmem((2, 80, D), F32),
        vmem((2, 80, D), BF16),
        vmem((2, 80, D), BF16),
        vmem((2, 80, D), BF16),
        vmem((2, 80, D), BF16),
        vmem((LANES, 24, 16, 128), F32),
        vmem((D, D), F32),
        vmem((D, 128), F32),
        vmem((D, D), BF16),
        vmem((D, BLOCK), F32),
        vmem((D, FFN), F32),
        vmem((D, FFN), BF16),
        vmem((FFN, D), BF16),
        vmem((D, D), BF16),
        vmem((D, D), BF16),
        vmem((80, D), BF16),
        vmem((4, 80, D), F32),
        vmem((D, D), F32),
        vmem((D, D), BF16),
        vmem((D, BLOCK), BF16),
        vmem((D, D), F32),
        vmem((LANES, 64, 128), F32),
        pltpu.SemaphoreType.DMA((13,)),
        pltpu.SemaphoreType.DMA((4,)),
        pltpu.SemaphoreType.DMA((4,)),
        pltpu.SemaphoreType.DMA((5,)),
        pltpu.SemaphoreType.DMA((5,)),
    ]
    batch = reduce_scratch(sizes)
    batch = batch[:-1] + list(batch[-1])
    scratch += batch + batch
    scratch += [vmem((2, FEW, 128), BF16), vmem((FEW, 128), BF16)]
    scratch += [vmem((count, FEW, 128), BF16) for count in (sizes[0], sizes[1], 2 * sizes[2])]
    few_slots = 2 + sizes[0] + sizes[1] + 2 * sizes[2]
    scratch += [vmem((FEW, 128), BF16), pltpu.SemaphoreType.DMA((few_slots,)), pltpu.SemaphoreType.DMA((few_slots,))]
    operands = [inputs, by_cell, land_sea, kernel, norm_gain, w_expand, w_reduce, head_rows]
    operands = [pltpu.with_memory_space_constraint(operand, pltpu.HBM) for operand in operands]
    o1, o2, o3, direct = pl.pallas_call(
        lambda *refs: work(sizes, *refs),
        out_shape=(
            jax.ShapeDtypeStruct((2, HALF, 128), BF16),
            jax.ShapeDtypeStruct((2, HALF, 128), BF16),
            jax.ShapeDtypeStruct((2, FEW, 128), BF16),
            jax.ShapeDtypeStruct(inputs.shape, F32),
        ),
        in_specs=[in_hbm] * 8,
        out_specs=(anywhere,) * 4,
        scratch_shapes=scratch,
        compiler_params=pltpu.CompilerParams(
            collective_id=0, has_side_effects=True, vmem_limit_bytes=48 * 1024 * 1024
        ),
        name="block_pass",
    )(*operands)
    g_inputs, g_kernel, g_gain, g_expand, g_reduce, g_head = pl.pallas_call(
        finish,
        out_shape=(
            jax.ShapeDtypeStruct(inputs.shape, F32),
            jax.ShapeDtypeStruct(kernel.shape, F32),
            jax.ShapeDtypeStruct((D,), F32),
            jax.ShapeDtypeStruct(w_expand.shape, F32),
            jax.ShapeDtypeStruct(w_reduce.shape, F32),
            jax.ShapeDtypeStruct(head_rows.shape, F32),
        ),
        compiler_params=pltpu.CompilerParams(vmem_limit_bytes=32 * 1024 * 1024),
        name="finish",
    )(o1, o2, o3, direct)
    return g_inputs, g_kernel, g_gain, g_expand, g_reduce, g_head.T


def solution(mesh):
    sizes = grid_of(mesh)
    return jax.shard_map(
        lambda *arrays: on_device(sizes, *arrays),
        mesh=mesh,
        in_specs=(
            P("ens", None, "tile", None),
            P(None, None, "tile"),
            P(None, "tile"),
            P(),
            P(),
            P(),
            P(),
            P(),
        ),
        out_specs=(P("ens", None, "tile", None), P(), P(), P(), P(), P()),
        check_vma=False,
    )
```

```python
import jax
import jax.numpy as jnp
from jax import lax
from jax.experimental import pallas as pl
from jax.experimental.pallas import tpu as pltpu
from jax.sharding import PartitionSpec as P

FAIR_WEIGHT = 0.95
SMOOTHING = 0.5
NORM_EPS = 1e-06
D = 384
FFN = 1536
LANES = 3
BLOCK = 512
BLOCKS = FFN // BLOCK
MEMBERS = 8
HALF = 2048
SHARD = 64
MAIN = 48
SLOTS = 48
THIRD = 1024
COUNT_BITS = 8
FEW = 128
F32 = jnp.float32
BF16 = jnp.bfloat16


def grid_of(mesh):
    tiles = mesh.shape["tile"]
    side = 4 if tiles == 64 else 2
    return side, side, tiles // (side * side)


def dot(a, b, dims):
    return lax.dot_general(a, b, (dims, ((), ())), preferred_element_type=F32)


NN = ((1,), (0,))
NT = ((1,), (1,))
TN = ((0,), (0,))


class Place:
    def __init__(self, sizes):
        self.nx, self.ny, self.nzh = sizes
        self.nz = 2 * self.nzh
        self.tiles = self.nx * self.ny * self.nzh
        self.ens = lax.axis_index("ens")
        self.tile = lax.axis_index("tile")
        self.core = lax.rem(self.ens, 2)
        self.zl = lax.div(self.ens, 2)
        self.zh = lax.rem(self.tile, self.nzh)
        self.x = lax.rem(lax.div(self.tile, self.nzh), self.nx)
        self.y = lax.div(self.tile, self.nzh * self.nx)
        self.z = self.zh * 2 + self.zl

    def at(self, x, y, z, core):
        return (lax.rem(z, 2) * 2 + core, (y * self.nx + x) * self.nzh + lax.div(z, 2))

    def along_x(self, d):
        return self.at(lax.rem(self.x + d, self.nx), self.y, self.z, self.core)

    def along_y(self, d):
        return self.at(self.x, lax.rem(self.y + d, self.ny), self.z, self.core)

    def along_z(self, d):
        return self.at(self.x, self.y, lax.rem(self.z + d, self.nz), self.core)

    def other_core(self):
        return self.at(self.x, self.y, self.z, 1 - self.core)

    def along_tile(self, d):
        return (self.ens, lax.rem(self.tile + d + self.tiles, self.tiles))

    def along_ens(self, d):
        return (lax.rem(self.ens + d, 4), self.tile)

    def everyone(self):
        peers = [self.along_tile(1), self.along_tile(-1)]
        peers += [self.along_ens(d) for d in range(1, 4)]
        peers += [self.along_x(d) for d in range(1, self.nx)]
        peers += [self.along_y(d) for d in range(1, self.ny)]
        peers += [self.along_z(d) for d in range(1, self.nz)]
        return peers


def remote(src, dst, send, recv, to):
    return pltpu.make_async_remote_copy(
        src_ref=src,
        dst_ref=dst,
        send_sem=send,
        recv_sem=recv,
        device_id=to,
        device_id_type=pl.DeviceIdType.MESH,
    )


def far_first(size):
    return sorted(range(1, size), key=lambda d: -min(d, size - d))


def summed(parts):
    value = None
    for part in parts:
        part = part.astype(F32)
        value = part if value is None else value + part
    return value.astype(BF16)


def from_row(start, count):
    return pl.ds(pl.multiple_of(start, 16), count)


class Group:
    def __init__(self, owner, whole, apart=False):
        self.owner, self.whole, self.apart = owner, whole, apart
        self.send, self.recv = owner.send.at[owner.slot()], owner.recv.at[owner.slot()]
        self.copies = []
        owner.groups.append(self)

    def start(self, src, dst, to):
        recv = self.owner.recv.at[self.owner.slot()] if self.apart else self.recv
        copy = remote(src, dst, self.send, recv, to)
        copy.start()
        self.copies.append(copy)
        self.to = to

    def all(self):
        return remote(self.whole, self.whole, self.send, self.recv, self.to)

    def received(self):
        self.all().wait_recv()

    def sent(self):
        self.all().wait_send()


class Copies:
    def __init__(self, send, recv):
        self.send, self.recv = send, recv
        self.slots = 0
        self.groups = []

    def slot(self):
        self.slots += 1
        return self.slots - 1

    def one(self, src, dst, to):
        group = Group(self, src)
        group.start(src, dst, to)
        return group

    def keep(self, src, dst):
        copy = pltpu.make_async_copy(src, dst, self.send.at[self.slot()])
        copy.start()
        return copy

    def settle(self):
        for group in self.groups:
            group.sent()
        self.groups = []


class Reduce(Copies):
    def __init__(self, place, refs, out, third):
        self.third = third
        self.p = place
        self.g, self.rc, self.s1, self.r1, self.s2, self.r2, self.sz, self.rz, self.oz, *sems = refs
        super().__init__(*sems)
        self.out = out
        self.n, self.nz = place.nx, place.nz
        self.c_rows = HALF // 2
        self.p_rows = self.c_rows // self.n
        self.q_rows = self.p_rows // self.n
        self.z_rows = 2 * self.q_rows // self.nz
        self.order, self.z_order = far_first(self.n), far_first(self.nz)
        self.core = [None, None]
        self.in_first = [None, None]

    def first(self, h):
        return self.p.x if h == 0 else self.p.y

    def second(self, h):
        return self.p.y if h == 0 else self.p.x

    def to_first(self, h, d):
        return self.p.along_x(d) if h == 0 else self.p.along_y(d)

    def to_second(self, h, d):
        return self.p.along_y(d) if h == 0 else self.p.along_x(d)

    def start_core(self, halves=(0, 1)):
        other = from_row((1 - self.p.core) * self.c_rows, self.c_rows)
        for h in halves:
            self.core[h] = self.one(self.g.at[h, other], self.rc.at[h], self.p.other_core())

    def core_to_first(self, halves=(0, 1)):
        for h in halves:
            self.core[h].received()
            group = self.in_first[h] = Group(self, self.r1.at[h])
            for d in (*self.order, 0):
                at = lax.rem(self.first(h) + d, self.n) * self.p_rows
                piece = from_row(at, self.p_rows)
                mine = from_row(self.p.core * self.c_rows + at, self.p_rows)
                self.s1[h, piece, :] = summed([self.g[h, mine, :], self.rc[h, piece, :]])
                if d:
                    group.start(self.s1.at[h, piece], self.r1.at[h, d - 1], self.to_first(h, d))

    def first_to_second(self):
        self.in_second = []
        for h in range(2):
            self.in_first[h].received()
            mine = self.s1[h, from_row(self.first(h) * self.p_rows, self.p_rows), :]
            self.s2[h] = summed([mine, *(self.r1[h, d] for d in range(self.n - 1))])
            group = Group(self, self.r2.at[h])
            self.in_second.append(group)
            for d in self.order:
                piece = from_row(lax.rem(self.second(h) + d, self.n) * self.q_rows, self.q_rows)
                group.start(self.s2.at[h, piece], self.r2.at[h, d - 1], self.to_second(h, d))

    def second_to_z(self):
        for h in range(2):
            self.in_second[h].received()
            mine = self.s2[h, from_row(self.second(h) * self.q_rows, self.q_rows), :]
            self.sz[h * self.q_rows : (h + 1) * self.q_rows, :] = summed(
                [mine, *(self.r2[h, d] for d in range(self.n - 1))]
            )
        self.in_z = Group(self, self.rz)
        for d in self.z_order:
            piece = from_row(lax.rem(self.p.z + d, self.nz) * self.z_rows, self.z_rows)
            self.in_z.start(self.sz.at[piece], self.rz.at[d - 1], self.p.along_z(d))

    def z_to_gather(self):
        self.in_z.received()
        mine = from_row(self.p.z * self.z_rows, self.z_rows)
        self.oz[mine, :] = summed([self.sz[mine, :], *(self.rz[d] for d in range(self.nz - 1))])
        self.out_z = Group(self, self.oz.at[pl.ds(0, (self.nz - 1) * self.z_rows)])
        for d in self.z_order:
            self.out_z.start(self.oz.at[mine], self.oz.at[mine], self.p.along_z(d))

    def shard(self, h):
        return self.p.core * self.c_rows + self.first(h) * self.p_rows + self.second(h) * self.q_rows

    def gather_to_second(self):
        self.out_z.received()
        self.out_second = []
        self.kept = []
        for h in range(2):
            at = from_row(self.shard(h), self.q_rows)
            mine = self.oz.at[pl.ds(h * self.q_rows, self.q_rows)]
            group = Group(self, self.out.at[h, pl.ds(0, (self.n - 1) * self.q_rows)])
            self.out_second.append(group)
            for d in self.order:
                group.start(mine, self.out.at[h, at], self.to_second(h, d))
            self.kept.append(self.keep(mine, self.out.at[h, at]))

    def piece(self, h, d):
        at = lax.rem(self.first(h) + d, self.n) * self.p_rows
        return self.out.at[h, from_row(self.p.core * self.c_rows + at, self.p_rows)]

    def second_to_first(self):
        self.out_first = []
        self.out_core = []
        for h in range(2):
            self.out_second[h].received()
            self.kept[h].wait()
            mine = self.piece(h, 0)
            group = Group(self, self.out.at[h, pl.ds(0, (self.n - 1) * self.p_rows)], apart=True)
            self.out_first.append(group)
            for d in self.order:
                group.start(mine, mine, self.to_first(h, d))
            group = Group(self, self.out.at[h, pl.ds(0, self.c_rows)])
            self.out_core.append(group)
            group.start(mine, mine, self.p.other_core())

    def first_to_core(self):
        for k, d in enumerate(self.order):
            for h in range(2):
                self.out_first[h].copies[k].wait_recv()
                came = self.piece(h, self.n - d)
                self.out_core[h].start(came, came, self.p.other_core())

    def finish(self):
        for group in self.out_core:
            group.received()
        self.settle()


class Few(Copies):
    def __init__(self, place, refs, out):
        self.p = p = place
        self.g, self.rc, self.s, self.rx, self.sy, self.sz, self.o, *sems = refs
        super().__init__(*sems)
        self.out = out
        self.x_rows = FEW // p.nx

    def piece(self, d):
        return from_row(lax.rem(self.p.x + d, self.p.nx) * self.x_rows, self.x_rows)

    def start(self):
        self.got = self.one(self.g.at[1 - self.p.core], self.rc, self.p.other_core())

    def to_x(self):
        p = self.p
        self.got.received()
        self.s[...] = summed([self.g[p.core], self.rc[...]])
        self.got = Group(self, self.rx)
        for d in far_first(p.nx):
            self.got.start(self.s.at[self.piece(d)], self.rx.at[d - 1], p.along_x(d))

    def to_y(self):
        p = self.p
        self.got.received()
        self.sy[p.y] = summed([self.s[self.piece(0), :], *(self.rx[d] for d in range(p.nx - 1))])
        self.got = Group(self, self.sy.at[pl.ds(0, p.ny - 1)])
        for d in far_first(p.ny):
            self.got.start(self.sy.at[p.y], self.sy.at[p.y], p.along_y(d))

    def to_z(self):
        p = self.p
        self.got.received()
        self.sz[p.z] = summed(self.sy[k] for k in range(p.ny))
        self.got = Group(self, self.sz.at[pl.ds(0, p.nz - 1)])
        for d in far_first(p.nz):
            self.got.start(self.sz.at[p.z], self.sz.at[p.z], p.along_z(d))

    def to_gather(self):
        p = self.p
        self.got.received()
        self.o[...] = summed(self.sz[k] for k in range(p.nz))
        mine = self.out.at[p.core, self.piece(0)]
        self.kept = self.keep(self.o, mine)
        self.got = Group(self, self.out.at[0, pl.ds(0, (p.nx - 1) * self.x_rows)])
        for d in far_first(p.nx):
            self.got.start(self.o, mine, p.along_x(d))
        self.last = Group(self, self.out.at[0])
        self.last.start(self.o, mine, p.other_core())

    def to_core(self):
        p = self.p
        self.got.received()
        for d in range(1, p.nx):
            came = self.out.at[p.core, self.piece(d)]
            self.last.start(came, came, p.other_core())

    def finish(self):
        self.last.received()
        self.kept.wait()
        self.settle()


class Third(Copies):
    def __init__(self, place, refs, out):
        self.p = p = place
        self.g, self.rc, self.s1, self.r1, self.s2, self.r2, self.sy, self.o, *sems = refs
        super().__init__(*sems)
        self.out = out
        self.z_rows = THIRD // 2 // p.nz
        self.x_rows = self.z_rows // p.nx
        self.order = far_first(p.nz)

    def piece(self, d):
        return from_row(lax.rem(self.p.z + d, self.p.nz) * self.z_rows, self.z_rows)

    def start_core(self):
        self.got = self.one(self.g.at[1 - self.p.core], self.rc, self.p.other_core())

    def core_to_first(self):
        p = self.p
        self.got.received()
        self.s1[...] = summed([self.g[p.core], self.rc[...]])
        self.got = Group(self, self.r1)
        for d in self.order:
            self.got.start(self.s1.at[self.piece(d)], self.r1.at[d - 1], p.along_z(d))

    def first_to_second(self):
        p = self.p
        self.got.received()
        self.s2[...] = summed([self.s1[self.piece(0), :], *(self.r1[k] for k in range(p.nz - 1))])
        self.got = Group(self, self.r2)
        for d in far_first(p.nx):
            piece = from_row(lax.rem(p.x + d, p.nx) * self.x_rows, self.x_rows)
            self.got.start(self.s2.at[piece], self.r2.at[d - 1], p.along_x(d))

    def second_to_y(self):
        p = self.p
        self.got.received()
        mine = self.s2[from_row(p.x * self.x_rows, self.x_rows), :]
        self.sy[p.y] = summed([mine, *(self.r2[d] for d in range(p.nx - 1))])
        self.got = Group(self, self.sy.at[pl.ds(0, p.ny - 1)])
        for d in far_first(p.ny):
            self.got.start(self.sy.at[p.y], self.sy.at[p.y], p.along_y(d))

    def y_to_second(self):
        p = self.p
        self.got.received()
        self.o[...] = summed(self.sy[k] for k in range(p.ny))
        mine = self.out.at[p.core, from_row(p.z * self.z_rows + p.x * self.x_rows, self.x_rows)]
        self.kept = self.keep(self.o, mine)
        self.got = Group(self, self.out.at[0, pl.ds(0, (p.nx - 1) * self.x_rows)])
        for d in far_first(p.nx):
            self.got.start(self.o, mine, p.along_x(d))

    def second_to_first(self):
        p = self.p
        self.got.received()
        self.kept.wait()
        mine = self.out.at[p.core, self.piece(0)]
        self.got = Group(self, self.out.at[0, pl.ds(0, (p.nz - 1) * self.z_rows)])
        for d in self.order:
            self.got.start(mine, mine, p.along_z(d))

    def first_to_core(self):
        p = self.p
        self.got.received()
        self.last = self.one(self.out.at[p.core], self.out.at[p.core], p.other_core())

    def finish(self):
        self.last.received()
        self.settle()


def third_scratch(sizes):
    nx, ny, nzh = sizes
    nz = 2 * nzh
    z_rows = THIRD // 2 // nz
    x_rows = z_rows // nx
    shapes = [
        (2, THIRD // 2, 128), (THIRD // 2, 128), (THIRD // 2, 128), (nz - 1, z_rows, 128), (z_rows, 128),
        (nx - 1, x_rows, 128), (ny, x_rows, 128), (x_rows, 128),
    ]
    return [pltpu.VMEM(shape, BF16) for shape in shapes] + [pltpu.SemaphoreType.DMA((SLOTS,))] * 2


def few_scratch(sizes):
    nx, ny, nzh = sizes
    x_rows = FEW // nx
    shapes = [
        (2, FEW, 128), (FEW, 128), (FEW, 128), (nx - 1, x_rows, 128), (ny, x_rows, 128), (2 * nzh, x_rows, 128),
        (x_rows, 128),
    ]
    return [pltpu.VMEM(shape, BF16) for shape in shapes] + [pltpu.SemaphoreType.DMA((SLOTS,))] * 2


def reduce_scratch(sizes):
    n, _, nzh = sizes
    nz = 2 * nzh
    c_rows = HALF // 2
    p_rows = c_rows // n
    q_rows = p_rows // n
    z_rows = 2 * q_rows // nz
    shapes = [
        (2, HALF, 128), (2, c_rows, 128), (2, c_rows, 128), (2, n - 1, p_rows, 128), (2, p_rows, 128),
        (2, n - 1, q_rows, 128), (2 * q_rows, 128), (nz - 1, z_rows, 128), (2 * q_rows, 128),
    ]
    return [pltpu.VMEM(shape, BF16) for shape in shapes] + [pltpu.SemaphoreType.DMA((SLOTS,))] * 2


def slope_of(offset):
    return offset * lax.rsqrt(offset * offset + SMOOTHING * SMOOTHING)


def places(flat, count):
    at = 0
    while at < count:
        here = flat + at
        if here < HALF:
            take, part, row = HALF - here, 0, here
        elif here < HALF + 32 * MAIN:
            shard, inner = divmod(here - HALF, MAIN)
            take, part, row = MAIN - inner, 1, shard * SHARD + inner
        else:
            row = here - HALF - 32 * MAIN
            part, row = 2 + row // (THIRD // 2), row % (THIRD // 2)
            take = THIRD // 2 - row
        take = min(take, count - at)
        yield at, part, row, take
        at += take


def part_of(halves, third, part):
    return halves.at[part] if part < 2 else third.at[part - 2]


def put_main(batch, flat, value):
    for at, part, row, take in places(flat, value.shape[0]):
        part_of(batch.g, batch.third.g, part)[row : row + take, :] = value[at : at + take].astype(BF16)


def put_small(batch, index, value):
    batch[1, index * SHARD + MAIN : (index + 1) * SHARD, :] = value.astype(BF16)


def put_few(batch, index, value):
    batch[index // 6, index % 6 * 16 : index % 6 * 16 + 16, :] = value.astype(BF16)


def work(sizes, *refs):
    (
        x_hbm, target_hbm, sea_hbm, kernel_hbm, gain_hbm, expand_hbm, reduce_hbm, head_hbm,
        out1, third1, out2, third2, out3, direct_out,
        xb, target, tall, tg, sea, taps, gain, we, wr, head,
        ext, dext, rim, hs, hr, hs2, hr2, mixed, standard, recip, normed, before, slope, hidden, hidden_t, normed_t,
        block, head_t, fall, d_block, d_block_b, d_before, d_norm, gk,
        in_sems, halo_send, halo_recv, ens_send, ens_recv,
        *rest,
    ) = refs
    place = Place(sizes)
    few = Few(place, rest[-9:], out3)
    pieces = (len(rest) - 9) // 2
    batch1, batch2 = (
        Reduce(place, mine[:-10], out, Third(place, mine[-10:], third))
        for mine, out, third in ((rest[:pieces], out1, third1), (rest[pieces : 2 * pieces], out2, third2))
    )

    loads = [
        pltpu.make_async_copy(x_hbm.at[0, 0:8], xb.at[0:8], in_sems.at[0]),
        pltpu.make_async_copy(x_hbm.at[1, 0:8], xb.at[8:16], in_sems.at[1]),
        pltpu.make_async_copy(x_hbm.at[0, 8:12], xb.at[16:20], in_sems.at[2]),
        pltpu.make_async_copy(x_hbm.at[1, 8:12], xb.at[20:24], in_sems.at[3]),
    ]
    tap_loads = [
        pltpu.make_async_copy(kernel_hbm.at[:, :, l * 128 : (l + 1) * 128], taps.at[l], in_sems.at[4 + l])
        for l in range(LANES)
    ]
    later = [
        pltpu.make_async_copy(gain_hbm, gain, in_sems.at[7]),
        pltpu.make_async_copy(head_hbm, head, in_sems.at[8]),
        pltpu.make_async_copy(expand_hbm, we, in_sems.at[9]),
        pltpu.make_async_copy(reduce_hbm, wr, in_sems.at[10]),
        pltpu.make_async_copy(target_hbm, target, in_sems.at[11]),
        pltpu.make_async_copy(sea_hbm, sea, in_sems.at[12]),
    ]
    for copy in loads + tap_loads + later:
        copy.start()

    barrier = pltpu.get_barrier_semaphore()
    peers = place.everyone()
    for peer in peers:
        pl.semaphore_signal(barrier, inc=1, device_id=peer, device_id_type=pl.DeviceIdType.MESH)

    def clear(i, _):
        l, m = lax.div(i, 2), lax.rem(i, 2)
        for ref in (ext, dext):
            ref[l, m, 0:3] = jnp.zeros((3, 32, 128), F32)
            ref[l, m, 15:18] = jnp.zeros((3, 32, 128), F32)
        ext[l, m, 3:15, 0:8] = jnp.zeros((12, 8, 128), F32)
        ext[l, m, 3:15, 24:32] = jnp.zeros((12, 8, 128), F32)
        return 0

    lax.fori_loop(0, 2 * LANES, clear, 0)
    gk[...] = jnp.zeros_like(gk)
    rim[...] = jnp.zeros_like(rim)
    few.g[...] = jnp.zeros_like(few.g)
    for copy in loads:
        copy.wait()
    for l in range(LANES):
        lanes = slice(l * 128, (l + 1) * 128)
        for m in range(2):
            ext[l, m, 3:11, 8:24, :] = xb[m * 8 : m * 8 + 8, :, lanes].astype(F32)
            ext[l, m, 11:15, 8:24, :] = xb[16 + m * 4 : 20 + m * 4, :, lanes].astype(F32)

    def rim_rows(m, j):
        return slice((m * 3 + j) * 12, (m * 3 + j) * 12 + 12)

    def pack(field, out):
        for side, col in ((0, 8), (1, 21)):
            for m in range(2):
                for j in range(3):
                    for l in range(LANES):
                        rim[side, l, rim_rows(m, j)] = field[l, m, 3:15, col + j, :]
        out[...] = rim[...].astype(BF16)

    def unpack(field, got, l):
        for side, col in ((0, 5), (1, 24)):
            rim[side, l] = got[side, l].astype(F32)
            for m in range(2):
                for j in range(3):
                    field[l, m, 3:15, col + j, :] = rim[side, l, rim_rows(m, j)]

    def halo(out, got, at):
        copies = [
            [
                remote(out.at[side, l], got.at[1 - side, l], halo_send.at[at + s], halo_recv.at[at + s], place.along_tile(to))
                for s, (side, to) in enumerate(((0, -1), (1, 1)), 2 * l)
            ]
            for l in range(LANES)
        ]
        for pair in copies:
            for copy in pair:
                copy.start()
        return copies

    pack(ext, hs)
    pl.semaphore_wait(barrier, len(peers))
    halo1 = halo(hs, hr, 0)

    for copy in tap_loads + later:
        copy.wait()
    for index in range(32):
        put_small(batch1.g, index, jnp.zeros((16, 128), F32))
        if index >= 15:
            put_small(batch2.g, index, jnp.zeros((16, 128), F32))
    outputs = head.shape[0]
    head_t[...] = jnp.concatenate([head[...].astype(F32), jnp.zeros((80 - outputs, D), F32)], axis=0).astype(BF16)
    diagonal = lax.broadcasted_iota(jnp.int32, (16, 16), 0) == lax.broadcasted_iota(jnp.int32, (16, 16), 1)
    tall[...] = jnp.zeros_like(tall)
    for a in range(12):
        water = jnp.broadcast_to(sea[a : a + 1, :].astype(F32), (16, 16))
        water = jnp.sum(jnp.where(diagonal, water, 0.0), axis=1, keepdims=True)
        for at in (a * 16,) if a < 8 else (a * 16, a * 16 + 64):
            tall[at : at + 16, 0:outputs] = target[a]
            tall[at : at + 16, outputs : outputs + 1] = water
    tg[...] = tall[...].T[0:80]
    def correlate(field, l, m, flip):
        total = jnp.zeros((12, 16, 128), F32)
        for j in range(7):
            shifted = field[l, m, :, 5 + j : 21 + j, :]
            for i in range(7):
                tap = taps[l, 6 - i, 6 - j : 7 - j, :] if flip else taps[l, i, j : j + 1, :]
                total = total + shifted[i : i + 12] * tap
        return total

    def mix(i, _):
        l, m = lax.div(i, 2), lax.rem(i, 2)
        total = correlate(ext, l, m, False)
        mixed[l, pl.ds(m * 8, 8)] = total[:8]
        mixed[l, pl.ds(16 + m * 4, 4)] = total[8:]
        return 0

    lax.fori_loop(0, 2 * LANES, mix, 0)
    sublane = lax.broadcasted_iota(jnp.int32, (18, 8, 128), 1)

    def edges(l, m):
        for first, taps_in in ((0, (0, 1, 2)), (8, (4, 5, 6))):
            total = jnp.zeros((12, 8, 128), F32)
            for j in taps_in:
                outside = sublane < 3 - j if first == 0 else sublane >= 11 - j
                shifted = jnp.where(outside, ext[l, m, :, 5 + first + j : 13 + first + j, :], 0.0)
                for i in range(7):
                    total = total + shifted[i : i + 12] * taps[l, i, j : j + 1, :]
            mixed[l, pl.ds(m * 8, 8), first : first + 8] += total[:8]
            mixed[l, pl.ds(16 + m * 4, 4), first : first + 8] += total[8:]

    for l in range(LANES):
        for copy in halo1[l]:
            copy.wait_recv()
        unpack(ext, hr, l)
        lax.fori_loop(0, 2, lambda m, _, l=l: (edges(l, m), 0)[1], 0)

    gain_row = gain[...].reshape(1, D)

    def norm(i, _):
        rows = pl.ds(pl.multiple_of(i * 64, 64), 64)
        parts = [mixed[l, pl.ds(i * 4, 4)].reshape(64, 128) for l in range(LANES)]
        mean = jnp.sum(parts[0] + parts[1] + parts[2], axis=-1, keepdims=True) / D
        centre = [part - mean for part in parts]
        square = centre[0] * centre[0] + centre[1] * centre[1] + centre[2] * centre[2]
        scale = lax.rsqrt(jnp.sum(square, axis=-1, keepdims=True) / D + NORM_EPS)
        recip[rows, :] = jnp.broadcast_to(scale, (64, 128))
        for l in range(LANES):
            lanes = slice(l * 128, (l + 1) * 128)
            value = centre[l] * scale
            standard[rows, lanes] = value
            normed[rows, lanes] = (value * gain_row[:, lanes]).astype(BF16)
        return 0

    lax.fori_loop(0, 6, norm, 0)

    total = xb[...].reshape(D, D).astype(F32)
    for b in range(BLOCKS):
        columns = slice(b * BLOCK, (b + 1) * BLOCK)
        before[...] = dot(normed[...], we[:, columns], NN)

        def gelu(i, _):
            rows = pl.ds(pl.multiple_of(i * 32, 32), 32)
            v = before[rows, :]
            square = v * v
            scale = 0.7978845608028654
            t = jnp.tanh(v * (scale + (scale * 0.044715) * square))
            half = 0.5 + 0.5 * t
            hidden[rows, columns] = (v * half).astype(BF16)
            slope[rows, columns] = half + (0.5 * v) * (1.0 - t * t) * (scale + (scale * 3 * 0.044715) * square)
            return 0

        lax.fori_loop(0, 12, gelu, 0)
        total = total + dot(hidden[:, columns], wr[columns, :], NN)
    block[...] = total.astype(BF16)

    own = dot(head_t[...], block[...], NT)
    fall[0] = own
    far = place.along_ens(2)
    far_copies = [
        remote(fall.at[0, pl.ds(r, 40)], fall.at[2, pl.ds(r, 40)], ens_send.at[k], ens_recv.at[k], far)
        for k, r in enumerate((0, 40))
    ]
    near_copy = remote(fall.at[0], fall.at[1], ens_send.at[2], ens_recv.at[2], place.other_core())
    relays = [
        remote(fall.at[2, pl.ds(r, 40)], fall.at[3, pl.ds(r, 40)], ens_send.at[3 + k], ens_recv.at[3 + k], place.other_core())
        for k, r in enumerate((0, 40))
    ]
    for copy in [*far_copies, near_copy]:
        copy.start()
    normed_t[...] = normed[...].T
    for b in range(BLOCKS):
        hidden_t[b * BLOCK : (b + 1) * BLOCK, :] = hidden[:, b * BLOCK : (b + 1) * BLOCK].T
    for came, relay in zip(far_copies, relays):
        came.wait_recv()
        relay.start()
    near_copy.wait_recv()

    spread = jnp.zeros((80, D), F32)
    for s in range(4):
        if s == 3:
            for copy in relays:
                copy.wait_recv()
        theirs = fall[s]
        swapped = jnp.concatenate(
            [theirs[:, 128:256], theirs[:, 0:128], pltpu.roll(theirs[:, 256:384], 64, 1)], axis=1
        )
        spread = spread + slope_of(own - theirs) + slope_of(own - swapped)
    observed = jnp.concatenate([tg[:, 0:128], tg[:, 0:128], tg[:, 128:256]], axis=1)
    ocean = observed[outputs : outputs + 1]
    slopes = slope_of(own - observed) / MEMBERS - FAIR_WEIGHT / (MEMBERS * (MEMBERS - 1)) * spread
    slopes_b = (slopes * ocean).astype(BF16)

    back = dot(slopes_b, head_t[...], TN)
    d_block[...] = back
    d_block_b[...] = back.astype(BF16)
    grad_reduce = dot(hidden_t[...], d_block_b[...], NN)
    for l in range(LANES):
        put_main(batch1, l * FFN, grad_reduce[:, l * 128 : (l + 1) * 128])
    batch1.start_core()
    batch1.third.start_core()

    grad_head = dot(slopes_b, block[...], NN)
    for r in range(5):
        for l in range(LANES):
            put_small(batch2.g, r * 3 + l, grad_head[r * 16 : r * 16 + 16, l * 128 : (l + 1) * 128])

    d_normed = jnp.zeros((D, D), F32)
    for b in range(BLOCKS):
        columns = slice(b * BLOCK, (b + 1) * BLOCK)
        before[...] = dot(d_block_b[...], wr[columns, :], NT)

        def gate(i, _):
            rows = pl.ds(pl.multiple_of(i * 32, 32), 32)
            d_before[rows, :] = (before[rows, :] * slope[rows, columns]).astype(BF16)
            return 0

        lax.fori_loop(0, 12, gate, 0)
        grad_expand = dot(normed_t[...], d_before[...], NN)
        for l in range(BLOCK // 128):
            put_main(batch2, (b * (BLOCK // 128) + l) * D, grad_expand[:, l * 128 : (l + 1) * 128])
        d_normed = d_normed + dot(d_before[...], we[:, columns], NT)
        if b == 1:
            batch2.start_core((0,))
            batch1.core_to_first()
            batch1.third.core_to_first()
    batch2.start_core((1,))
    batch2.third.start_core()
    batch2.core_to_first((0,))
    d_norm[...] = d_normed

    gk[0, 7:8, :] = jnp.zeros((1, 128), F32)

    def unnorm(i, _):
        rows = pl.ds(pl.multiple_of(i * 64, 64), 64)
        value = [d_norm[rows, l * 128 : (l + 1) * 128] for l in range(LANES)]
        std = [standard[rows, l * 128 : (l + 1) * 128] for l in range(LANES)]
        for l in range(LANES):
            gk[l, 7:8, :] += jnp.sum(value[l] * std[l], axis=0, keepdims=True)
        scaled = [value[l] * gain_row[:, l * 128 : (l + 1) * 128] for l in range(LANES)]
        mean = jnp.sum(scaled[0] + scaled[1] + scaled[2], axis=-1, keepdims=True) / D
        along = jnp.sum(scaled[0] * std[0] + scaled[1] * std[1] + scaled[2] * std[2], axis=-1, keepdims=True) / D
        for l in range(LANES):
            mixed[l, pl.ds(i * 4, 4)] = (recip[rows, :] * (scaled[l] - mean - std[l] * along)).reshape(4, 16, 128)
        return 0

    lax.fori_loop(0, 6, unnorm, 0)
    for l in range(LANES):
        for m in range(2):
            dext[l, m, 3:11, 8:24, :] = mixed[l, m * 8 : m * 8 + 8]
            dext[l, m, 11:15, 8:24, :] = mixed[l, 16 + m * 4 : 20 + m * 4]
    pack(dext, hs2)
    halo2 = halo(hs2, hr2, 6)

    def kernel_grad(l, _):
        for j in range(7):
            near = [ext[l, m, :, 5 + j : 21 + j, :] for m in range(2)]
            for i in range(7):
                part = jnp.zeros((16, 128), F32)
                for m in range(2):
                    part = part + jnp.sum(dext[l, m, 3:15, 8:24, :] * near[m][i : i + 12], axis=0)
                gk[l, i * 8 + j : i * 8 + j + 1, :] = jnp.sum(part, axis=0, keepdims=True)
        return 0

    lax.fori_loop(0, 1, kernel_grad, 0)
    batch2.core_to_first((1,))
    batch2.third.core_to_first()
    lax.fori_loop(1, 3, kernel_grad, 0)
    count = jnp.sum(sea[...].astype(F32)).astype(jnp.int32)
    lane = lax.broadcasted_iota(jnp.int32, (1, 128), 1)
    bits = lax.bitwise_and(lax.shift_right_logical(jnp.broadcast_to(count, (1, 128)), jnp.minimum(lane, 31)), 1)
    gk[0, 15:16, :] = jnp.where(lane < COUNT_BITS, bits, 0).astype(F32)
    for r in range(4):
        for l in range(LANES):
            put_few(few.g, r * 3 + l, gk[l, r * 16 : r * 16 + 16, :])
    few.start()
    batch1.first_to_second()
    batch1.third.first_to_second()
    few.to_x()
    for l in range(LANES):
        for copy in halo2[l]:
            copy.wait_recv()
        unpack(dext, hr2, l)

    def mix_back(i, _):
        l, m = lax.div(i, 2), lax.rem(i, 2)
        mixed_back = correlate(dext, l, m, True)
        mixed[l, pl.ds(m * 8, 8)] = mixed_back[:8]
        mixed[l, pl.ds(16 + m * 4, 4)] = mixed_back[8:]
        return 0

    lax.fori_loop(0, 2, mix_back, 0)
    batch1.second_to_z()
    batch1.third.second_to_y()
    lax.fori_loop(2, 4, mix_back, 0)
    batch2.first_to_second()
    batch2.third.first_to_second()
    few.to_y()
    lax.fori_loop(4, 6, mix_back, 0)
    for l in range(LANES):
        lanes = slice(l * 128, (l + 1) * 128)
        mixed[l] = mixed[l] + d_block[:, lanes].reshape(24, 16, 128)
    direct = []
    for l in range(LANES):
        for m in range(2):
            lanes = slice(l * 128, (l + 1) * 128)
            at = (l * 2 + m) * 2
            direct.append(
                pltpu.make_async_copy(
                    mixed.at[l, m * 8 : m * 8 + 8], direct_out.at[m, 0:8, :, lanes], in_sems.at[at]
                )
            )
            direct.append(
                pltpu.make_async_copy(
                    mixed.at[l, 16 + m * 4 : 20 + m * 4], direct_out.at[m, 8:12, :, lanes], in_sems.at[at + 1]
                )
            )
    for copy in direct:
        copy.start()
    batch1.third.y_to_second()
    batch1.z_to_gather()
    batch2.second_to_z()
    batch2.third.second_to_y()
    few.to_z()
    batch1.third.second_to_first()
    batch1.gather_to_second()
    batch2.third.y_to_second()
    batch2.z_to_gather()
    for each in (few, batch1, batch1.third, batch2, batch2.third):
        each.settle()
    few.to_gather()
    batch1.second_to_first()
    batch2.third.second_to_first()
    batch2.gather_to_second()
    few.to_core()
    batch1.third.first_to_core()
    batch2.second_to_first()
    batch1.first_to_core()
    batch2.third.first_to_core()
    batch2.first_to_core()
    for copy in sum(halo1 + halo2, []) + far_copies + [near_copy] + relays:
        copy.wait_send()
    for copy in direct:
        copy.wait()
    few.finish()
    for batch in (batch1, batch2):
        batch.third.finish()
        batch.finish()


def finish(
    o1, t1, o2, t2, o3, direct, g_inputs, g_kernel, g_gain, g_expand, g_reduce, g_head, kernel, gain, expand, reduce, head, sems
):
    copies = []

    def write(src, dst):
        copy = pltpu.make_async_copy(src, dst, sems.at[len(copies)])
        copy.start()
        copies.append(copy)

    def few(index):
        return o3[index // 6, index % 6 * 16 : index % 6 * 16 + 16, :].astype(F32)

    write(direct, g_inputs)
    rows = [[few(r * 3 + l) for l in range(LANES)] for r in range(4)]
    weight = lax.broadcasted_iota(jnp.int32, (1, 128), 1)
    weight = jnp.where(weight < COUNT_BITS, lax.shift_left(1, jnp.minimum(weight, 15)), 0).astype(F32)
    total = jnp.sum(rows[0][0][15:16] * weight, axis=-1, keepdims=True) / 4
    scale = 1.0 / total

    def main(halves, third, flat, count):
        for at, part, row, take in places(flat, count):
            yield at, take, part_of(halves, third, part)[row : row + take, :].astype(F32) * scale

    for r in range(0, FFN, 512):
        for l in range(LANES):
            for at, take, part in main(o1, t1, l * FFN + r, 512):
                reduce[r + at : r + at + take, l * 128 : (l + 1) * 128] = part
        write(reduce.at[r : r + 512], g_reduce.at[r : r + 512])
    for r in range(0, D, 128):
        for l in range(FFN // 128):
            for at, take, part in main(o2, t2, l * D + r, 128):
                expand[r + at : r + at + take, l * 128 : (l + 1) * 128] = part
        write(expand.at[r : r + 128], g_expand.at[r : r + 128])
    for l in range(LANES):
        lanes = slice(l * 128, (l + 1) * 128)
        for i in range(7):
            at = (i % 2) * 8
            kernel[i, :, lanes] = rows[i // 2][l][at : at + 7] * scale
        gain[lanes] = (rows[0][l][7:8] * scale).reshape(128)
        for r in range(5):
            index = r * 3 + l
            part = o2[1, index * SHARD + MAIN : (index + 1) * SHARD, :].astype(F32) * scale
            count = min(16, head.shape[0] - r * 16)
            head[r * 16 : r * 16 + count, lanes] = part[:count]
    write(kernel, g_kernel)
    write(gain, g_gain)
    write(head, g_head)
    for copy in copies:
        copy.wait()


def on_device(sizes, inputs, target, land_sea, kernel, norm_gain, w_expand, w_reduce, head_weight):
    outputs = target.shape[0]
    by_cell = jnp.transpose(target, (1, 2, 0))
    head_rows = head_weight.T
    anywhere = pl.BlockSpec(memory_space=pl.ANY)
    in_hbm = pl.BlockSpec(memory_space=pltpu.HBM)
    vmem = pltpu.VMEM
    scratch = [
        vmem((24, 16, D), BF16),
        vmem((12, 16, outputs), F32),
        vmem((256, 128), F32),
        vmem((80, 256), F32),
        vmem((12, 16), jnp.int32),
        vmem((LANES, 7, 7, 128), F32),
        vmem((D,), F32),
        vmem((D, FFN), BF16),
        vmem((FFN, D), BF16),
        vmem((outputs, D), BF16),
        vmem((LANES, 2, 18, 32, 128), F32),
        vmem((LANES, 2, 18, 32, 128), F32),
        vmem((2, LANES, 80, 128), F32),
        vmem((2, LANES, 80, 128), BF16),
        vmem((2, LANES, 80, 128), BF16),
        vmem((2, LANES, 80, 128), BF16),
        vmem((2, LANES, 80, 128), BF16),
        vmem((LANES, 24, 16, 128), F32),
        vmem((D, D), F32),
        vmem((D, 128), F32),
        vmem((D, D), BF16),
        vmem((D, BLOCK), F32),
        vmem((D, FFN), F32),
        vmem((D, FFN), BF16),
        vmem((FFN, D), BF16),
        vmem((D, D), BF16),
        vmem((D, D), BF16),
        vmem((80, D), BF16),
        vmem((4, 80, D), F32),
        vmem((D, D), F32),
        vmem((D, D), BF16),
        vmem((D, BLOCK), BF16),
        vmem((D, D), F32),
        vmem((LANES, 64, 128), F32),
        pltpu.SemaphoreType.DMA((13,)),
        pltpu.SemaphoreType.DMA((12,)),
        pltpu.SemaphoreType.DMA((12,)),
        pltpu.SemaphoreType.DMA((5,)),
        pltpu.SemaphoreType.DMA((5,)),
    ]
    batch = reduce_scratch(sizes)
    batch = [*batch, *third_scratch(sizes)]
    scratch += batch + batch + few_scratch(sizes)
    operands = [inputs, by_cell, land_sea, kernel, norm_gain, w_expand, w_reduce, head_rows]
    operands = [pltpu.with_memory_space_constraint(operand, pltpu.HBM) for operand in operands]
    *reduced, direct = pl.pallas_call(
        lambda *refs: work(sizes, *refs),
        out_shape=(
            *(jax.ShapeDtypeStruct((2, rows, 128), BF16) for rows in (HALF, THIRD // 2, HALF, THIRD // 2, FEW)),
            jax.ShapeDtypeStruct(inputs.shape, F32),
        ),
        in_specs=[in_hbm] * 8,
        out_specs=(anywhere,) * 6,
        scratch_shapes=scratch,
        compiler_params=pltpu.CompilerParams(
            collective_id=0, has_side_effects=True, vmem_limit_bytes=48 * 1024 * 1024
        ),
        name="block_pass",
    )(*operands)
    in_vmem = pl.BlockSpec(memory_space=pltpu.VMEM)
    shapes = (kernel.shape, norm_gain.shape, w_expand.shape, w_reduce.shape, head_rows.shape)
    g_inputs, g_kernel, g_gain, g_expand, g_reduce, g_head = pl.pallas_call(
        finish,
        out_shape=tuple(jax.ShapeDtypeStruct(shape, F32) for shape in (inputs.shape, *shapes)),
        in_specs=[in_vmem] * 5 + [anywhere],
        out_specs=(anywhere,) * 6,
        scratch_shapes=[vmem(shape, F32) for shape in shapes] + [pltpu.SemaphoreType.DMA((11,))],
        compiler_params=pltpu.CompilerParams(vmem_limit_bytes=32 * 1024 * 1024),
        name="finish",
    )(*reduced, direct)
    return g_inputs, g_kernel, g_gain, g_expand, g_reduce, g_head.T


def solution(mesh):
    sizes = grid_of(mesh)
    return jax.shard_map(
        lambda *arrays: on_device(sizes, *arrays),
        mesh=mesh,
        in_specs=(
            P("ens", None, "tile", None),
            P(None, None, "tile"),
            P(None, "tile"),
            P(),
            P(),
            P(),
            P(),
            P(),
        ),
        out_specs=(P("ens", None, "tile", None), P(), P(), P(), P(), P()),
        check_vma=False,
    )
```

```python
import jax
import jax.numpy as jnp
from jax import lax
from jax.experimental import pallas as pl
from jax.experimental.pallas import tpu as pltpu
from jax.sharding import PartitionSpec as P

FAIR_WEIGHT = 0.95
SMOOTHING = 0.5
NORM_EPS = 1e-06
D = 384
FFN = 1536
LANES = 3
BLOCK = 512
BLOCKS = FFN // BLOCK
MEMBERS = 8
HALF = 2048
SHARD = 64
MAIN = 48
SLOTS = 48
THIRD = 1024
COUNT_BITS = 8
FEW = 128
F32 = jnp.float32
BF16 = jnp.bfloat16


def grid_of(mesh):
    tiles = mesh.shape["tile"]
    side = 4 if tiles == 64 else 2
    return side, side, tiles // (side * side)


def dot(a, b, dims):
    return lax.dot_general(a, b, (dims, ((), ())), preferred_element_type=F32)


NN = ((1,), (0,))
NT = ((1,), (1,))
TN = ((0,), (0,))


class Place:
    def __init__(self, sizes):
        self.nx, self.ny, self.nzh = sizes
        self.nz = 2 * self.nzh
        self.tiles = self.nx * self.ny * self.nzh
        self.ens = lax.axis_index("ens")
        self.tile = lax.axis_index("tile")
        self.core = lax.rem(self.ens, 2)
        self.zl = lax.div(self.ens, 2)
        self.zh = lax.rem(self.tile, self.nzh)
        self.x = lax.rem(lax.div(self.tile, self.nzh), self.nx)
        self.y = lax.div(self.tile, self.nzh * self.nx)
        self.z = self.zh * 2 + self.zl

    def at(self, x, y, z, core):
        return (lax.rem(z, 2) * 2 + core, (y * self.nx + x) * self.nzh + lax.div(z, 2))

    def along_x(self, d):
        return self.at(lax.rem(self.x + d, self.nx), self.y, self.z, self.core)

    def along_y(self, d):
        return self.at(self.x, lax.rem(self.y + d, self.ny), self.z, self.core)

    def along_z(self, d):
        return self.at(self.x, self.y, lax.rem(self.z + d, self.nz), self.core)

    def other_core(self):
        return self.at(self.x, self.y, self.z, 1 - self.core)

    def along_tile(self, d):
        return (self.ens, lax.rem(self.tile + d + self.tiles, self.tiles))

    def along_ens(self, d):
        return (lax.rem(self.ens + d, 4), self.tile)

    def everyone(self):
        peers = [self.along_tile(1), self.along_tile(-1)]
        peers += [self.along_ens(d) for d in range(1, 4)]
        peers += [self.along_x(d) for d in range(1, self.nx)]
        peers += [self.along_y(d) for d in range(1, self.ny)]
        peers += [self.along_z(d) for d in range(1, self.nz)]
        return peers


def remote(src, dst, send, recv, to):
    return pltpu.make_async_remote_copy(
        src_ref=src,
        dst_ref=dst,
        send_sem=send,
        recv_sem=recv,
        device_id=to,
        device_id_type=pl.DeviceIdType.MESH,
    )


def far_first(size):
    return sorted(range(1, size), key=lambda d: -min(d, size - d))


def summed(parts):
    value = None
    for part in parts:
        part = part.astype(F32)
        value = part if value is None else value + part
    return value.astype(BF16)


def from_row(start, count):
    return pl.ds(pl.multiple_of(start, 16), count)


class Group:
    def __init__(self, owner, whole, apart=False):
        self.owner, self.whole, self.apart = owner, whole, apart
        self.send, self.recv = owner.send.at[owner.slot()], owner.recv.at[owner.slot()]
        self.copies = []
        owner.groups.append(self)

    def start(self, src, dst, to):
        recv = self.owner.recv.at[self.owner.slot()] if self.apart else self.recv
        copy = remote(src, dst, self.send, recv, to)
        copy.start()
        self.copies.append(copy)
        self.to = to

    def all(self):
        return remote(self.whole, self.whole, self.send, self.recv, self.to)

    def received(self):
        self.all().wait_recv()

    def sent(self):
        self.all().wait_send()


class Copies:
    def __init__(self, send, recv):
        self.send, self.recv = send, recv
        self.slots = 0
        self.groups = []

    def slot(self):
        self.slots += 1
        return self.slots - 1

    def one(self, src, dst, to):
        group = Group(self, src)
        group.start(src, dst, to)
        return group

    def keep(self, src, dst):
        copy = pltpu.make_async_copy(src, dst, self.send.at[self.slot()])
        copy.start()
        return copy

    def settle(self):
        for group in self.groups:
            group.sent()
        self.groups = []


class Reduce(Copies):
    def __init__(self, place, refs, out, third):
        self.third = third
        self.p = place
        self.g, self.rc, self.s1, self.r1, self.s2, self.r2, self.sz, self.rz, self.oz, *sems = refs
        super().__init__(*sems)
        self.out = out
        self.n, self.nz = place.nx, place.nz
        self.c_rows = HALF // 2
        self.p_rows = self.c_rows // self.n
        self.q_rows = self.p_rows // self.n
        self.z_rows = 2 * self.q_rows // self.nz
        self.order, self.z_order = far_first(self.n), far_first(self.nz)
        self.core = [None, None]
        self.in_first = [None, None]
        self.in_second = [None, None]

    def first(self, h):
        return self.p.x if h == 0 else self.p.y

    def second(self, h):
        return self.p.y if h == 0 else self.p.x

    def to_first(self, h, d):
        return self.p.along_x(d) if h == 0 else self.p.along_y(d)

    def to_second(self, h, d):
        return self.p.along_y(d) if h == 0 else self.p.along_x(d)

    def start_core(self, halves=(0, 1)):
        other = from_row((1 - self.p.core) * self.c_rows, self.c_rows)
        for h in halves:
            self.core[h] = self.one(self.g.at[h, other], self.rc.at[h], self.p.other_core())

    def core_to_first(self, halves=(0, 1)):
        for h in halves:
            self.core[h].received()
            group = self.in_first[h] = Group(self, self.r1.at[h])
            for d in (*self.order, 0):
                at = lax.rem(self.first(h) + d, self.n) * self.p_rows
                piece = from_row(at, self.p_rows)
                mine = from_row(self.p.core * self.c_rows + at, self.p_rows)
                self.s1[h, piece, :] = summed([self.g[h, mine, :], self.rc[h, piece, :]])
                if d:
                    group.start(self.s1.at[h, piece], self.r1.at[h, d - 1], self.to_first(h, d))

    def first_to_second(self, halves=(0, 1)):
        for h in halves:
            self.in_first[h].received()
            mine = self.s1[h, from_row(self.first(h) * self.p_rows, self.p_rows), :]
            self.s2[h] = summed([mine, *(self.r1[h, d] for d in range(self.n - 1))])
            group = self.in_second[h] = Group(self, self.r2.at[h])
            for d in self.order:
                piece = from_row(lax.rem(self.second(h) + d, self.n) * self.q_rows, self.q_rows)
                group.start(self.s2.at[h, piece], self.r2.at[h, d - 1], self.to_second(h, d))

    def second_to_z(self):
        for h in range(2):
            self.in_second[h].received()
            mine = self.s2[h, from_row(self.second(h) * self.q_rows, self.q_rows), :]
            self.sz[h * self.q_rows : (h + 1) * self.q_rows, :] = summed(
                [mine, *(self.r2[h, d] for d in range(self.n - 1))]
            )
        self.in_z = Group(self, self.rz)
        for d in self.z_order:
            piece = from_row(lax.rem(self.p.z + d, self.nz) * self.z_rows, self.z_rows)
            self.in_z.start(self.sz.at[piece], self.rz.at[d - 1], self.p.along_z(d))

    def z_to_gather(self):
        self.in_z.received()
        mine = from_row(self.p.z * self.z_rows, self.z_rows)
        self.oz[mine, :] = summed([self.sz[mine, :], *(self.rz[d] for d in range(self.nz - 1))])
        self.out_z = Group(self, self.oz.at[pl.ds(0, (self.nz - 1) * self.z_rows)])
        for d in self.z_order:
            self.out_z.start(self.oz.at[mine], self.oz.at[mine], self.p.along_z(d))

    def shard(self, h):
        return self.p.core * self.c_rows + self.first(h) * self.p_rows + self.second(h) * self.q_rows

    def gather_to_second(self):
        self.out_z.received()
        self.out_second = []
        self.kept = []
        for h in range(2):
            at = from_row(self.shard(h), self.q_rows)
            mine = self.oz.at[pl.ds(h * self.q_rows, self.q_rows)]
            group = Group(self, self.out.at[h, pl.ds(0, (self.n - 1) * self.q_rows)])
            self.out_second.append(group)
            for d in self.order:
                group.start(mine, self.out.at[h, at], self.to_second(h, d))
            self.kept.append(self.keep(mine, self.out.at[h, at]))

    def piece(self, h, d):
        at = lax.rem(self.first(h) + d, self.n) * self.p_rows
        return self.out.at[h, from_row(self.p.core * self.c_rows + at, self.p_rows)]

    def second_to_first(self):
        self.out_first = []
        self.out_core = []
        for h in range(2):
            self.out_second[h].received()
            self.kept[h].wait()
            mine = self.piece(h, 0)
            group = Group(self, self.out.at[h, pl.ds(0, (self.n - 1) * self.p_rows)], apart=True)
            self.out_first.append(group)
            for d in self.order:
                group.start(mine, mine, self.to_first(h, d))
            group = Group(self, self.out.at[h, pl.ds(0, self.c_rows)])
            self.out_core.append(group)
            group.start(mine, mine, self.p.other_core())

    def first_to_core(self):
        for k, d in enumerate(self.order):
            for h in range(2):
                self.out_first[h].copies[k].wait_recv()
                came = self.piece(h, self.n - d)
                self.out_core[h].start(came, came, self.p.other_core())

    def finish(self):
        for group in self.out_core:
            group.received()
        self.settle()


class Few(Copies):
    def __init__(self, place, refs, out):
        self.p = p = place
        self.g, self.rc, self.s, self.rx, self.sy, self.sz, self.o, *sems = refs
        super().__init__(*sems)
        self.out = out
        self.x_rows = FEW // p.nx

    def piece(self, d):
        return from_row(lax.rem(self.p.x + d, self.p.nx) * self.x_rows, self.x_rows)

    def start(self):
        self.got = self.one(self.g.at[1 - self.p.core], self.rc, self.p.other_core())

    def to_x(self):
        p = self.p
        self.got.received()
        self.s[...] = summed([self.g[p.core], self.rc[...]])
        self.got = Group(self, self.rx)
        for d in far_first(p.nx):
            self.got.start(self.s.at[self.piece(d)], self.rx.at[d - 1], p.along_x(d))

    def to_y(self):
        p = self.p
        self.got.received()
        self.sy[p.y] = summed([self.s[self.piece(0), :], *(self.rx[d] for d in range(p.nx - 1))])
        self.got = Group(self, self.sy.at[pl.ds(0, p.ny - 1)])
        for d in far_first(p.ny):
            self.got.start(self.sy.at[p.y], self.sy.at[p.y], p.along_y(d))

    def to_z(self):
        p = self.p
        self.got.received()
        self.sz[p.z] = summed(self.sy[k] for k in range(p.ny))
        self.got = Group(self, self.sz.at[pl.ds(0, p.nz - 1)])
        for d in far_first(p.nz):
            self.got.start(self.sz.at[p.z], self.sz.at[p.z], p.along_z(d))

    def to_gather(self):
        p = self.p
        self.got.received()
        self.o[...] = summed(self.sz[k] for k in range(p.nz))
        mine = self.out.at[p.core, self.piece(0)]
        self.kept = self.keep(self.o, mine)
        self.got = Group(self, self.out.at[0, pl.ds(0, (p.nx - 1) * self.x_rows)])
        for d in far_first(p.nx):
            self.got.start(self.o, mine, p.along_x(d))
        self.last = Group(self, self.out.at[0])
        self.last.start(self.o, mine, p.other_core())

    def to_core(self):
        p = self.p
        self.got.received()
        for d in range(1, p.nx):
            came = self.out.at[p.core, self.piece(d)]
            self.last.start(came, came, p.other_core())

    def finish(self):
        self.last.received()
        self.kept.wait()
        self.settle()


class Third(Copies):
    def __init__(self, place, refs, out):
        self.p = p = place
        self.g, self.rc, self.s1, self.r1, self.s2, self.r2, self.sy, self.o, *sems = refs
        super().__init__(*sems)
        self.out = out
        self.z_rows = THIRD // 2 // p.nz
        self.x_rows = self.z_rows // p.nx
        self.order = far_first(p.nz)

    def piece(self, d):
        return from_row(lax.rem(self.p.z + d, self.p.nz) * self.z_rows, self.z_rows)

    def start_core(self):
        self.got = self.one(self.g.at[1 - self.p.core], self.rc, self.p.other_core())

    def core_to_first(self):
        p = self.p
        self.got.received()
        self.s1[...] = summed([self.g[p.core], self.rc[...]])
        self.got = Group(self, self.r1)
        for d in self.order:
            self.got.start(self.s1.at[self.piece(d)], self.r1.at[d - 1], p.along_z(d))

    def first_to_second(self):
        p = self.p
        self.got.received()
        self.s2[...] = summed([self.s1[self.piece(0), :], *(self.r1[k] for k in range(p.nz - 1))])
        self.got = Group(self, self.r2)
        for d in far_first(p.nx):
            piece = from_row(lax.rem(p.x + d, p.nx) * self.x_rows, self.x_rows)
            self.got.start(self.s2.at[piece], self.r2.at[d - 1], p.along_x(d))

    def second_to_y(self):
        p = self.p
        self.got.received()
        mine = self.s2[from_row(p.x * self.x_rows, self.x_rows), :]
        self.sy[p.y] = summed([mine, *(self.r2[d] for d in range(p.nx - 1))])
        self.got = Group(self, self.sy.at[pl.ds(0, p.ny - 1)])
        for d in far_first(p.ny):
            self.got.start(self.sy.at[p.y], self.sy.at[p.y], p.along_y(d))

    def y_to_second(self):
        p = self.p
        self.got.received()
        self.o[...] = summed(self.sy[k] for k in range(p.ny))
        mine = self.out.at[p.core, from_row(p.z * self.z_rows + p.x * self.x_rows, self.x_rows)]
        self.kept = self.keep(self.o, mine)
        self.got = Group(self, self.out.at[0, pl.ds(0, (p.nx - 1) * self.x_rows)])
        for d in far_first(p.nx):
            self.got.start(self.o, mine, p.along_x(d))

    def second_to_first(self):
        p = self.p
        self.got.received()
        self.kept.wait()
        mine = self.out.at[p.core, self.piece(0)]
        self.got = Group(self, self.out.at[0, pl.ds(0, (p.nz - 1) * self.z_rows)])
        for d in self.order:
            self.got.start(mine, mine, p.along_z(d))

    def first_to_core(self):
        p = self.p
        self.got.received()
        self.last = self.one(self.out.at[p.core], self.out.at[p.core], p.other_core())

    def finish(self):
        self.last.received()
        self.settle()


def third_scratch(sizes):
    nx, ny, nzh = sizes
    nz = 2 * nzh
    z_rows = THIRD // 2 // nz
    x_rows = z_rows // nx
    shapes = [
        (2, THIRD // 2, 128), (THIRD // 2, 128), (THIRD // 2, 128), (nz - 1, z_rows, 128), (z_rows, 128),
        (nx - 1, x_rows, 128), (ny, x_rows, 128), (x_rows, 128),
    ]
    return [pltpu.VMEM(shape, BF16) for shape in shapes] + [pltpu.SemaphoreType.DMA((SLOTS,))] * 2


def few_scratch(sizes):
    nx, ny, nzh = sizes
    x_rows = FEW // nx
    shapes = [
        (2, FEW, 128), (FEW, 128), (FEW, 128), (nx - 1, x_rows, 128), (ny, x_rows, 128), (2 * nzh, x_rows, 128),
        (x_rows, 128),
    ]
    return [pltpu.VMEM(shape, BF16) for shape in shapes] + [pltpu.SemaphoreType.DMA((SLOTS,))] * 2


def reduce_scratch(sizes):
    n, _, nzh = sizes
    nz = 2 * nzh
    c_rows = HALF // 2
    p_rows = c_rows // n
    q_rows = p_rows // n
    z_rows = 2 * q_rows // nz
    shapes = [
        (2, HALF, 128), (2, c_rows, 128), (2, c_rows, 128), (2, n - 1, p_rows, 128), (2, p_rows, 128),
        (2, n - 1, q_rows, 128), (2 * q_rows, 128), (nz - 1, z_rows, 128), (2 * q_rows, 128),
    ]
    return [pltpu.VMEM(shape, BF16) for shape in shapes] + [pltpu.SemaphoreType.DMA((SLOTS,))] * 2


def slope_of(offset):
    return offset * lax.rsqrt(offset * offset + SMOOTHING * SMOOTHING)


def places(flat, count):
    at = 0
    while at < count:
        here = flat + at
        if here < HALF:
            take, part, row = HALF - here, 0, here
        elif here < HALF + 32 * MAIN:
            shard, inner = divmod(here - HALF, MAIN)
            take, part, row = MAIN - inner, 1, shard * SHARD + inner
        else:
            row = here - HALF - 32 * MAIN
            part, row = 2 + row // (THIRD // 2), row % (THIRD // 2)
            take = THIRD // 2 - row
        take = min(take, count - at)
        yield at, part, row, take
        at += take


def part_of(halves, third, part):
    return halves.at[part] if part < 2 else third.at[part - 2]


def put_main(batch, flat, value):
    for at, part, row, take in places(flat, value.shape[0]):
        part_of(batch.g, batch.third.g, part)[row : row + take, :] = value[at : at + take].astype(BF16)


def put_small(batch, index, value):
    batch[1, index * SHARD + MAIN : (index + 1) * SHARD, :] = value.astype(BF16)


def put_few(batch, index, value):
    batch[index // 6, index % 6 * 16 : index % 6 * 16 + 16, :] = value.astype(BF16)


def work(sizes, *refs):
    (
        x_hbm, target_hbm, sea_hbm, kernel_hbm, gain_hbm, expand_hbm, reduce_hbm, head_hbm,
        out1, third1, out2, third2, out3, direct_out,
        xb, target, tall, tg, sea, taps, gain, we, wr, head,
        ext, dext, rim, hs, hr, hs2, hr2, mixed, standard, recip, normed, before, slope, hidden, hidden_t, normed_t,
        block, head_t, fall, d_block, d_block_b, d_before, d_norm, gk,
        in_sems, halo_send, halo_recv, ens_send, ens_recv,
        *rest,
    ) = refs
    place = Place(sizes)
    few = Few(place, rest[-9:], out3)
    pieces = (len(rest) - 9) // 2
    batch1, batch2 = (
        Reduce(place, mine[:-10], out, Third(place, mine[-10:], third))
        for mine, out, third in ((rest[:pieces], out1, third1), (rest[pieces : 2 * pieces], out2, third2))
    )

    loads = [
        pltpu.make_async_copy(x_hbm.at[0, 0:8], xb.at[0:8], in_sems.at[0]),
        pltpu.make_async_copy(x_hbm.at[1, 0:8], xb.at[8:16], in_sems.at[1]),
        pltpu.make_async_copy(x_hbm.at[0, 8:12], xb.at[16:20], in_sems.at[2]),
        pltpu.make_async_copy(x_hbm.at[1, 8:12], xb.at[20:24], in_sems.at[3]),
    ]
    tap_loads = [
        pltpu.make_async_copy(kernel_hbm.at[:, :, l * 128 : (l + 1) * 128], taps.at[l], in_sems.at[4 + l])
        for l in range(LANES)
    ]
    later = [
        pltpu.make_async_copy(gain_hbm, gain, in_sems.at[7]),
        pltpu.make_async_copy(head_hbm, head, in_sems.at[8]),
        pltpu.make_async_copy(expand_hbm, we, in_sems.at[9]),
        pltpu.make_async_copy(reduce_hbm, wr, in_sems.at[10]),
        pltpu.make_async_copy(target_hbm, target, in_sems.at[11]),
        pltpu.make_async_copy(sea_hbm, sea, in_sems.at[12]),
    ]
    for copy in loads + tap_loads + later:
        copy.start()

    barrier = pltpu.get_barrier_semaphore()
    peers = place.everyone()
    for peer in peers:
        pl.semaphore_signal(barrier, inc=1, device_id=peer, device_id_type=pl.DeviceIdType.MESH)

    def clear(i, _):
        l, m = lax.div(i, 2), lax.rem(i, 2)
        for ref in (ext, dext):
            ref[l, m, 0:3] = jnp.zeros((3, 32, 128), F32)
            ref[l, m, 15:18] = jnp.zeros((3, 32, 128), F32)
        ext[l, m, 3:15, 0:8] = jnp.zeros((12, 8, 128), F32)
        ext[l, m, 3:15, 24:32] = jnp.zeros((12, 8, 128), F32)
        return 0

    lax.fori_loop(0, 2 * LANES, clear, 0)
    gk[...] = jnp.zeros_like(gk)
    rim[...] = jnp.zeros_like(rim)
    few.g[...] = jnp.zeros_like(few.g)
    for copy in loads:
        copy.wait()
    for l in range(LANES):
        lanes = slice(l * 128, (l + 1) * 128)
        for m in range(2):
            ext[l, m, 3:11, 8:24, :] = xb[m * 8 : m * 8 + 8, :, lanes].astype(F32)
            ext[l, m, 11:15, 8:24, :] = xb[16 + m * 4 : 20 + m * 4, :, lanes].astype(F32)

    def rim_rows(m, j):
        return slice((m * 3 + j) * 12, (m * 3 + j) * 12 + 12)

    def pack(field, out):
        for side, col in ((0, 8), (1, 21)):
            for m in range(2):
                for j in range(3):
                    for l in range(LANES):
                        rim[side, l, rim_rows(m, j)] = field[l, m, 3:15, col + j, :]
        out[...] = rim[...].astype(BF16)

    def unpack(field, got, l):
        for side, col in ((0, 5), (1, 24)):
            rim[side, l] = got[side, l].astype(F32)
            for m in range(2):
                for j in range(3):
                    field[l, m, 3:15, col + j, :] = rim[side, l, rim_rows(m, j)]

    def halo(out, got, at):
        copies = [
            [
                remote(out.at[side, l], got.at[1 - side, l], halo_send.at[at + s], halo_recv.at[at + s], place.along_tile(to))
                for s, (side, to) in enumerate(((0, -1), (1, 1)), 2 * l)
            ]
            for l in range(LANES)
        ]
        for pair in copies:
            for copy in pair:
                copy.start()
        return copies

    pack(ext, hs)
    pl.semaphore_wait(barrier, len(peers))
    halo1 = halo(hs, hr, 0)

    for copy in tap_loads + later:
        copy.wait()
    for index in range(32):
        put_small(batch1.g, index, jnp.zeros((16, 128), F32))
        if index >= 15:
            put_small(batch2.g, index, jnp.zeros((16, 128), F32))
    outputs = head.shape[0]
    head_t[...] = jnp.concatenate([head[...].astype(F32), jnp.zeros((80 - outputs, D), F32)], axis=0).astype(BF16)
    diagonal = lax.broadcasted_iota(jnp.int32, (16, 16), 0) == lax.broadcasted_iota(jnp.int32, (16, 16), 1)
    tall[...] = jnp.zeros_like(tall)
    for a in range(12):
        water = jnp.broadcast_to(sea[a : a + 1, :].astype(F32), (16, 16))
        water = jnp.sum(jnp.where(diagonal, water, 0.0), axis=1, keepdims=True)
        for at in (a * 16,) if a < 8 else (a * 16, a * 16 + 64):
            tall[at : at + 16, 0:outputs] = target[a]
            tall[at : at + 16, outputs : outputs + 1] = water
    tg[...] = tall[...].T[0:80]
    def correlate(field, l, m, flip):
        total = jnp.zeros((12, 16, 128), F32)
        for j in range(7):
            shifted = field[l, m, :, 5 + j : 21 + j, :]
            for i in range(7):
                tap = taps[l, 6 - i, 6 - j : 7 - j, :] if flip else taps[l, i, j : j + 1, :]
                total = total + shifted[i : i + 12] * tap
        return total

    def mix(i, _):
        l, m = lax.div(i, 2), lax.rem(i, 2)
        total = correlate(ext, l, m, False)
        mixed[l, pl.ds(m * 8, 8)] = total[:8]
        mixed[l, pl.ds(16 + m * 4, 4)] = total[8:]
        return 0

    lax.fori_loop(0, 2 * LANES, mix, 0)
    sublane = lax.broadcasted_iota(jnp.int32, (18, 8, 128), 1)

    def edges(l, m):
        for first, taps_in in ((0, (0, 1, 2)), (8, (4, 5, 6))):
            total = jnp.zeros((12, 8, 128), F32)
            for j in taps_in:
                outside = sublane < 3 - j if first == 0 else sublane >= 11 - j
                shifted = jnp.where(outside, ext[l, m, :, 5 + first + j : 13 + first + j, :], 0.0)
                for i in range(7):
                    total = total + shifted[i : i + 12] * taps[l, i, j : j + 1, :]
            mixed[l, pl.ds(m * 8, 8), first : first + 8] += total[:8]
            mixed[l, pl.ds(16 + m * 4, 4), first : first + 8] += total[8:]

    for l in range(LANES):
        for copy in halo1[l]:
            copy.wait_recv()
        unpack(ext, hr, l)
        lax.fori_loop(0, 2, lambda m, _, l=l: (edges(l, m), 0)[1], 0)

    gain_row = gain[...].reshape(1, D)

    def norm(i, _):
        rows = pl.ds(pl.multiple_of(i * 64, 64), 64)
        parts = [mixed[l, pl.ds(i * 4, 4)].reshape(64, 128) for l in range(LANES)]
        mean = jnp.sum(parts[0] + parts[1] + parts[2], axis=-1, keepdims=True) / D
        centre = [part - mean for part in parts]
        square = centre[0] * centre[0] + centre[1] * centre[1] + centre[2] * centre[2]
        scale = lax.rsqrt(jnp.sum(square, axis=-1, keepdims=True) / D + NORM_EPS)
        recip[rows, :] = jnp.broadcast_to(scale, (64, 128))
        for l in range(LANES):
            lanes = slice(l * 128, (l + 1) * 128)
            value = centre[l] * scale
            standard[rows, lanes] = value
            normed[rows, lanes] = (value * gain_row[:, lanes]).astype(BF16)
        return 0

    lax.fori_loop(0, 6, norm, 0)

    total = xb[...].reshape(D, D).astype(F32)
    for b in range(BLOCKS):
        columns = slice(b * BLOCK, (b + 1) * BLOCK)
        before[...] = dot(normed[...], we[:, columns], NN)

        def gelu(i, _):
            rows = pl.ds(pl.multiple_of(i * 32, 32), 32)
            v = before[rows, :]
            square = v * v
            scale = 0.7978845608028654
            t = jnp.tanh(v * (scale + (scale * 0.044715) * square))
            half = 0.5 + 0.5 * t
            hidden[rows, columns] = (v * half).astype(BF16)
            slope[rows, columns] = half + (0.5 * v) * (1.0 - t * t) * (scale + (scale * 3 * 0.044715) * square)
            return 0

        lax.fori_loop(0, 12, gelu, 0)
        total = total + dot(hidden[:, columns], wr[columns, :], NN)
    block[...] = total.astype(BF16)

    own = dot(head_t[...], block[...], NT)
    fall[0] = own
    far = place.along_ens(2)
    far_copies = [
        remote(fall.at[0, pl.ds(r, 40)], fall.at[2, pl.ds(r, 40)], ens_send.at[k], ens_recv.at[k], far)
        for k, r in enumerate((0, 40))
    ]
    near_copy = remote(fall.at[0], fall.at[1], ens_send.at[2], ens_recv.at[2], place.other_core())
    relays = [
        remote(fall.at[2, pl.ds(r, 40)], fall.at[3, pl.ds(r, 40)], ens_send.at[3 + k], ens_recv.at[3 + k], place.other_core())
        for k, r in enumerate((0, 40))
    ]
    for copy in [*far_copies, near_copy]:
        copy.start()
    normed_t[...] = normed[...].T
    for b in range(BLOCKS):
        hidden_t[b * BLOCK : (b + 1) * BLOCK, :] = hidden[:, b * BLOCK : (b + 1) * BLOCK].T
    for came, relay in zip(far_copies, relays):
        came.wait_recv()
        relay.start()
    near_copy.wait_recv()

    spread = jnp.zeros((80, D), F32)
    for s in range(4):
        if s == 3:
            for copy in relays:
                copy.wait_recv()
        theirs = fall[s]
        swapped = jnp.concatenate(
            [theirs[:, 128:256], theirs[:, 0:128], pltpu.roll(theirs[:, 256:384], 64, 1)], axis=1
        )
        spread = spread + slope_of(own - theirs) + slope_of(own - swapped)
    observed = jnp.concatenate([tg[:, 0:128], tg[:, 0:128], tg[:, 128:256]], axis=1)
    ocean = observed[outputs : outputs + 1]
    slopes = slope_of(own - observed) / MEMBERS - FAIR_WEIGHT / (MEMBERS * (MEMBERS - 1)) * spread
    slopes_b = (slopes * ocean).astype(BF16)

    back = dot(slopes_b, head_t[...], TN)
    d_block[...] = back
    d_block_b[...] = back.astype(BF16)
    grad_reduce = dot(hidden_t[...], d_block_b[...], NN)
    for l in range(LANES):
        put_main(batch1, l * FFN, grad_reduce[:, l * 128 : (l + 1) * 128])
    batch1.start_core()
    batch1.third.start_core()

    grad_head = dot(slopes_b, block[...], NN)
    for r in range(5):
        for l in range(LANES):
            put_small(batch2.g, r * 3 + l, grad_head[r * 16 : r * 16 + 16, l * 128 : (l + 1) * 128])

    for b in range(BLOCKS):
        columns = slice(b * BLOCK, (b + 1) * BLOCK)
        before[...] = dot(d_block_b[...], wr[columns, :], NT)

        def gate(i, _):
            rows = pl.ds(pl.multiple_of(i * 32, 32), 32)
            d_before[rows, columns] = (before[rows, :] * slope[rows, columns]).astype(BF16)
            return 0

        lax.fori_loop(0, 12, gate, 0)
        grad_expand = dot(normed_t[...], d_before[:, columns], NN)
        for l in range(BLOCK // 128):
            put_main(batch2, (b * (BLOCK // 128) + l) * D, grad_expand[:, l * 128 : (l + 1) * 128])
        if b == 1:
            batch2.start_core((0,))
            batch1.core_to_first()
            batch1.third.core_to_first()
    batch2.start_core((1,))
    batch2.third.start_core()
    batch2.core_to_first((0,))
    d_norm[...] = dot(d_before[...], we[...], NT)
    batch2.core_to_first((1,))
    batch2.third.core_to_first()

    gk[0, 7:8, :] = jnp.zeros((1, 128), F32)

    def unnorm(i, _):
        rows = pl.ds(pl.multiple_of(i * 64, 64), 64)
        value = [d_norm[rows, l * 128 : (l + 1) * 128] for l in range(LANES)]
        std = [standard[rows, l * 128 : (l + 1) * 128] for l in range(LANES)]
        for l in range(LANES):
            gk[l, 7:8, :] += jnp.sum(value[l] * std[l], axis=0, keepdims=True)
        scaled = [value[l] * gain_row[:, l * 128 : (l + 1) * 128] for l in range(LANES)]
        mean = jnp.sum(scaled[0] + scaled[1] + scaled[2], axis=-1, keepdims=True) / D
        along = jnp.sum(scaled[0] * std[0] + scaled[1] * std[1] + scaled[2] * std[2], axis=-1, keepdims=True) / D
        for l in range(LANES):
            mixed[l, pl.ds(i * 4, 4)] = (recip[rows, :] * (scaled[l] - mean - std[l] * along)).reshape(4, 16, 128)
        return 0

    lax.fori_loop(0, 6, unnorm, 0)
    for l in range(LANES):
        for m in range(2):
            dext[l, m, 3:11, 8:24, :] = mixed[l, m * 8 : m * 8 + 8]
            dext[l, m, 11:15, 8:24, :] = mixed[l, 16 + m * 4 : 20 + m * 4]
    pack(dext, hs2)
    halo2 = halo(hs2, hr2, 6)

    def kernel_grad(l, _):
        for j in range(7):
            near = [ext[l, m, :, 5 + j : 21 + j, :] for m in range(2)]
            for i in range(7):
                part = jnp.zeros((16, 128), F32)
                for m in range(2):
                    part = part + jnp.sum(dext[l, m, 3:15, 8:24, :] * near[m][i : i + 12], axis=0)
                gk[l, i * 8 + j : i * 8 + j + 1, :] = jnp.sum(part, axis=0, keepdims=True)
        return 0

    batch1.first_to_second()
    batch2.first_to_second((0,))
    lax.fori_loop(0, 1, kernel_grad, 0)
    batch1.third.first_to_second()
    batch2.first_to_second((1,))
    batch1.second_to_z()
    lax.fori_loop(1, 2, kernel_grad, 0)
    batch2.third.first_to_second()
    lax.fori_loop(2, 3, kernel_grad, 0)
    count = jnp.sum(sea[...].astype(F32)).astype(jnp.int32)
    lane = lax.broadcasted_iota(jnp.int32, (1, 128), 1)
    bits = lax.bitwise_and(lax.shift_right_logical(jnp.broadcast_to(count, (1, 128)), jnp.minimum(lane, 31)), 1)
    gk[0, 15:16, :] = jnp.where(lane < COUNT_BITS, bits, 0).astype(F32)
    for r in range(4):
        for l in range(LANES):
            put_few(few.g, r * 3 + l, gk[l, r * 16 : r * 16 + 16, :])
    few.start()
    batch2.second_to_z()
    batch1.third.second_to_y()
    for l in range(LANES):
        for copy in halo2[l]:
            copy.wait_recv()
        unpack(dext, hr2, l)

    def mix_back(i, _):
        l, m = lax.div(i, 2), lax.rem(i, 2)
        mixed_back = correlate(dext, l, m, True)
        mixed[l, pl.ds(m * 8, 8)] = mixed_back[:8]
        mixed[l, pl.ds(16 + m * 4, 4)] = mixed_back[8:]
        return 0

    lax.fori_loop(0, 2, mix_back, 0)
    batch1.z_to_gather()
    batch2.third.second_to_y()
    few.to_x()
    lax.fori_loop(2, 4, mix_back, 0)
    batch2.z_to_gather()
    batch1.third.y_to_second()
    lax.fori_loop(4, 6, mix_back, 0)
    for l in range(LANES):
        lanes = slice(l * 128, (l + 1) * 128)
        mixed[l] = mixed[l] + d_block[:, lanes].reshape(24, 16, 128)
    direct = []
    for l in range(LANES):
        for m in range(2):
            lanes = slice(l * 128, (l + 1) * 128)
            at = (l * 2 + m) * 2
            direct.append(
                pltpu.make_async_copy(
                    mixed.at[l, m * 8 : m * 8 + 8], direct_out.at[m, 0:8, :, lanes], in_sems.at[at]
                )
            )
            direct.append(
                pltpu.make_async_copy(
                    mixed.at[l, 16 + m * 4 : 20 + m * 4], direct_out.at[m, 8:12, :, lanes], in_sems.at[at + 1]
                )
            )
    for copy in direct:
        copy.start()
    batch1.gather_to_second()
    few.to_y()
    batch2.third.y_to_second()
    batch2.gather_to_second()
    batch1.third.second_to_first()
    for each in (few, batch1, batch1.third, batch2, batch2.third):
        each.settle()
    batch1.second_to_first()
    few.to_z()
    batch2.third.second_to_first()
    batch2.second_to_first()
    batch1.third.first_to_core()
    batch1.first_to_core()
    few.to_gather()
    batch2.third.first_to_core()
    batch2.first_to_core()
    few.to_core()
    for copy in sum(halo1 + halo2, []) + far_copies + [near_copy] + relays:
        copy.wait_send()
    for copy in direct:
        copy.wait()
    few.finish()
    for batch in (batch1, batch2):
        batch.third.finish()
        batch.finish()


def finish(
    o1, t1, o2, t2, o3, direct, g_inputs, g_kernel, g_gain, g_expand, g_reduce, g_head, kernel, gain, expand, reduce, head, sems
):
    copies = []

    def write(src, dst):
        copy = pltpu.make_async_copy(src, dst, sems.at[len(copies)])
        copy.start()
        copies.append(copy)

    def few(index):
        return o3[index // 6, index % 6 * 16 : index % 6 * 16 + 16, :].astype(F32)

    write(direct, g_inputs)
    rows = [[few(r * 3 + l) for l in range(LANES)] for r in range(4)]
    weight = lax.broadcasted_iota(jnp.int32, (1, 128), 1)
    weight = jnp.where(weight < COUNT_BITS, lax.shift_left(1, jnp.minimum(weight, 15)), 0).astype(F32)
    total = jnp.sum(rows[0][0][15:16] * weight, axis=-1, keepdims=True) / 4
    scale = 1.0 / total

    def main(halves, third, flat, count):
        for at, part, row, take in places(flat, count):
            yield at, take, part_of(halves, third, part)[row : row + take, :].astype(F32) * scale

    for r in range(0, FFN, 512):
        for l in range(LANES):
            for at, take, part in main(o1, t1, l * FFN + r, 512):
                reduce[r + at : r + at + take, l * 128 : (l + 1) * 128] = part
        write(reduce.at[r : r + 512], g_reduce.at[r : r + 512])
    for r in range(0, D, 128):
        for l in range(FFN // 128):
            for at, take, part in main(o2, t2, l * D + r, 128):
                expand[r + at : r + at + take, l * 128 : (l + 1) * 128] = part
        write(expand.at[r : r + 128], g_expand.at[r : r + 128])
    for l in range(LANES):
        lanes = slice(l * 128, (l + 1) * 128)
        for i in range(7):
            at = (i % 2) * 8
            kernel[i, :, lanes] = rows[i // 2][l][at : at + 7] * scale
        gain[lanes] = (rows[0][l][7:8] * scale).reshape(128)
        for r in range(5):
            index = r * 3 + l
            part = o2[1, index * SHARD + MAIN : (index + 1) * SHARD, :].astype(F32) * scale
            count = min(16, head.shape[0] - r * 16)
            head[r * 16 : r * 16 + count, lanes] = part[:count]
    write(kernel, g_kernel)
    write(gain, g_gain)
    write(head, g_head)
    for copy in copies:
        copy.wait()


def on_device(sizes, inputs, target, land_sea, kernel, norm_gain, w_expand, w_reduce, head_weight):
    outputs = target.shape[0]
    by_cell = jnp.transpose(target, (1, 2, 0))
    head_rows = head_weight.T
    anywhere = pl.BlockSpec(memory_space=pl.ANY)
    in_hbm = pl.BlockSpec(memory_space=pltpu.HBM)
    vmem = pltpu.VMEM
    scratch = [
        vmem((24, 16, D), BF16),
        vmem((12, 16, outputs), F32),
        vmem((256, 128), F32),
        vmem((80, 256), F32),
        vmem((12, 16), jnp.int32),
        vmem((LANES, 7, 7, 128), F32),
        vmem((D,), F32),
        vmem((D, FFN), BF16),
        vmem((FFN, D), BF16),
        vmem((outputs, D), BF16),
        vmem((LANES, 2, 18, 32, 128), F32),
        vmem((LANES, 2, 18, 32, 128), F32),
        vmem((2, LANES, 80, 128), F32),
        vmem((2, LANES, 80, 128), BF16),
        vmem((2, LANES, 80, 128), BF16),
        vmem((2, LANES, 80, 128), BF16),
        vmem((2, LANES, 80, 128), BF16),
        vmem((LANES, 24, 16, 128), F32),
        vmem((D, D), F32),
        vmem((D, 128), F32),
        vmem((D, D), BF16),
        vmem((D, BLOCK), F32),
        vmem((D, FFN), F32),
        vmem((D, FFN), BF16),
        vmem((FFN, D), BF16),
        vmem((D, D), BF16),
        vmem((D, D), BF16),
        vmem((80, D), BF16),
        vmem((4, 80, D), F32),
        vmem((D, D), F32),
        vmem((D, D), BF16),
        vmem((D, FFN), BF16),
        vmem((D, D), F32),
        vmem((LANES, 64, 128), F32),
        pltpu.SemaphoreType.DMA((13,)),
        pltpu.SemaphoreType.DMA((12,)),
        pltpu.SemaphoreType.DMA((12,)),
        pltpu.SemaphoreType.DMA((5,)),
        pltpu.SemaphoreType.DMA((5,)),
    ]
    batch = reduce_scratch(sizes)
    batch = [*batch, *third_scratch(sizes)]
    scratch += batch + batch + few_scratch(sizes)
    operands = [inputs, by_cell, land_sea, kernel, norm_gain, w_expand, w_reduce, head_rows]
    operands = [pltpu.with_memory_space_constraint(operand, pltpu.HBM) for operand in operands]
    *reduced, direct = pl.pallas_call(
        lambda *refs: work(sizes, *refs),
        out_shape=(
            *(jax.ShapeDtypeStruct((2, rows, 128), BF16) for rows in (HALF, THIRD // 2, HALF, THIRD // 2, FEW)),
            jax.ShapeDtypeStruct(inputs.shape, F32),
        ),
        in_specs=[in_hbm] * 8,
        out_specs=(anywhere,) * 6,
        scratch_shapes=scratch,
        compiler_params=pltpu.CompilerParams(
            collective_id=0, has_side_effects=True, vmem_limit_bytes=48 * 1024 * 1024
        ),
        name="block_pass",
    )(*operands)
    in_vmem = pl.BlockSpec(memory_space=pltpu.VMEM)
    shapes = (kernel.shape, norm_gain.shape, w_expand.shape, w_reduce.shape, head_rows.shape)
    g_inputs, g_kernel, g_gain, g_expand, g_reduce, g_head = pl.pallas_call(
        finish,
        out_shape=tuple(jax.ShapeDtypeStruct(shape, F32) for shape in (inputs.shape, *shapes)),
        in_specs=[in_vmem] * 5 + [anywhere],
        out_specs=(anywhere,) * 6,
        scratch_shapes=[vmem(shape, F32) for shape in shapes] + [pltpu.SemaphoreType.DMA((11,))],
        compiler_params=pltpu.CompilerParams(vmem_limit_bytes=32 * 1024 * 1024),
        name="finish",
    )(*reduced, direct)
    return g_inputs, g_kernel, g_gain, g_expand, g_reduce, g_head.T


def solution(mesh):
    sizes = grid_of(mesh)
    return jax.shard_map(
        lambda *arrays: on_device(sizes, *arrays),
        mesh=mesh,
        in_specs=(
            P("ens", None, "tile", None),
            P(None, None, "tile"),
            P(None, "tile"),
            P(),
            P(),
            P(),
            P(),
            P(),
        ),
        out_specs=(P("ens", None, "tile", None), P(), P(), P(), P(), P()),
        check_vma=False,
    )
```

```python
import jax
import jax.numpy as jnp
from jax import lax
from jax.experimental import pallas as pl
from jax.experimental.pallas import tpu as pltpu
from jax.sharding import PartitionSpec as P

FAIR_WEIGHT = 0.95
SMOOTHING = 0.5
NORM_EPS = 1e-06
D = 384
FFN = 1536
LANES = 3
BLOCK = 512
BLOCKS = FFN // BLOCK
MEMBERS = 8
HALF = 2048
SHARD = 64
MAIN = 48
SLOTS = 48
THIRD = 1024
COUNT_BITS = 8
FEW = 128
F32 = jnp.float32
BF16 = jnp.bfloat16


def grid_of(mesh):
    tiles = mesh.shape["tile"]
    side = 4 if tiles == 64 else 2
    return side, side, tiles // (side * side)


def dot(a, b, dims):
    return lax.dot_general(a, b, (dims, ((), ())), preferred_element_type=F32)


NN = ((1,), (0,))
NT = ((1,), (1,))
TN = ((0,), (0,))


class Place:
    def __init__(self, sizes):
        self.nx, self.ny, self.nzh = sizes
        self.nz = 2 * self.nzh
        self.tiles = self.nx * self.ny * self.nzh
        self.ens = lax.axis_index("ens")
        self.tile = lax.axis_index("tile")
        self.core = lax.rem(self.ens, 2)
        self.zl = lax.div(self.ens, 2)
        self.zh = lax.rem(self.tile, self.nzh)
        self.x = lax.rem(lax.div(self.tile, self.nzh), self.nx)
        self.y = lax.div(self.tile, self.nzh * self.nx)
        self.z = self.zh * 2 + self.zl

    def at(self, x, y, z, core):
        return (lax.rem(z, 2) * 2 + core, (y * self.nx + x) * self.nzh + lax.div(z, 2))

    def along_x(self, d):
        return self.at(lax.rem(self.x + d, self.nx), self.y, self.z, self.core)

    def along_y(self, d):
        return self.at(self.x, lax.rem(self.y + d, self.ny), self.z, self.core)

    def along_z(self, d):
        return self.at(self.x, self.y, lax.rem(self.z + d, self.nz), self.core)

    def other_core(self):
        return self.at(self.x, self.y, self.z, 1 - self.core)

    def along_tile(self, d):
        return (self.ens, lax.rem(self.tile + d + self.tiles, self.tiles))

    def along_ens(self, d):
        return (lax.rem(self.ens + d, 4), self.tile)

    def everyone(self):
        peers = [self.along_tile(1), self.along_tile(-1)]
        peers += [self.along_ens(d) for d in range(1, 4)]
        peers += [self.along_x(d) for d in range(1, self.nx)]
        peers += [self.along_y(d) for d in range(1, self.ny)]
        peers += [self.along_z(d) for d in range(1, self.nz)]
        return peers


def remote(src, dst, send, recv, to):
    return pltpu.make_async_remote_copy(
        src_ref=src,
        dst_ref=dst,
        send_sem=send,
        recv_sem=recv,
        device_id=to,
        device_id_type=pl.DeviceIdType.MESH,
    )


def far_first(size):
    return sorted(range(1, size), key=lambda d: -min(d, size - d))


def summed(parts):
    value = None
    for part in parts:
        part = part.astype(F32)
        value = part if value is None else value + part
    return value.astype(BF16)


def from_row(start, count):
    return pl.ds(pl.multiple_of(start, 16), count)


class Group:
    def __init__(self, owner, whole, apart=False):
        self.owner, self.whole, self.apart = owner, whole, apart
        self.send, self.recv = owner.send.at[owner.slot()], owner.recv.at[owner.slot()]
        self.copies = []
        owner.groups.append(self)

    def start(self, src, dst, to):
        recv = self.owner.recv.at[self.owner.slot()] if self.apart else self.recv
        copy = remote(src, dst, self.send, recv, to)
        copy.start()
        self.copies.append(copy)
        self.to = to

    def all(self):
        return remote(self.whole, self.whole, self.send, self.recv, self.to)

    def received(self):
        self.all().wait_recv()

    def sent(self):
        self.all().wait_send()


class Copies:
    def __init__(self, send, recv):
        self.send, self.recv = send, recv
        self.slots = 0
        self.groups = []

    def slot(self):
        self.slots += 1
        return self.slots - 1

    def one(self, src, dst, to):
        group = Group(self, src)
        group.start(src, dst, to)
        return group

    def keep(self, src, dst):
        copy = pltpu.make_async_copy(src, dst, self.send.at[self.slot()])
        copy.start()
        return copy

    def settle(self):
        for group in self.groups:
            group.sent()
        self.groups = []


class Reduce(Copies):
    def __init__(self, place, refs, out, third):
        self.third = third
        self.p = place
        self.g, self.rc, self.s1, self.r1, self.s2, self.r2, self.sz, self.rz, self.oz, *sems = refs
        super().__init__(*sems)
        self.out = out
        self.n, self.nz = place.nx, place.nz
        self.c_rows = HALF // 2
        self.p_rows = self.c_rows // self.n
        self.q_rows = self.p_rows // self.n
        self.z_rows = 2 * self.q_rows // self.nz
        self.order, self.z_order = far_first(self.n), far_first(self.nz)
        self.core = [None, None]
        self.in_first = [None, None]
        self.in_second = [None, None]

    def first(self, h):
        return self.p.x if h == 0 else self.p.y

    def second(self, h):
        return self.p.y if h == 0 else self.p.x

    def to_first(self, h, d):
        return self.p.along_x(d) if h == 0 else self.p.along_y(d)

    def to_second(self, h, d):
        return self.p.along_y(d) if h == 0 else self.p.along_x(d)

    def start_core(self, halves=(0, 1)):
        other = from_row((1 - self.p.core) * self.c_rows, self.c_rows)
        for h in halves:
            self.core[h] = self.one(self.g.at[h, other], self.rc.at[h], self.p.other_core())

    def core_to_first(self, halves=(0, 1)):
        for h in halves:
            self.core[h].received()
            group = self.in_first[h] = Group(self, self.r1.at[h])
            for d in (*self.order, 0):
                at = lax.rem(self.first(h) + d, self.n) * self.p_rows
                piece = from_row(at, self.p_rows)
                mine = from_row(self.p.core * self.c_rows + at, self.p_rows)
                self.s1[h, piece, :] = summed([self.g[h, mine, :], self.rc[h, piece, :]])
                if d:
                    group.start(self.s1.at[h, piece], self.r1.at[h, d - 1], self.to_first(h, d))

    def first_to_second(self, halves=(0, 1)):
        for h in halves:
            self.in_first[h].received()
            mine = self.s1[h, from_row(self.first(h) * self.p_rows, self.p_rows), :]
            self.s2[h] = summed([mine, *(self.r1[h, d] for d in range(self.n - 1))])
            group = self.in_second[h] = Group(self, self.r2.at[h])
            for d in self.order:
                piece = from_row(lax.rem(self.second(h) + d, self.n) * self.q_rows, self.q_rows)
                group.start(self.s2.at[h, piece], self.r2.at[h, d - 1], self.to_second(h, d))

    def second_to_z(self):
        for h in range(2):
            self.in_second[h].received()
            mine = self.s2[h, from_row(self.second(h) * self.q_rows, self.q_rows), :]
            self.sz[h * self.q_rows : (h + 1) * self.q_rows, :] = summed(
                [mine, *(self.r2[h, d] for d in range(self.n - 1))]
            )
        self.in_z = Group(self, self.rz)
        for d in self.z_order:
            piece = from_row(lax.rem(self.p.z + d, self.nz) * self.z_rows, self.z_rows)
            self.in_z.start(self.sz.at[piece], self.rz.at[d - 1], self.p.along_z(d))

    def z_to_gather(self):
        self.in_z.received()
        mine = from_row(self.p.z * self.z_rows, self.z_rows)
        self.oz[mine, :] = summed([self.sz[mine, :], *(self.rz[d] for d in range(self.nz - 1))])
        self.out_z = Group(self, self.oz.at[pl.ds(0, (self.nz - 1) * self.z_rows)])
        for d in self.z_order:
            self.out_z.start(self.oz.at[mine], self.oz.at[mine], self.p.along_z(d))

    def shard(self, h):
        return self.p.core * self.c_rows + self.first(h) * self.p_rows + self.second(h) * self.q_rows

    def gather_to_second(self):
        self.out_z.received()
        self.out_second = []
        self.kept = []
        for h in range(2):
            at = from_row(self.shard(h), self.q_rows)
            mine = self.oz.at[pl.ds(h * self.q_rows, self.q_rows)]
            group = Group(self, self.out.at[h, pl.ds(0, (self.n - 1) * self.q_rows)])
            self.out_second.append(group)
            for d in self.order:
                group.start(mine, self.out.at[h, at], self.to_second(h, d))
            self.kept.append(self.keep(mine, self.out.at[h, at]))

    def piece(self, h, d):
        at = lax.rem(self.first(h) + d, self.n) * self.p_rows
        return self.out.at[h, from_row(self.p.core * self.c_rows + at, self.p_rows)]

    def second_to_first(self):
        self.out_first = []
        self.out_core = []
        for h in range(2):
            self.out_second[h].received()
            self.kept[h].wait()
            mine = self.piece(h, 0)
            group = Group(self, self.out.at[h, pl.ds(0, (self.n - 1) * self.p_rows)], apart=True)
            self.out_first.append(group)
            for d in self.order:
                group.start(mine, mine, self.to_first(h, d))
            group = Group(self, self.out.at[h, pl.ds(0, self.c_rows)])
            self.out_core.append(group)
            group.start(mine, mine, self.p.other_core())

    def first_to_core(self):
        for k, d in enumerate(self.order):
            for h in range(2):
                self.out_first[h].copies[k].wait_recv()
                came = self.piece(h, self.n - d)
                self.out_core[h].start(came, came, self.p.other_core())

    def finish(self):
        for group in self.out_core:
            group.received()
        self.settle()


class Few(Copies):
    def __init__(self, place, refs, out):
        self.p = p = place
        self.g, self.rc, self.s, self.rx, self.sy, self.sz, self.o, *sems = refs
        super().__init__(*sems)
        self.out = out
        self.x_rows = FEW // p.nx

    def piece(self, d):
        return from_row(lax.rem(self.p.x + d, self.p.nx) * self.x_rows, self.x_rows)

    def start(self):
        self.got = self.one(self.g.at[1 - self.p.core], self.rc, self.p.other_core())

    def to_x(self):
        p = self.p
        self.got.received()
        self.s[...] = summed([self.g[p.core], self.rc[...]])
        self.got = Group(self, self.rx)
        for d in far_first(p.nx):
            self.got.start(self.s.at[self.piece(d)], self.rx.at[d - 1], p.along_x(d))

    def to_y(self):
        p = self.p
        self.got.received()
        self.sy[p.y] = summed([self.s[self.piece(0), :], *(self.rx[d] for d in range(p.nx - 1))])
        self.got = Group(self, self.sy.at[pl.ds(0, p.ny - 1)])
        for d in far_first(p.ny):
            self.got.start(self.sy.at[p.y], self.sy.at[p.y], p.along_y(d))

    def to_z(self):
        p = self.p
        self.got.received()
        self.sz[p.z] = summed(self.sy[k] for k in range(p.ny))
        self.got = Group(self, self.sz.at[pl.ds(0, p.nz - 1)])
        for d in far_first(p.nz):
            self.got.start(self.sz.at[p.z], self.sz.at[p.z], p.along_z(d))

    def to_gather(self):
        p = self.p
        self.got.received()
        self.o[...] = summed(self.sz[k] for k in range(p.nz))
        mine = self.out.at[p.core, self.piece(0)]
        self.kept = self.keep(self.o, mine)
        self.got = Group(self, self.out.at[0, pl.ds(0, (p.nx - 1) * self.x_rows)])
        for d in far_first(p.nx):
            self.got.start(self.o, mine, p.along_x(d))
        self.last = Group(self, self.out.at[0])
        self.last.start(self.o, mine, p.other_core())

    def to_core(self):
        p = self.p
        self.got.received()
        for d in range(1, p.nx):
            came = self.out.at[p.core, self.piece(d)]
            self.last.start(came, came, p.other_core())

    def finish(self):
        self.last.received()
        self.kept.wait()
        self.settle()


class Third(Copies):
    def __init__(self, place, refs, out):
        self.p = p = place
        self.g, self.rc, self.s1, self.r1, self.s2, self.r2, self.sy, self.o, *sems = refs
        super().__init__(*sems)
        self.out = out
        self.z_rows = THIRD // 2 // p.nz
        self.x_rows = self.z_rows // p.nx
        self.order = far_first(p.nz)

    def piece(self, d):
        return from_row(lax.rem(self.p.z + d, self.p.nz) * self.z_rows, self.z_rows)

    def start_core(self):
        self.got = self.one(self.g.at[1 - self.p.core], self.rc, self.p.other_core())

    def core_to_first(self):
        p = self.p
        self.got.received()
        self.s1[...] = summed([self.g[p.core], self.rc[...]])
        self.got = Group(self, self.r1)
        for d in self.order:
            self.got.start(self.s1.at[self.piece(d)], self.r1.at[d - 1], p.along_z(d))

    def first_to_second(self):
        p = self.p
        self.got.received()
        self.s2[...] = summed([self.s1[self.piece(0), :], *(self.r1[k] for k in range(p.nz - 1))])
        self.got = Group(self, self.r2)
        for d in far_first(p.nx):
            piece = from_row(lax.rem(p.x + d, p.nx) * self.x_rows, self.x_rows)
            self.got.start(self.s2.at[piece], self.r2.at[d - 1], p.along_x(d))

    def second_to_y(self):
        p = self.p
        self.got.received()
        mine = self.s2[from_row(p.x * self.x_rows, self.x_rows), :]
        self.sy[p.y] = summed([mine, *(self.r2[d] for d in range(p.nx - 1))])
        self.got = Group(self, self.sy.at[pl.ds(0, p.ny - 1)])
        for d in far_first(p.ny):
            self.got.start(self.sy.at[p.y], self.sy.at[p.y], p.along_y(d))

    def y_to_second(self):
        p = self.p
        self.got.received()
        self.o[...] = summed(self.sy[k] for k in range(p.ny))
        mine = self.out.at[p.core, from_row(p.z * self.z_rows + p.x * self.x_rows, self.x_rows)]
        self.kept = self.keep(self.o, mine)
        self.got = Group(self, self.out.at[0, pl.ds(0, (p.nx - 1) * self.x_rows)])
        for d in far_first(p.nx):
            self.got.start(self.o, mine, p.along_x(d))

    def second_to_first(self):
        p = self.p
        self.got.received()
        self.kept.wait()
        mine = self.out.at[p.core, self.piece(0)]
        self.got = Group(self, self.out.at[0, pl.ds(0, (p.nz - 1) * self.z_rows)])
        for d in self.order:
            self.got.start(mine, mine, p.along_z(d))

    def first_to_core(self):
        p = self.p
        self.got.received()
        self.last = self.one(self.out.at[p.core], self.out.at[p.core], p.other_core())

    def finish(self):
        self.last.received()
        self.settle()


def third_scratch(sizes):
    nx, ny, nzh = sizes
    nz = 2 * nzh
    z_rows = THIRD // 2 // nz
    x_rows = z_rows // nx
    shapes = [
        (2, THIRD // 2, 128), (THIRD // 2, 128), (THIRD // 2, 128), (nz - 1, z_rows, 128), (z_rows, 128),
        (nx - 1, x_rows, 128), (ny, x_rows, 128), (x_rows, 128),
    ]
    return [pltpu.VMEM(shape, BF16) for shape in shapes] + [pltpu.SemaphoreType.DMA((SLOTS,))] * 2


def few_scratch(sizes):
    nx, ny, nzh = sizes
    x_rows = FEW // nx
    shapes = [
        (2, FEW, 128), (FEW, 128), (FEW, 128), (nx - 1, x_rows, 128), (ny, x_rows, 128), (2 * nzh, x_rows, 128),
        (x_rows, 128),
    ]
    return [pltpu.VMEM(shape, BF16) for shape in shapes] + [pltpu.SemaphoreType.DMA((SLOTS,))] * 2


def reduce_scratch(sizes):
    n, _, nzh = sizes
    nz = 2 * nzh
    c_rows = HALF // 2
    p_rows = c_rows // n
    q_rows = p_rows // n
    z_rows = 2 * q_rows // nz
    shapes = [
        (2, HALF, 128), (2, c_rows, 128), (2, c_rows, 128), (2, n - 1, p_rows, 128), (2, p_rows, 128),
        (2, n - 1, q_rows, 128), (2 * q_rows, 128), (nz - 1, z_rows, 128), (2 * q_rows, 128),
    ]
    return [pltpu.VMEM(shape, BF16) for shape in shapes] + [pltpu.SemaphoreType.DMA((SLOTS,))] * 2


def slope_of(offset):
    return offset * lax.rsqrt(offset * offset + SMOOTHING * SMOOTHING)


def places(flat, count):
    at = 0
    while at < count:
        here = flat + at
        if here < HALF:
            take, part, row = HALF - here, 0, here
        elif here < HALF + 32 * MAIN:
            shard, inner = divmod(here - HALF, MAIN)
            take, part, row = MAIN - inner, 1, shard * SHARD + inner
        else:
            row = here - HALF - 32 * MAIN
            part, row = 2 + row // (THIRD // 2), row % (THIRD // 2)
            take = THIRD // 2 - row
        take = min(take, count - at)
        yield at, part, row, take
        at += take


def part_of(halves, third, part):
    return halves.at[part] if part < 2 else third.at[part - 2]


def put_main(batch, flat, value):
    for at, part, row, take in places(flat, value.shape[0]):
        part_of(batch.g, batch.third.g, part)[row : row + take, :] = value[at : at + take].astype(BF16)


def put_small(batch, index, value):
    batch[1, index * SHARD + MAIN : (index + 1) * SHARD, :] = value.astype(BF16)


def put_few(batch, index, value):
    batch[index // 6, index % 6 * 16 : index % 6 * 16 + 16, :] = value.astype(BF16)


def work(sizes, *refs):
    (
        x_hbm, target_hbm, sea_hbm, kernel_hbm, gain_hbm, expand_hbm, reduce_hbm, head_hbm,
        out1, third1, out2, third2, out3, direct_out,
        xb, target, tall, tg, sea, taps, gain, we, wr, head,
        ext, dext, rim, hs, hr, hs2, hr2, mixed, standard, recip, normed, before, slope, hidden, hidden_t, normed_t,
        block, head_t, fall, d_block, d_block_b, d_before, d_norm, gk,
        in_sems, halo_send, halo_recv, ens_send, ens_recv,
        *rest,
    ) = refs
    place = Place(sizes)
    few = Few(place, rest[-9:], out3)
    pieces = (len(rest) - 9) // 2
    batch1, batch2 = (
        Reduce(place, mine[:-10], out, Third(place, mine[-10:], third))
        for mine, out, third in ((rest[:pieces], out1, third1), (rest[pieces : 2 * pieces], out2, third2))
    )

    loads = [
        pltpu.make_async_copy(x_hbm.at[0, 0:8], xb.at[0:8], in_sems.at[0]),
        pltpu.make_async_copy(x_hbm.at[1, 0:8], xb.at[8:16], in_sems.at[1]),
        pltpu.make_async_copy(x_hbm.at[0, 8:12], xb.at[16:20], in_sems.at[2]),
        pltpu.make_async_copy(x_hbm.at[1, 8:12], xb.at[20:24], in_sems.at[3]),
    ]
    tap_loads = [
        pltpu.make_async_copy(kernel_hbm.at[:, :, l * 128 : (l + 1) * 128], taps.at[l], in_sems.at[4 + l])
        for l in range(LANES)
    ]
    later = [
        pltpu.make_async_copy(gain_hbm, gain, in_sems.at[7]),
        pltpu.make_async_copy(head_hbm, head, in_sems.at[8]),
        pltpu.make_async_copy(expand_hbm, we, in_sems.at[9]),
        pltpu.make_async_copy(reduce_hbm, wr, in_sems.at[10]),
        pltpu.make_async_copy(target_hbm, target, in_sems.at[11]),
        pltpu.make_async_copy(sea_hbm, sea, in_sems.at[12]),
    ]
    for copy in loads + tap_loads + later:
        copy.start()

    barrier = pltpu.get_barrier_semaphore()
    peers = place.everyone()
    for peer in peers:
        pl.semaphore_signal(barrier, inc=1, device_id=peer, device_id_type=pl.DeviceIdType.MESH)

    def clear(i, _):
        l, m = lax.div(i, 2), lax.rem(i, 2)
        ext[l, m, 0:3] = jnp.zeros((3, 32, 128), F32)
        ext[l, m, 15:18] = jnp.zeros((3, 32, 128), F32)
        ext[l, m, 3:15, 0:8] = jnp.zeros((12, 8, 128), F32)
        ext[l, m, 3:15, 24:32] = jnp.zeros((12, 8, 128), F32)
        return 0

    lax.fori_loop(0, 2 * LANES, clear, 0)
    rim[...] = jnp.zeros_like(rim)
    for copy in loads:
        copy.wait()
    for l in range(LANES):
        lanes = slice(l * 128, (l + 1) * 128)
        for m in range(2):
            ext[l, m, 3:11, 8:24, :] = xb[m * 8 : m * 8 + 8, :, lanes].astype(F32)
            ext[l, m, 11:15, 8:24, :] = xb[16 + m * 4 : 20 + m * 4, :, lanes].astype(F32)

    def rim_rows(m, j):
        return slice((m * 3 + j) * 12, (m * 3 + j) * 12 + 12)

    def pack(field, out):
        for side, col in ((0, 8), (1, 21)):
            for m in range(2):
                for j in range(3):
                    for l in range(LANES):
                        rim[side, l, rim_rows(m, j)] = field[l, m, 3:15, col + j, :]
        out[...] = rim[...].astype(BF16)

    def unpack(field, got, l):
        for side, col in ((0, 5), (1, 24)):
            rim[side, l] = got[side, l].astype(F32)
            for m in range(2):
                for j in range(3):
                    field[l, m, 3:15, col + j, :] = rim[side, l, rim_rows(m, j)]

    def halo(out, got, at):
        copies = [
            [
                remote(out.at[side, l], got.at[1 - side, l], halo_send.at[at + s], halo_recv.at[at + s], place.along_tile(to))
                for s, (side, to) in enumerate(((0, -1), (1, 1)), 2 * l)
            ]
            for l in range(LANES)
        ]
        for pair in copies:
            for copy in pair:
                copy.start()
        return copies

    pack(ext, hs)
    pl.semaphore_wait(barrier, len(peers))
    halo1 = halo(hs, hr, 0)

    for copy in tap_loads:
        copy.wait()
    def correlate(field, l, m, flip):
        total = jnp.zeros((12, 16, 128), F32)
        for j in range(7):
            shifted = field[l, m, :, 5 + j : 21 + j, :]
            for i in range(7):
                tap = taps[l, 6 - i, 6 - j : 7 - j, :] if flip else taps[l, i, j : j + 1, :]
                total = total + shifted[i : i + 12] * tap
        return total

    def mix(i, _):
        l, m = lax.div(i, 2), lax.rem(i, 2)
        total = correlate(ext, l, m, False)
        mixed[l, pl.ds(m * 8, 8)] = total[:8]
        mixed[l, pl.ds(16 + m * 4, 4)] = total[8:]
        return 0

    lax.fori_loop(0, 2 * LANES, mix, 0)
    sublane = lax.broadcasted_iota(jnp.int32, (18, 8, 128), 1)

    def edges(l, m):
        for first, taps_in in ((0, (0, 1, 2)), (8, (4, 5, 6))):
            total = jnp.zeros((12, 8, 128), F32)
            for j in taps_in:
                outside = sublane < 3 - j if first == 0 else sublane >= 11 - j
                shifted = jnp.where(outside, ext[l, m, :, 5 + first + j : 13 + first + j, :], 0.0)
                for i in range(7):
                    total = total + shifted[i : i + 12] * taps[l, i, j : j + 1, :]
            mixed[l, pl.ds(m * 8, 8), first : first + 8] += total[:8]
            mixed[l, pl.ds(16 + m * 4, 4), first : first + 8] += total[8:]

    for l in range(LANES):
        for copy in halo1[l]:
            copy.wait_recv()
        unpack(ext, hr, l)
        lax.fori_loop(0, 2, lambda m, _, l=l: (edges(l, m), 0)[1], 0)

    for copy in later:
        copy.wait()
    outputs = head.shape[0]
    head_t[...] = jnp.concatenate([head[...].astype(F32), jnp.zeros((80 - outputs, D), F32)], axis=0).astype(BF16)
    gain_row = gain[...].reshape(1, D)

    def norm(i, _):
        rows = pl.ds(pl.multiple_of(i * 64, 64), 64)
        parts = [mixed[l, pl.ds(i * 4, 4)].reshape(64, 128) for l in range(LANES)]
        mean = jnp.sum(parts[0] + parts[1] + parts[2], axis=-1, keepdims=True) / D
        centre = [part - mean for part in parts]
        square = centre[0] * centre[0] + centre[1] * centre[1] + centre[2] * centre[2]
        scale = lax.rsqrt(jnp.sum(square, axis=-1, keepdims=True) / D + NORM_EPS)
        recip[rows, :] = jnp.broadcast_to(scale, (64, 128))
        for l in range(LANES):
            lanes = slice(l * 128, (l + 1) * 128)
            value = centre[l] * scale
            standard[rows, lanes] = value
            normed[rows, lanes] = (value * gain_row[:, lanes]).astype(BF16)
        return 0

    lax.fori_loop(0, 6, norm, 0, unroll=True)

    total = xb[...].reshape(D, D).astype(F32)
    for b in range(BLOCKS):
        columns = slice(b * BLOCK, (b + 1) * BLOCK)
        before[b] = dot(normed[...], we[:, columns], NN)

        def gelu(i, _, b=b, columns=columns):
            rows = pl.ds(pl.multiple_of(i * 32, 32), 32)
            v = before[b, rows, :]
            square = v * v
            scale = 0.7978845608028654
            t = jnp.tanh(v * (scale + (scale * 0.044715) * square))
            half = 0.5 + 0.5 * t
            hidden[rows, columns] = (v * half).astype(BF16)
            slope[rows, columns] = half + (0.5 * v) * (1.0 - t * t) * (scale + (scale * 3 * 0.044715) * square)
            return 0

        lax.fori_loop(0, 12, gelu, 0, unroll=True)
        total = total + dot(hidden[:, columns], wr[columns, :], NN)
    block[...] = total.astype(BF16)

    own = dot(head_t[...], block[...], NT)
    fall[0] = own
    far = place.along_ens(2)
    far_copies = [
        remote(fall.at[0, pl.ds(r, 40)], fall.at[2, pl.ds(r, 40)], ens_send.at[k], ens_recv.at[k], far)
        for k, r in enumerate((0, 40))
    ]
    near_copy = remote(fall.at[0], fall.at[1], ens_send.at[2], ens_recv.at[2], place.other_core())
    relays = [
        remote(fall.at[2, pl.ds(r, 40)], fall.at[3, pl.ds(r, 40)], ens_send.at[3 + k], ens_recv.at[3 + k], place.other_core())
        for k, r in enumerate((0, 40))
    ]
    for copy in [*far_copies, near_copy]:
        copy.start()
    for index in range(32):
        put_small(batch1.g, index, jnp.zeros((16, 128), F32))
        if index >= 15:
            put_small(batch2.g, index, jnp.zeros((16, 128), F32))
    gk[...] = jnp.zeros_like(gk)
    few.g[...] = jnp.zeros_like(few.g)

    def clear_back(i, _):
        l, m = lax.div(i, 2), lax.rem(i, 2)
        dext[l, m, 0:3] = jnp.zeros((3, 32, 128), F32)
        dext[l, m, 15:18] = jnp.zeros((3, 32, 128), F32)
        return 0

    lax.fori_loop(0, 2 * LANES, clear_back, 0)
    diagonal = lax.broadcasted_iota(jnp.int32, (16, 16), 0) == lax.broadcasted_iota(jnp.int32, (16, 16), 1)
    tall[...] = jnp.zeros_like(tall)
    for a in range(12):
        water = jnp.broadcast_to(sea[a : a + 1, :].astype(F32), (16, 16))
        water = jnp.sum(jnp.where(diagonal, water, 0.0), axis=1, keepdims=True)
        for at in (a * 16,) if a < 8 else (a * 16, a * 16 + 64):
            tall[at : at + 16, 0:outputs] = target[a]
            tall[at : at + 16, outputs : outputs + 1] = water
    tg[...] = tall[...].T[0:80]
    normed_t[...] = normed[...].T
    for b in range(BLOCKS):
        hidden_t[b * BLOCK : (b + 1) * BLOCK, :] = hidden[:, b * BLOCK : (b + 1) * BLOCK].T
    for came, relay in zip(far_copies, relays):
        came.wait_recv()
        relay.start()
    near_copy.wait_recv()

    spread = jnp.zeros((80, D), F32)
    for s in range(4):
        if s == 3:
            for copy in relays:
                copy.wait_recv()
        theirs = fall[s]
        swapped = jnp.concatenate(
            [theirs[:, 128:256], theirs[:, 0:128], pltpu.roll(theirs[:, 256:384], 64, 1)], axis=1
        )
        spread = spread + slope_of(own - theirs) + slope_of(own - swapped)
    observed = jnp.concatenate([tg[:, 0:128], tg[:, 0:128], tg[:, 128:256]], axis=1)
    ocean = observed[outputs : outputs + 1]
    slopes = slope_of(own - observed) / MEMBERS - FAIR_WEIGHT / (MEMBERS * (MEMBERS - 1)) * spread
    slopes_b = (slopes * ocean).astype(BF16)

    back = dot(slopes_b, head_t[...], TN)
    d_block[...] = back
    d_block_b[...] = back.astype(BF16)
    grad_reduce = dot(hidden_t[...], d_block_b[...], NN)
    for l in range(LANES):
        put_main(batch1, l * FFN, grad_reduce[:, l * 128 : (l + 1) * 128])
    batch1.start_core()
    batch1.third.start_core()

    grad_head = dot(slopes_b, block[...], NN)
    for r in range(5):
        for l in range(LANES):
            put_small(batch2.g, r * 3 + l, grad_head[r * 16 : r * 16 + 16, l * 128 : (l + 1) * 128])

    for b in range(BLOCKS):
        columns = slice(b * BLOCK, (b + 1) * BLOCK)
        before[b] = dot(d_block_b[...], wr[columns, :], NT)

        def gate(i, _, b=b, columns=columns):
            rows = pl.ds(pl.multiple_of(i * 32, 32), 32)
            d_before[rows, columns] = (before[b, rows, :] * slope[rows, columns]).astype(BF16)
            return 0

        lax.fori_loop(0, 12, gate, 0, unroll=True)
        grad_expand = dot(normed_t[...], d_before[:, columns], NN)
        for l in range(BLOCK // 128):
            put_main(batch2, (b * (BLOCK // 128) + l) * D, grad_expand[:, l * 128 : (l + 1) * 128])
        if b == 1:
            batch2.start_core((0,))
            batch1.core_to_first()
            batch1.third.core_to_first()
    batch2.start_core((1,))
    batch2.third.start_core()
    batch2.core_to_first((0,))
    d_norm[...] = dot(d_before[...], we[...], NT)
    batch2.core_to_first((1,))
    batch2.third.core_to_first()

    gk[0, 7:8, :] = jnp.zeros((1, 128), F32)

    def unnorm(i, _):
        rows = pl.ds(pl.multiple_of(i * 64, 64), 64)
        value = [d_norm[rows, l * 128 : (l + 1) * 128] for l in range(LANES)]
        std = [standard[rows, l * 128 : (l + 1) * 128] for l in range(LANES)]
        for l in range(LANES):
            gk[l, 7:8, :] += jnp.sum(value[l] * std[l], axis=0, keepdims=True)
        scaled = [value[l] * gain_row[:, l * 128 : (l + 1) * 128] for l in range(LANES)]
        mean = jnp.sum(scaled[0] + scaled[1] + scaled[2], axis=-1, keepdims=True) / D
        along = jnp.sum(scaled[0] * std[0] + scaled[1] * std[1] + scaled[2] * std[2], axis=-1, keepdims=True) / D
        for l in range(LANES):
            mixed[l, pl.ds(i * 4, 4)] = (recip[rows, :] * (scaled[l] - mean - std[l] * along)).reshape(4, 16, 128)
        return 0

    lax.fori_loop(0, 6, unnorm, 0, unroll=True)
    for l in range(LANES):
        for m in range(2):
            dext[l, m, 3:11, 8:24, :] = mixed[l, m * 8 : m * 8 + 8]
            dext[l, m, 11:15, 8:24, :] = mixed[l, 16 + m * 4 : 20 + m * 4]
    pack(dext, hs2)
    halo2 = halo(hs2, hr2, 6)

    def kernel_grad(l, _):
        for j in range(7):
            near = [ext[l, m, :, 5 + j : 21 + j, :] for m in range(2)]
            for i in range(7):
                part = jnp.zeros((16, 128), F32)
                for m in range(2):
                    part = part + jnp.sum(dext[l, m, 3:15, 8:24, :] * near[m][i : i + 12], axis=0)
                gk[l, i * 8 + j : i * 8 + j + 1, :] = jnp.sum(part, axis=0, keepdims=True)
        return 0

    batch1.first_to_second()
    batch2.first_to_second((0,))
    lax.fori_loop(0, 1, kernel_grad, 0)
    batch1.third.first_to_second()
    batch2.first_to_second((1,))
    batch1.second_to_z()
    lax.fori_loop(1, 2, kernel_grad, 0)
    batch2.third.first_to_second()
    lax.fori_loop(2, 3, kernel_grad, 0)
    count = jnp.sum(sea[...].astype(F32)).astype(jnp.int32)
    lane = lax.broadcasted_iota(jnp.int32, (1, 128), 1)
    bits = lax.bitwise_and(lax.shift_right_logical(jnp.broadcast_to(count, (1, 128)), jnp.minimum(lane, 31)), 1)
    gk[0, 15:16, :] = jnp.where(lane < COUNT_BITS, bits, 0).astype(F32)
    for r in range(4):
        for l in range(LANES):
            put_few(few.g, r * 3 + l, gk[l, r * 16 : r * 16 + 16, :])
    few.start()
    batch2.second_to_z()
    batch1.third.second_to_y()
    for l in range(LANES):
        for copy in halo2[l]:
            copy.wait_recv()
        unpack(dext, hr2, l)

    def mix_back(i, _):
        l, m = lax.div(i, 2), lax.rem(i, 2)
        mixed_back = correlate(dext, l, m, True)
        mixed[l, pl.ds(m * 8, 8)] = mixed_back[:8]
        mixed[l, pl.ds(16 + m * 4, 4)] = mixed_back[8:]
        return 0

    lax.fori_loop(0, 2, mix_back, 0)
    batch1.z_to_gather()
    batch2.third.second_to_y()
    few.to_x()
    lax.fori_loop(2, 4, mix_back, 0)
    batch2.z_to_gather()
    batch1.third.y_to_second()
    lax.fori_loop(4, 6, mix_back, 0)
    for l in range(LANES):
        lanes = slice(l * 128, (l + 1) * 128)
        mixed[l] = mixed[l] + d_block[:, lanes].reshape(24, 16, 128)
    direct = []
    for l in range(LANES):
        for m in range(2):
            lanes = slice(l * 128, (l + 1) * 128)
            at = (l * 2 + m) * 2
            direct.append(
                pltpu.make_async_copy(
                    mixed.at[l, m * 8 : m * 8 + 8], direct_out.at[m, 0:8, :, lanes], in_sems.at[at]
                )
            )
            direct.append(
                pltpu.make_async_copy(
                    mixed.at[l, 16 + m * 4 : 20 + m * 4], direct_out.at[m, 8:12, :, lanes], in_sems.at[at + 1]
                )
            )
    for copy in direct:
        copy.start()
    batch1.gather_to_second()
    few.to_y()
    batch2.third.y_to_second()
    batch2.gather_to_second()
    batch1.third.second_to_first()
    for each in (few, batch1, batch1.third, batch2, batch2.third):
        each.settle()
    batch1.second_to_first()
    few.to_z()
    batch2.third.second_to_first()
    batch2.second_to_first()
    batch1.third.first_to_core()
    batch1.first_to_core()
    few.to_gather()
    batch2.third.first_to_core()
    batch2.first_to_core()
    few.to_core()
    for copy in sum(halo1 + halo2, []) + far_copies + [near_copy] + relays:
        copy.wait_send()
    for copy in direct:
        copy.wait()
    few.finish()
    for batch in (batch1, batch2):
        batch.third.finish()
        batch.finish()


def finish(
    o1, t1, o2, t2, o3, direct, g_inputs, g_kernel, g_gain, g_expand, g_reduce, g_head, kernel, gain, expand, reduce, head, sems
):
    copies = []

    def write(src, dst):
        copy = pltpu.make_async_copy(src, dst, sems.at[len(copies)])
        copy.start()
        copies.append(copy)

    def few(index):
        return o3[index // 6, index % 6 * 16 : index % 6 * 16 + 16, :].astype(F32)

    write(direct, g_inputs)
    rows = [[few(r * 3 + l) for l in range(LANES)] for r in range(4)]
    weight = lax.broadcasted_iota(jnp.int32, (1, 128), 1)
    weight = jnp.where(weight < COUNT_BITS, lax.shift_left(1, jnp.minimum(weight, 15)), 0).astype(F32)
    total = jnp.sum(rows[0][0][15:16] * weight, axis=-1, keepdims=True) / 4
    scale = 1.0 / total

    def main(halves, third, flat, count):
        for at, part, row, take in places(flat, count):
            yield at, take, part_of(halves, third, part)[row : row + take, :].astype(F32) * scale

    for r in range(0, FFN, 512):
        for l in range(LANES):
            for at, take, part in main(o1, t1, l * FFN + r, 512):
                reduce[r + at : r + at + take, l * 128 : (l + 1) * 128] = part
        write(reduce.at[r : r + 512], g_reduce.at[r : r + 512])
    for r in range(0, D, 128):
        for l in range(FFN // 128):
            for at, take, part in main(o2, t2, l * D + r, 128):
                expand[r + at : r + at + take, l * 128 : (l + 1) * 128] = part
        write(expand.at[r : r + 128], g_expand.at[r : r + 128])
    for l in range(LANES):
        lanes = slice(l * 128, (l + 1) * 128)
        for i in range(7):
            at = (i % 2) * 8
            kernel[i, :, lanes] = rows[i // 2][l][at : at + 7] * scale
        gain[lanes] = (rows[0][l][7:8] * scale).reshape(128)
        for r in range(5):
            index = r * 3 + l
            part = o2[1, index * SHARD + MAIN : (index + 1) * SHARD, :].astype(F32) * scale
            count = min(16, head.shape[0] - r * 16)
            head[r * 16 : r * 16 + count, lanes] = part[:count]
    write(kernel, g_kernel)
    write(gain, g_gain)
    write(head, g_head)
    for copy in copies:
        copy.wait()


def on_device(sizes, inputs, target, land_sea, kernel, norm_gain, w_expand, w_reduce, head_weight):
    outputs = target.shape[0]
    by_cell = jnp.transpose(target, (1, 2, 0))
    head_rows = head_weight.T
    anywhere = pl.BlockSpec(memory_space=pl.ANY)
    in_hbm = pl.BlockSpec(memory_space=pltpu.HBM)
    vmem = pltpu.VMEM
    scratch = [
        vmem((24, 16, D), BF16),
        vmem((12, 16, outputs), F32),
        vmem((256, 128), F32),
        vmem((80, 256), F32),
        vmem((12, 16), jnp.int32),
        vmem((LANES, 7, 7, 128), F32),
        vmem((D,), F32),
        vmem((D, FFN), BF16),
        vmem((FFN, D), BF16),
        vmem((outputs, D), BF16),
        vmem((LANES, 2, 18, 32, 128), F32),
        vmem((LANES, 2, 18, 32, 128), F32),
        vmem((2, LANES, 80, 128), F32),
        vmem((2, LANES, 80, 128), BF16),
        vmem((2, LANES, 80, 128), BF16),
        vmem((2, LANES, 80, 128), BF16),
        vmem((2, LANES, 80, 128), BF16),
        vmem((LANES, 24, 16, 128), F32),
        vmem((D, D), F32),
        vmem((D, 128), F32),
        vmem((D, D), BF16),
        vmem((BLOCKS, D, BLOCK), F32),
        vmem((D, FFN), F32),
        vmem((D, FFN), BF16),
        vmem((FFN, D), BF16),
        vmem((D, D), BF16),
        vmem((D, D), BF16),
        vmem((80, D), BF16),
        vmem((4, 80, D), F32),
        vmem((D, D), F32),
        vmem((D, D), BF16),
        vmem((D, FFN), BF16),
        vmem((D, D), F32),
        vmem((LANES, 64, 128), F32),
        pltpu.SemaphoreType.DMA((13,)),
        pltpu.SemaphoreType.DMA((12,)),
        pltpu.SemaphoreType.DMA((12,)),
        pltpu.SemaphoreType.DMA((5,)),
        pltpu.SemaphoreType.DMA((5,)),
    ]
    batch = reduce_scratch(sizes)
    batch = [*batch, *third_scratch(sizes)]
    scratch += batch + batch + few_scratch(sizes)
    operands = [inputs, by_cell, land_sea, kernel, norm_gain, w_expand, w_reduce, head_rows]
    operands = [pltpu.with_memory_space_constraint(operand, pltpu.HBM) for operand in operands]
    *reduced, direct = pl.pallas_call(
        lambda *refs: work(sizes, *refs),
        out_shape=(
            *(jax.ShapeDtypeStruct((2, rows, 128), BF16) for rows in (HALF, THIRD // 2, HALF, THIRD // 2, FEW)),
            jax.ShapeDtypeStruct(inputs.shape, F32),
        ),
        in_specs=[in_hbm] * 8,
        out_specs=(anywhere,) * 6,
        scratch_shapes=scratch,
        compiler_params=pltpu.CompilerParams(
            collective_id=0, has_side_effects=True, vmem_limit_bytes=48 * 1024 * 1024
        ),
        name="block_pass",
    )(*operands)
    in_vmem = pl.BlockSpec(memory_space=pltpu.VMEM)
    shapes = (kernel.shape, norm_gain.shape, w_expand.shape, w_reduce.shape, head_rows.shape)
    g_inputs, g_kernel, g_gain, g_expand, g_reduce, g_head = pl.pallas_call(
        finish,
        out_shape=tuple(jax.ShapeDtypeStruct(shape, F32) for shape in (inputs.shape, *shapes)),
        in_specs=[in_vmem] * 5 + [anywhere],
        out_specs=(anywhere,) * 6,
        scratch_shapes=[vmem(shape, F32) for shape in shapes] + [pltpu.SemaphoreType.DMA((11,))],
        compiler_params=pltpu.CompilerParams(vmem_limit_bytes=32 * 1024 * 1024),
        name="finish",
    )(*reduced, direct)
    return g_inputs, g_kernel, g_gain, g_expand, g_reduce, g_head.T


def solution(mesh):
    sizes = grid_of(mesh)
    return jax.shard_map(
        lambda *arrays: on_device(sizes, *arrays),
        mesh=mesh,
        in_specs=(
            P("ens", None, "tile", None),
            P(None, None, "tile"),
            P(None, "tile"),
            P(),
            P(),
            P(),
            P(),
            P(),
        ),
        out_specs=(P("ens", None, "tile", None), P(), P(), P(), P(), P()),
        check_vma=False,
    )
```

```python
import jax
import jax.numpy as jnp
from jax import lax
from jax.experimental import pallas as pl
from jax.experimental.pallas import tpu as pltpu
from jax.sharding import PartitionSpec as P

FAIR_WEIGHT = 0.95
SMOOTHING = 0.5
NORM_EPS = 1e-06
D = 384
FFN = 1536
LANES = 3
BLOCK = 512
BLOCKS = FFN // BLOCK
MEMBERS = 8
HALF = 2048
SHARD = 64
MAIN = 48
SLOTS = 48
THIRD = 1024
COUNT_BITS = 8
FEW = 128
F32 = jnp.float32
BF16 = jnp.bfloat16


def grid_of(mesh):
    tiles = mesh.shape["tile"]
    side = 4 if tiles == 64 else 2
    return side, side, tiles // (side * side)


def dot(a, b, dims):
    return lax.dot_general(a, b, (dims, ((), ())), preferred_element_type=F32)


NN = ((1,), (0,))
NT = ((1,), (1,))
TN = ((0,), (0,))


class Place:
    def __init__(self, sizes):
        self.nx, self.ny, self.nzh = sizes
        self.nz = 2 * self.nzh
        self.tiles = self.nx * self.ny * self.nzh
        self.ens = lax.axis_index("ens")
        self.tile = lax.axis_index("tile")
        self.core = lax.rem(self.ens, 2)
        self.zl = lax.div(self.ens, 2)
        self.zh = lax.rem(self.tile, self.nzh)
        self.x = lax.rem(lax.div(self.tile, self.nzh), self.nx)
        self.y = lax.div(self.tile, self.nzh * self.nx)
        self.z = self.zh * 2 + self.zl

    def at(self, x, y, z, core):
        return (lax.rem(z, 2) * 2 + core, (y * self.nx + x) * self.nzh + lax.div(z, 2))

    def along_x(self, d):
        return self.at(lax.rem(self.x + d, self.nx), self.y, self.z, self.core)

    def along_y(self, d):
        return self.at(self.x, lax.rem(self.y + d, self.ny), self.z, self.core)

    def along_z(self, d):
        return self.at(self.x, self.y, lax.rem(self.z + d, self.nz), self.core)

    def other_core(self):
        return self.at(self.x, self.y, self.z, 1 - self.core)

    def along_tile(self, d):
        return (self.ens, lax.rem(self.tile + d + self.tiles, self.tiles))

    def along_ens(self, d):
        return (lax.rem(self.ens + d, 4), self.tile)

    def everyone(self):
        peers = [self.along_tile(1), self.along_tile(-1)]
        peers += [self.along_ens(d) for d in range(1, 4)]
        peers += [self.along_x(d) for d in range(1, self.nx)]
        peers += [self.along_y(d) for d in range(1, self.ny)]
        peers += [self.along_z(d) for d in range(1, self.nz)]
        return peers


def remote(src, dst, send, recv, to):
    return pltpu.make_async_remote_copy(
        src_ref=src,
        dst_ref=dst,
        send_sem=send,
        recv_sem=recv,
        device_id=to,
        device_id_type=pl.DeviceIdType.MESH,
    )


def far_first(size):
    return sorted(range(1, size), key=lambda d: -min(d, size - d))


def summed(parts):
    value = None
    for part in parts:
        part = part.astype(F32)
        value = part if value is None else value + part
    return value.astype(BF16)


def from_row(start, count):
    return pl.ds(pl.multiple_of(start, 16), count)


class Group:
    def __init__(self, owner, whole, apart=False):
        self.owner, self.whole, self.apart = owner, whole, apart
        self.send, self.recv = owner.send.at[owner.slot()], owner.recv.at[owner.slot()]
        self.copies = []
        owner.groups.append(self)

    def start(self, src, dst, to):
        recv = self.owner.recv.at[self.owner.slot()] if self.apart else self.recv
        copy = remote(src, dst, self.send, recv, to)
        copy.start()
        self.copies.append(copy)
        self.to = to

    def all(self):
        return remote(self.whole, self.whole, self.send, self.recv, self.to)

    def received(self):
        self.all().wait_recv()

    def sent(self):
        self.all().wait_send()


class Copies:
    def __init__(self, send, recv):
        self.send, self.recv = send, recv
        self.slots = 0
        self.groups = []

    def slot(self):
        self.slots += 1
        return self.slots - 1

    def one(self, src, dst, to):
        group = Group(self, src)
        group.start(src, dst, to)
        return group

    def keep(self, src, dst):
        copy = pltpu.make_async_copy(src, dst, self.send.at[self.slot()])
        copy.start()
        return copy

    def settle(self):
        for group in self.groups:
            group.sent()
        self.groups = []


class Reduce(Copies):
    def __init__(self, place, refs, out, third):
        self.third = third
        self.p = place
        self.g, self.rc, self.s1, self.r1, self.s2, self.r2, self.sz, self.rz, self.oz, *sems = refs
        super().__init__(*sems)
        self.out = out
        self.n, self.nz = place.nx, place.nz
        self.c_rows = HALF // 2
        self.p_rows = self.c_rows // self.n
        self.q_rows = self.p_rows // self.n
        self.z_rows = 2 * self.q_rows // self.nz
        self.order, self.z_order = far_first(self.n), far_first(self.nz)
        self.core = [None, None]
        self.in_first = [None, None]
        self.in_second = [None, None]

    def first(self, h):
        return self.p.x if h == 0 else self.p.y

    def second(self, h):
        return self.p.y if h == 0 else self.p.x

    def to_first(self, h, d):
        return self.p.along_x(d) if h == 0 else self.p.along_y(d)

    def to_second(self, h, d):
        return self.p.along_y(d) if h == 0 else self.p.along_x(d)

    def start_core(self, halves=(0, 1)):
        other = from_row((1 - self.p.core) * self.c_rows, self.c_rows)
        for h in halves:
            self.core[h] = self.one(self.g.at[h, other], self.rc.at[h], self.p.other_core())

    def core_to_first(self, halves=(0, 1)):
        for h in halves:
            self.core[h].received()
            group = self.in_first[h] = Group(self, self.r1.at[h])
            for d in (*self.order, 0):
                at = lax.rem(self.first(h) + d, self.n) * self.p_rows
                piece = from_row(at, self.p_rows)
                mine = from_row(self.p.core * self.c_rows + at, self.p_rows)
                self.s1[h, piece, :] = summed([self.g[h, mine, :], self.rc[h, piece, :]])
                if d:
                    group.start(self.s1.at[h, piece], self.r1.at[h, d - 1], self.to_first(h, d))

    def first_to_second(self, halves=(0, 1)):
        for h in halves:
            self.in_first[h].received()
            mine = self.s1[h, from_row(self.first(h) * self.p_rows, self.p_rows), :]
            self.s2[h] = summed([mine, *(self.r1[h, d] for d in range(self.n - 1))])
            group = self.in_second[h] = Group(self, self.r2.at[h])
            for d in self.order:
                piece = from_row(lax.rem(self.second(h) + d, self.n) * self.q_rows, self.q_rows)
                group.start(self.s2.at[h, piece], self.r2.at[h, d - 1], self.to_second(h, d))

    def second_to_z(self):
        for h in range(2):
            self.in_second[h].received()
            mine = self.s2[h, from_row(self.second(h) * self.q_rows, self.q_rows), :]
            self.sz[h * self.q_rows : (h + 1) * self.q_rows, :] = summed(
                [mine, *(self.r2[h, d] for d in range(self.n - 1))]
            )
        self.in_z = Group(self, self.rz)
        for d in self.z_order:
            piece = from_row(lax.rem(self.p.z + d, self.nz) * self.z_rows, self.z_rows)
            self.in_z.start(self.sz.at[piece], self.rz.at[d - 1], self.p.along_z(d))

    def z_to_gather(self):
        self.in_z.received()
        mine = from_row(self.p.z * self.z_rows, self.z_rows)
        self.oz[mine, :] = summed([self.sz[mine, :], *(self.rz[d] for d in range(self.nz - 1))])
        self.out_z = Group(self, self.oz.at[pl.ds(0, (self.nz - 1) * self.z_rows)])
        for d in self.z_order:
            self.out_z.start(self.oz.at[mine], self.oz.at[mine], self.p.along_z(d))

    def shard(self, h):
        return self.p.core * self.c_rows + self.first(h) * self.p_rows + self.second(h) * self.q_rows

    def gather_to_second(self):
        self.out_z.received()
        self.out_second = []
        self.kept = []
        for h in range(2):
            at = from_row(self.shard(h), self.q_rows)
            mine = self.oz.at[pl.ds(h * self.q_rows, self.q_rows)]
            group = Group(self, self.out.at[h, pl.ds(0, (self.n - 1) * self.q_rows)])
            self.out_second.append(group)
            for d in self.order:
                group.start(mine, self.out.at[h, at], self.to_second(h, d))
            self.kept.append(self.keep(mine, self.out.at[h, at]))

    def piece(self, h, d):
        at = lax.rem(self.first(h) + d, self.n) * self.p_rows
        return self.out.at[h, from_row(self.p.core * self.c_rows + at, self.p_rows)]

    def second_to_first(self):
        self.out_first = []
        self.out_core = []
        for h in range(2):
            self.out_second[h].received()
            self.kept[h].wait()
            mine = self.piece(h, 0)
            group = Group(self, self.out.at[h, pl.ds(0, (self.n - 1) * self.p_rows)], apart=True)
            self.out_first.append(group)
            for d in self.order:
                group.start(mine, mine, self.to_first(h, d))
            group = Group(self, self.out.at[h, pl.ds(0, self.c_rows)])
            self.out_core.append(group)
            group.start(mine, mine, self.p.other_core())

    def first_to_core(self):
        for k, d in enumerate(self.order):
            for h in range(2):
                self.out_first[h].copies[k].wait_recv()
                came = self.piece(h, self.n - d)
                self.out_core[h].start(came, came, self.p.other_core())

    def finish(self):
        self.settle()
        for group in self.out_core:
            group.received()


class Few(Copies):
    def __init__(self, place, refs, out):
        self.p = p = place
        self.g, self.rc, self.s, self.rx, self.sy, self.sz, self.o, *sems = refs
        super().__init__(*sems)
        self.out = out
        self.x_rows = FEW // p.nx

    def piece(self, d):
        return from_row(lax.rem(self.p.x + d, self.p.nx) * self.x_rows, self.x_rows)

    def start(self):
        self.got = self.one(self.g.at[1 - self.p.core], self.rc, self.p.other_core())

    def to_x(self):
        p = self.p
        self.got.received()
        self.s[...] = summed([self.g[p.core], self.rc[...]])
        self.got = Group(self, self.rx)
        for d in far_first(p.nx):
            self.got.start(self.s.at[self.piece(d)], self.rx.at[d - 1], p.along_x(d))

    def to_y(self):
        p = self.p
        self.got.received()
        self.sy[p.y] = summed([self.s[self.piece(0), :], *(self.rx[d] for d in range(p.nx - 1))])
        self.got = Group(self, self.sy.at[pl.ds(0, p.ny - 1)])
        for d in far_first(p.ny):
            self.got.start(self.sy.at[p.y], self.sy.at[p.y], p.along_y(d))

    def to_z(self):
        p = self.p
        self.got.received()
        self.sz[p.z] = summed(self.sy[k] for k in range(p.ny))
        self.got = Group(self, self.sz.at[pl.ds(0, p.nz - 1)])
        for d in far_first(p.nz):
            self.got.start(self.sz.at[p.z], self.sz.at[p.z], p.along_z(d))

    def to_gather(self):
        p = self.p
        self.got.received()
        self.o[...] = summed(self.sz[k] for k in range(p.nz))
        mine = self.out.at[p.core, self.piece(0)]
        self.kept = self.keep(self.o, mine)
        self.got = Group(self, self.out.at[0, pl.ds(0, (p.nx - 1) * self.x_rows)])
        for d in far_first(p.nx):
            self.got.start(self.o, mine, p.along_x(d))
        self.last = Group(self, self.out.at[0])
        self.last.start(self.o, mine, p.other_core())

    def to_core(self):
        p = self.p
        self.got.received()
        for d in range(1, p.nx):
            came = self.out.at[p.core, self.piece(d)]
            self.last.start(came, came, p.other_core())

    def finish(self):
        self.settle()
        self.kept.wait()
        self.last.received()


class Third(Copies):
    def __init__(self, place, refs, out):
        self.p = p = place
        self.g, self.rc, self.s1, self.r1, self.s2, self.r2, self.sy, self.o, *sems = refs
        super().__init__(*sems)
        self.out = out
        self.z_rows = THIRD // 2 // p.nz
        self.x_rows = self.z_rows // p.nx
        self.order = far_first(p.nz)

    def piece(self, d):
        return from_row(lax.rem(self.p.z + d, self.p.nz) * self.z_rows, self.z_rows)

    def start_core(self):
        self.got = self.one(self.g.at[1 - self.p.core], self.rc, self.p.other_core())

    def core_to_first(self):
        p = self.p
        self.got.received()
        self.s1[...] = summed([self.g[p.core], self.rc[...]])
        self.got = Group(self, self.r1)
        for d in self.order:
            self.got.start(self.s1.at[self.piece(d)], self.r1.at[d - 1], p.along_z(d))

    def first_to_second(self):
        p = self.p
        self.got.received()
        self.s2[...] = summed([self.s1[self.piece(0), :], *(self.r1[k] for k in range(p.nz - 1))])
        self.got = Group(self, self.r2)
        for d in far_first(p.nx):
            piece = from_row(lax.rem(p.x + d, p.nx) * self.x_rows, self.x_rows)
            self.got.start(self.s2.at[piece], self.r2.at[d - 1], p.along_x(d))

    def second_to_y(self):
        p = self.p
        self.got.received()
        mine = self.s2[from_row(p.x * self.x_rows, self.x_rows), :]
        self.sy[p.y] = summed([mine, *(self.r2[d] for d in range(p.nx - 1))])
        self.got = Group(self, self.sy.at[pl.ds(0, p.ny - 1)])
        for d in far_first(p.ny):
            self.got.start(self.sy.at[p.y], self.sy.at[p.y], p.along_y(d))

    def y_to_second(self):
        p = self.p
        self.got.received()
        self.o[...] = summed(self.sy[k] for k in range(p.ny))
        mine = self.out.at[p.core, from_row(p.z * self.z_rows + p.x * self.x_rows, self.x_rows)]
        self.kept = self.keep(self.o, mine)
        self.got = Group(self, self.out.at[0, pl.ds(0, (p.nx - 1) * self.x_rows)])
        for d in far_first(p.nx):
            self.got.start(self.o, mine, p.along_x(d))

    def second_to_first(self):
        p = self.p
        self.got.received()
        self.kept.wait()
        mine = self.out.at[p.core, self.piece(0)]
        self.got = Group(self, self.out.at[0, pl.ds(0, (p.nz - 1) * self.z_rows)])
        for d in self.order:
            self.got.start(mine, mine, p.along_z(d))

    def first_to_core(self):
        p = self.p
        self.got.received()
        self.last = self.one(self.out.at[p.core], self.out.at[p.core], p.other_core())

    def finish(self):
        self.settle()
        self.last.received()


def third_scratch(sizes):
    nx, ny, nzh = sizes
    nz = 2 * nzh
    z_rows = THIRD // 2 // nz
    x_rows = z_rows // nx
    shapes = [
        (2, THIRD // 2, 128), (THIRD // 2, 128), (THIRD // 2, 128), (nz - 1, z_rows, 128), (z_rows, 128),
        (nx - 1, x_rows, 128), (ny, x_rows, 128), (x_rows, 128),
    ]
    return [pltpu.VMEM(shape, BF16) for shape in shapes] + [pltpu.SemaphoreType.DMA((SLOTS,))] * 2


def few_scratch(sizes):
    nx, ny, nzh = sizes
    x_rows = FEW // nx
    shapes = [
        (2, FEW, 128), (FEW, 128), (FEW, 128), (nx - 1, x_rows, 128), (ny, x_rows, 128), (2 * nzh, x_rows, 128),
        (x_rows, 128),
    ]
    return [pltpu.VMEM(shape, BF16) for shape in shapes] + [pltpu.SemaphoreType.DMA((SLOTS,))] * 2


def reduce_scratch(sizes):
    n, _, nzh = sizes
    nz = 2 * nzh
    c_rows = HALF // 2
    p_rows = c_rows // n
    q_rows = p_rows // n
    z_rows = 2 * q_rows // nz
    shapes = [
        (2, HALF, 128), (2, c_rows, 128), (2, c_rows, 128), (2, n - 1, p_rows, 128), (2, p_rows, 128),
        (2, n - 1, q_rows, 128), (2 * q_rows, 128), (nz - 1, z_rows, 128), (2 * q_rows, 128),
    ]
    return [pltpu.VMEM(shape, BF16) for shape in shapes] + [pltpu.SemaphoreType.DMA((SLOTS,))] * 2


def slope_of(offset):
    return offset * lax.rsqrt(offset * offset + SMOOTHING * SMOOTHING)


def places(flat, count):
    at = 0
    while at < count:
        here = flat + at
        if here < HALF:
            take, part, row = HALF - here, 0, here
        elif here < HALF + 32 * MAIN:
            shard, inner = divmod(here - HALF, MAIN)
            take, part, row = MAIN - inner, 1, shard * SHARD + inner
        else:
            row = here - HALF - 32 * MAIN
            part, row = 2 + row // (THIRD // 2), row % (THIRD // 2)
            take = THIRD // 2 - row
        take = min(take, count - at)
        yield at, part, row, take
        at += take


def part_of(halves, third, part):
    return halves.at[part] if part < 2 else third.at[part - 2]


def put_main(batch, flat, value):
    for at, part, row, take in places(flat, value.shape[0]):
        part_of(batch.g, batch.third.g, part)[row : row + take, :] = value[at : at + take].astype(BF16)


def put_small(batch, index, value):
    batch[1, index * SHARD + MAIN : (index + 1) * SHARD, :] = value.astype(BF16)


def put_few(batch, index, value):
    batch[index // 6, index % 6 * 16 : index % 6 * 16 + 16, :] = value.astype(BF16)


def work(sizes, *refs):
    (
        x_hbm, target_hbm, sea_hbm, kernel_hbm, gain_hbm, expand_hbm, reduce_hbm, head_hbm,
        out1, third1, out2, third2, out3, direct_out,
        xb, target, tall, tg, sea, taps, gain, we, wr, head,
        ext, dext, rim, hs, hr, hs2, hr2, mixed, standard, recip, normed, before, slope, hidden, hidden_t, normed_t,
        block, head_t, fall, d_block, d_block_b, d_before, d_norm, gk,
        in_sems, halo_send, halo_recv, ens_send, ens_recv,
        *rest,
    ) = refs
    place = Place(sizes)
    few = Few(place, rest[-9:], out3)
    pieces = (len(rest) - 9) // 2
    batch1, batch2 = (
        Reduce(place, mine[:-10], out, Third(place, mine[-10:], third))
        for mine, out, third in ((rest[:pieces], out1, third1), (rest[pieces : 2 * pieces], out2, third2))
    )

    loads = [
        pltpu.make_async_copy(x_hbm.at[0, 0:8], xb.at[0:8], in_sems.at[0]),
        pltpu.make_async_copy(x_hbm.at[1, 0:8], xb.at[8:16], in_sems.at[1]),
        pltpu.make_async_copy(x_hbm.at[0, 8:12], xb.at[16:20], in_sems.at[2]),
        pltpu.make_async_copy(x_hbm.at[1, 8:12], xb.at[20:24], in_sems.at[3]),
    ]
    tap_loads = [
        pltpu.make_async_copy(kernel_hbm.at[:, :, l * 128 : (l + 1) * 128], taps.at[l], in_sems.at[4 + l])
        for l in range(LANES)
    ]
    later = [
        pltpu.make_async_copy(gain_hbm, gain, in_sems.at[7]),
        pltpu.make_async_copy(head_hbm, head, in_sems.at[8]),
        pltpu.make_async_copy(expand_hbm, we, in_sems.at[9]),
        pltpu.make_async_copy(reduce_hbm, wr, in_sems.at[10]),
        pltpu.make_async_copy(target_hbm, target, in_sems.at[11]),
        pltpu.make_async_copy(sea_hbm, sea, in_sems.at[12]),
    ]
    for copy in loads:
        copy.start()

    barrier = pltpu.get_barrier_semaphore()
    peers = place.everyone()
    for peer in peers:
        pl.semaphore_signal(barrier, inc=1, device_id=peer, device_id_type=pl.DeviceIdType.MESH)

    for copy in tap_loads + later:
        copy.start()

    def clear(i, _):
        l, m = lax.div(i, 2), lax.rem(i, 2)
        ext[l, m, 0:3] = jnp.zeros((3, 32, 128), F32)
        ext[l, m, 15:18] = jnp.zeros((3, 32, 128), F32)
        ext[l, m, 3:15, 0:8] = jnp.zeros((12, 8, 128), F32)
        ext[l, m, 3:15, 24:32] = jnp.zeros((12, 8, 128), F32)
        return 0

    lax.fori_loop(0, 2 * LANES, clear, 0)
    rim[...] = jnp.zeros_like(rim)
    for copy in loads:
        copy.wait()
    for l in range(LANES):
        lanes = slice(l * 128, (l + 1) * 128)
        for m in range(2):
            ext[l, m, 3:11, 8:24, :] = xb[m * 8 : m * 8 + 8, :, lanes].astype(F32)
            ext[l, m, 11:15, 8:24, :] = xb[16 + m * 4 : 20 + m * 4, :, lanes].astype(F32)

    def rim_rows(m, j):
        return slice((m * 3 + j) * 12, (m * 3 + j) * 12 + 12)

    def pack(field, out):
        for side, col in ((0, 8), (1, 21)):
            for m in range(2):
                for j in range(3):
                    for l in range(LANES):
                        rim[side, l, rim_rows(m, j)] = field[l, m, 3:15, col + j, :]
        out[...] = rim[...].astype(BF16)

    def unpack(field, got, l):
        for side, col in ((0, 5), (1, 24)):
            rim[side, l] = got[side, l].astype(F32)
            for m in range(2):
                for j in range(3):
                    field[l, m, 3:15, col + j, :] = rim[side, l, rim_rows(m, j)]

    def halo(out, got, at):
        copies = [
            [
                remote(out.at[side, l], got.at[1 - side, l], halo_send.at[at + s], halo_recv.at[at + s], place.along_tile(to))
                for s, (side, to) in enumerate(((0, -1), (1, 1)), 2 * l)
            ]
            for l in range(LANES)
        ]
        for pair in copies:
            for copy in pair:
                copy.start()
        return copies

    pack(ext, hs)
    pl.semaphore_wait(barrier, len(peers))
    halo1 = halo(hs, hr, 0)

    for copy in tap_loads:
        copy.wait()
    def correlate(field, l, m, flip):
        total = jnp.zeros((12, 16, 128), F32)
        for j in range(7):
            shifted = field[l, m, :, 5 + j : 21 + j, :]
            for i in range(7):
                tap = taps[l, 6 - i, 6 - j : 7 - j, :] if flip else taps[l, i, j : j + 1, :]
                total = total + shifted[i : i + 12] * tap
        return total

    def mix(i, _):
        l, m = lax.div(i, 2), lax.rem(i, 2)
        total = correlate(ext, l, m, False)
        mixed[l, pl.ds(m * 8, 8)] = total[:8]
        mixed[l, pl.ds(16 + m * 4, 4)] = total[8:]
        return 0

    lax.fori_loop(0, 2 * LANES, mix, 0)
    sublane = lax.broadcasted_iota(jnp.int32, (18, 8, 128), 1)

    def edges(l, m):
        for first, taps_in in ((0, (0, 1, 2)), (8, (4, 5, 6))):
            total = jnp.zeros((12, 8, 128), F32)
            for j in taps_in:
                outside = sublane < 3 - j if first == 0 else sublane >= 11 - j
                shifted = jnp.where(outside, ext[l, m, :, 5 + first + j : 13 + first + j, :], 0.0)
                for i in range(7):
                    total = total + shifted[i : i + 12] * taps[l, i, j : j + 1, :]
            mixed[l, pl.ds(m * 8, 8), first : first + 8] += total[:8]
            mixed[l, pl.ds(16 + m * 4, 4), first : first + 8] += total[8:]

    for l in range(LANES):
        for copy in halo1[l]:
            copy.wait_recv()
        unpack(ext, hr, l)
        lax.fori_loop(0, 2, lambda m, _, l=l: (edges(l, m), 0)[1], 0)

    for copy in later:
        copy.wait()
    outputs = head.shape[0]
    head_t[...] = jnp.concatenate([head[...].astype(F32), jnp.zeros((80 - outputs, D), F32)], axis=0).astype(BF16)
    gain_row = gain[...].reshape(1, D)

    def norm(i, _):
        rows = pl.ds(pl.multiple_of(i * 64, 64), 64)
        parts = [mixed[l, pl.ds(i * 4, 4)].reshape(64, 128) for l in range(LANES)]
        mean = jnp.sum(parts[0] + parts[1] + parts[2], axis=-1, keepdims=True) / D
        centre = [part - mean for part in parts]
        square = centre[0] * centre[0] + centre[1] * centre[1] + centre[2] * centre[2]
        scale = lax.rsqrt(jnp.sum(square, axis=-1, keepdims=True) / D + NORM_EPS)
        recip[rows, :] = jnp.broadcast_to(scale, (64, 128))
        for l in range(LANES):
            lanes = slice(l * 128, (l + 1) * 128)
            value = centre[l] * scale
            standard[rows, lanes] = value
            normed[rows, lanes] = (value * gain_row[:, lanes]).astype(BF16)
        return 0

    lax.fori_loop(0, 6, norm, 0, unroll=True)

    total = xb[...].reshape(D, D).astype(F32)
    for b in range(BLOCKS):
        columns = slice(b * BLOCK, (b + 1) * BLOCK)
        before[b] = dot(normed[...], we[:, columns], NN)

        def gelu(i, _, b=b, columns=columns):
            rows = pl.ds(pl.multiple_of(i * 32, 32), 32)
            v = before[b, rows, :]
            square = v * v
            scale = 0.7978845608028654
            t = jnp.tanh(v * (scale + (scale * 0.044715) * square))
            half = 0.5 + 0.5 * t
            hidden[rows, columns] = (v * half).astype(BF16)
            slope[rows, columns] = half + (0.5 * v) * (1.0 - t * t) * (scale + (scale * 3 * 0.044715) * square)
            return 0

        lax.fori_loop(0, 12, gelu, 0, unroll=True)
        total = total + dot(hidden[:, columns], wr[columns, :], NN)
    block[...] = total.astype(BF16)

    own = dot(head_t[...], block[...], NT)
    fall[0] = own
    far = place.along_ens(2)
    far_copies = [
        remote(fall.at[0, pl.ds(r, 40)], fall.at[2, pl.ds(r, 40)], ens_send.at[k], ens_recv.at[k], far)
        for k, r in enumerate((0, 40))
    ]
    near_copy = remote(fall.at[0], fall.at[1], ens_send.at[2], ens_recv.at[2], place.other_core())
    relays = [
        remote(fall.at[2, pl.ds(r, 40)], fall.at[3, pl.ds(r, 40)], ens_send.at[3 + k], ens_recv.at[3 + k], place.other_core())
        for k, r in enumerate((0, 40))
    ]
    for copy in [*far_copies, near_copy]:
        copy.start()
    for index in range(32):
        put_small(batch1.g, index, jnp.zeros((16, 128), F32))
        if index >= 15:
            put_small(batch2.g, index, jnp.zeros((16, 128), F32))
    gk[...] = jnp.zeros_like(gk)
    few.g[...] = jnp.zeros_like(few.g)

    def clear_back(i, _):
        l, m = lax.div(i, 2), lax.rem(i, 2)
        dext[l, m, 0:3] = jnp.zeros((3, 32, 128), F32)
        dext[l, m, 15:18] = jnp.zeros((3, 32, 128), F32)
        return 0

    lax.fori_loop(0, 2 * LANES, clear_back, 0)
    diagonal = lax.broadcasted_iota(jnp.int32, (16, 16), 0) == lax.broadcasted_iota(jnp.int32, (16, 16), 1)
    tall[...] = jnp.zeros_like(tall)
    for a in range(12):
        water = jnp.broadcast_to(sea[a : a + 1, :].astype(F32), (16, 16))
        water = jnp.sum(jnp.where(diagonal, water, 0.0), axis=1, keepdims=True)
        for at in (a * 16,) if a < 8 else (a * 16, a * 16 + 64):
            tall[at : at + 16, 0:outputs] = target[a]
            tall[at : at + 16, outputs : outputs + 1] = water
    tg[...] = tall[...].T[0:80]
    normed_t[...] = normed[...].T
    for b in range(BLOCKS):
        hidden_t[b * BLOCK : (b + 1) * BLOCK, :] = hidden[:, b * BLOCK : (b + 1) * BLOCK].T
    for came, relay in zip(far_copies, relays):
        came.wait_recv()
        relay.start()
    near_copy.wait_recv()

    spread = jnp.zeros((80, D), F32)
    for s in range(4):
        if s == 3:
            for copy in relays:
                copy.wait_recv()
        theirs = fall[s]
        swapped = jnp.concatenate(
            [theirs[:, 128:256], theirs[:, 0:128], pltpu.roll(theirs[:, 256:384], 64, 1)], axis=1
        )
        spread = spread + slope_of(own - theirs) + slope_of(own - swapped)
    observed = jnp.concatenate([tg[:, 0:128], tg[:, 0:128], tg[:, 128:256]], axis=1)
    ocean = observed[outputs : outputs + 1]
    slopes = slope_of(own - observed) / MEMBERS - FAIR_WEIGHT / (MEMBERS * (MEMBERS - 1)) * spread
    slopes_b = (slopes * ocean).astype(BF16)

    back = dot(slopes_b, head_t[...], TN)
    d_block[...] = back
    d_block_b[...] = back.astype(BF16)
    grad_reduce = dot(hidden_t[...], d_block_b[...], NN)
    for l in range(LANES):
        put_main(batch1, l * FFN, grad_reduce[:, l * 128 : (l + 1) * 128])
    batch1.start_core()
    batch1.third.start_core()

    grad_head = dot(slopes_b, block[...], NN)
    for r in range(5):
        for l in range(LANES):
            put_small(batch2.g, r * 3 + l, grad_head[r * 16 : r * 16 + 16, l * 128 : (l + 1) * 128])

    for b in range(BLOCKS):
        columns = slice(b * BLOCK, (b + 1) * BLOCK)
        before[b] = dot(d_block_b[...], wr[columns, :], NT)

        def gate(i, _, b=b, columns=columns):
            rows = pl.ds(pl.multiple_of(i * 32, 32), 32)
            d_before[rows, columns] = (before[b, rows, :] * slope[rows, columns]).astype(BF16)
            return 0

        lax.fori_loop(0, 12, gate, 0, unroll=True)
        grad_expand = dot(normed_t[...], d_before[:, columns], NN)
        for l in range(BLOCK // 128):
            put_main(batch2, (b * (BLOCK // 128) + l) * D, grad_expand[:, l * 128 : (l + 1) * 128])
        if b == 1:
            batch2.start_core((0,))
            batch1.core_to_first()
            batch1.third.core_to_first()
    batch2.start_core((1,))
    batch2.third.start_core()
    batch2.core_to_first((0,))
    d_norm[...] = dot(d_before[...], we[...], NT)
    batch2.core_to_first((1,))
    batch2.third.core_to_first()

    gk[0, 7:8, :] = jnp.zeros((1, 128), F32)

    def unnorm(i, _):
        rows = pl.ds(pl.multiple_of(i * 64, 64), 64)
        value = [d_norm[rows, l * 128 : (l + 1) * 128] for l in range(LANES)]
        std = [standard[rows, l * 128 : (l + 1) * 128] for l in range(LANES)]
        for l in range(LANES):
            gk[l, 7:8, :] += jnp.sum(value[l] * std[l], axis=0, keepdims=True)
        scaled = [value[l] * gain_row[:, l * 128 : (l + 1) * 128] for l in range(LANES)]
        mean = jnp.sum(scaled[0] + scaled[1] + scaled[2], axis=-1, keepdims=True) / D
        along = jnp.sum(scaled[0] * std[0] + scaled[1] * std[1] + scaled[2] * std[2], axis=-1, keepdims=True) / D
        for l in range(LANES):
            mixed[l, pl.ds(i * 4, 4)] = (recip[rows, :] * (scaled[l] - mean - std[l] * along)).reshape(4, 16, 128)
        return 0

    lax.fori_loop(0, 6, unnorm, 0, unroll=True)
    for l in range(LANES):
        for m in range(2):
            dext[l, m, 3:11, 8:24, :] = mixed[l, m * 8 : m * 8 + 8]
            dext[l, m, 11:15, 8:24, :] = mixed[l, 16 + m * 4 : 20 + m * 4]
    pack(dext, hs2)
    halo2 = halo(hs2, hr2, 6)

    def kernel_grad(l, _):
        for j in range(7):
            near = [ext[l, m, :, 5 + j : 21 + j, :] for m in range(2)]
            for i in range(7):
                part = jnp.zeros((16, 128), F32)
                for m in range(2):
                    part = part + jnp.sum(dext[l, m, 3:15, 8:24, :] * near[m][i : i + 12], axis=0)
                gk[l, i * 8 + j : i * 8 + j + 1, :] = jnp.sum(part, axis=0, keepdims=True)
        return 0

    batch1.first_to_second()
    batch2.first_to_second((0,))
    lax.fori_loop(0, 1, kernel_grad, 0)
    batch1.third.first_to_second()
    batch2.first_to_second((1,))
    batch1.second_to_z()
    lax.fori_loop(1, 2, kernel_grad, 0)
    batch2.third.first_to_second()
    lax.fori_loop(2, 3, kernel_grad, 0)
    count = jnp.sum(sea[...].astype(F32)).astype(jnp.int32)
    lane = lax.broadcasted_iota(jnp.int32, (1, 128), 1)
    bits = lax.bitwise_and(lax.shift_right_logical(jnp.broadcast_to(count, (1, 128)), jnp.minimum(lane, 31)), 1)
    gk[0, 15:16, :] = jnp.where(lane < COUNT_BITS, bits, 0).astype(F32)
    for r in range(4):
        for l in range(LANES):
            put_few(few.g, r * 3 + l, gk[l, r * 16 : r * 16 + 16, :])
    few.start()
    batch2.second_to_z()
    batch1.third.second_to_y()
    for l in range(LANES):
        for copy in halo2[l]:
            copy.wait_recv()
        unpack(dext, hr2, l)

    def mix_back(i, _):
        l, m = lax.div(i, 2), lax.rem(i, 2)
        mixed_back = correlate(dext, l, m, True)
        mixed[l, pl.ds(m * 8, 8)] = mixed_back[:8]
        mixed[l, pl.ds(16 + m * 4, 4)] = mixed_back[8:]
        return 0

    lax.fori_loop(0, 2, mix_back, 0)
    few.to_x()
    batch1.z_to_gather()
    batch2.third.second_to_y()
    lax.fori_loop(2, 4, mix_back, 0)
    batch1.third.y_to_second()
    batch2.z_to_gather()
    few.to_y()
    lax.fori_loop(4, 6, mix_back, 0)
    for l in range(LANES):
        lanes = slice(l * 128, (l + 1) * 128)
        mixed[l] = mixed[l] + d_block[:, lanes].reshape(24, 16, 128)
    direct = []
    for l in range(LANES):
        for m in range(2):
            lanes = slice(l * 128, (l + 1) * 128)
            at = (l * 2 + m) * 2
            direct.append(
                pltpu.make_async_copy(
                    mixed.at[l, m * 8 : m * 8 + 8], direct_out.at[m, 0:8, :, lanes], in_sems.at[at]
                )
            )
            direct.append(
                pltpu.make_async_copy(
                    mixed.at[l, 16 + m * 4 : 20 + m * 4], direct_out.at[m, 8:12, :, lanes], in_sems.at[at + 1]
                )
            )
    for copy in direct:
        copy.start()
    batch2.third.y_to_second()
    batch1.gather_to_second()
    few.to_z()
    batch1.third.second_to_first()
    batch2.gather_to_second()
    batch2.third.second_to_first()
    batch1.second_to_first()
    few.to_gather()
    batch2.second_to_first()
    batch1.third.first_to_core()
    few.to_core()
    batch1.first_to_core()
    batch2.third.first_to_core()
    batch2.first_to_core()
    for copy in sum(halo1 + halo2, []) + far_copies + [near_copy] + relays:
        copy.wait_send()
    for copy in direct:
        copy.wait()
    few.finish()
    for batch in (batch1, batch2):
        batch.third.finish()
        batch.finish()


def finish(
    o1, t1, o2, t2, o3, direct, g_inputs, g_kernel, g_gain, g_expand, g_reduce, g_head, kernel, gain, expand, reduce, head, sems
):
    copies = []

    def write(src, dst):
        copy = pltpu.make_async_copy(src, dst, sems.at[len(copies)])
        copy.start()
        copies.append(copy)

    def few(index):
        return o3[index // 6, index % 6 * 16 : index % 6 * 16 + 16, :].astype(F32)

    write(direct, g_inputs)
    rows = [[few(r * 3 + l) for l in range(LANES)] for r in range(4)]
    weight = lax.broadcasted_iota(jnp.int32, (1, 128), 1)
    weight = jnp.where(weight < COUNT_BITS, lax.shift_left(1, jnp.minimum(weight, 15)), 0).astype(F32)
    total = jnp.sum(rows[0][0][15:16] * weight, axis=-1, keepdims=True) / 4
    scale = 1.0 / total

    def main(halves, third, flat, count):
        for at, part, row, take in places(flat, count):
            yield at, take, part_of(halves, third, part)[row : row + take, :].astype(F32) * scale

    for r in range(0, FFN, 512):
        for l in range(LANES):
            for at, take, part in main(o1, t1, l * FFN + r, 512):
                reduce[r + at : r + at + take, l * 128 : (l + 1) * 128] = part
        write(reduce.at[r : r + 512], g_reduce.at[r : r + 512])
    for r in range(0, D, 128):
        for l in range(FFN // 128):
            for at, take, part in main(o2, t2, l * D + r, 128):
                expand[r + at : r + at + take, l * 128 : (l + 1) * 128] = part
        write(expand.at[r : r + 128], g_expand.at[r : r + 128])
    for l in range(LANES):
        lanes = slice(l * 128, (l + 1) * 128)
        for i in range(7):
            at = (i % 2) * 8
            kernel[i, :, lanes] = rows[i // 2][l][at : at + 7] * scale
        gain[lanes] = (rows[0][l][7:8] * scale).reshape(128)
        for r in range(5):
            index = r * 3 + l
            part = o2[1, index * SHARD + MAIN : (index + 1) * SHARD, :].astype(F32) * scale
            count = min(16, head.shape[0] - r * 16)
            head[r * 16 : r * 16 + count, lanes] = part[:count]
    write(kernel, g_kernel)
    write(gain, g_gain)
    write(head, g_head)
    for copy in copies:
        copy.wait()


def on_device(sizes, inputs, target, land_sea, kernel, norm_gain, w_expand, w_reduce, head_weight):
    outputs = target.shape[0]
    by_cell = jnp.transpose(target, (1, 2, 0))
    head_rows = head_weight.T
    anywhere = pl.BlockSpec(memory_space=pl.ANY)
    in_hbm = pl.BlockSpec(memory_space=pltpu.HBM)
    vmem = pltpu.VMEM
    scratch = [
        vmem((24, 16, D), BF16),
        vmem((12, 16, outputs), F32),
        vmem((256, 128), F32),
        vmem((80, 256), F32),
        vmem((12, 16), jnp.int32),
        vmem((LANES, 7, 7, 128), F32),
        vmem((D,), F32),
        vmem((D, FFN), BF16),
        vmem((FFN, D), BF16),
        vmem((outputs, D), BF16),
        vmem((LANES, 2, 18, 32, 128), F32),
        vmem((LANES, 2, 18, 32, 128), F32),
        vmem((2, LANES, 80, 128), F32),
        vmem((2, LANES, 80, 128), BF16),
        vmem((2, LANES, 80, 128), BF16),
        vmem((2, LANES, 80, 128), BF16),
        vmem((2, LANES, 80, 128), BF16),
        vmem((LANES, 24, 16, 128), F32),
        vmem((D, D), F32),
        vmem((D, 128), F32),
        vmem((D, D), BF16),
        vmem((BLOCKS, D, BLOCK), F32),
        vmem((D, FFN), F32),
        vmem((D, FFN), BF16),
        vmem((FFN, D), BF16),
        vmem((D, D), BF16),
        vmem((D, D), BF16),
        vmem((80, D), BF16),
        vmem((4, 80, D), F32),
        vmem((D, D), F32),
        vmem((D, D), BF16),
        vmem((D, FFN), BF16),
        vmem((D, D), F32),
        vmem((LANES, 64, 128), F32),
        pltpu.SemaphoreType.DMA((13,)),
        pltpu.SemaphoreType.DMA((12,)),
        pltpu.SemaphoreType.DMA((12,)),
        pltpu.SemaphoreType.DMA((5,)),
        pltpu.SemaphoreType.DMA((5,)),
    ]
    batch = reduce_scratch(sizes)
    batch = [*batch, *third_scratch(sizes)]
    scratch += batch + batch + few_scratch(sizes)
    operands = [inputs, by_cell, land_sea, kernel, norm_gain, w_expand, w_reduce, head_rows]
    operands = [pltpu.with_memory_space_constraint(operand, pltpu.HBM) for operand in operands]
    *reduced, direct = pl.pallas_call(
        lambda *refs: work(sizes, *refs),
        out_shape=(
            *(jax.ShapeDtypeStruct((2, rows, 128), BF16) for rows in (HALF, THIRD // 2, HALF, THIRD // 2, FEW)),
            jax.ShapeDtypeStruct(inputs.shape, F32),
        ),
        in_specs=[in_hbm] * 8,
        out_specs=(anywhere,) * 6,
        scratch_shapes=scratch,
        compiler_params=pltpu.CompilerParams(
            collective_id=0, has_side_effects=True, vmem_limit_bytes=48 * 1024 * 1024
        ),
        name="block_pass",
    )(*operands)
    in_vmem = pl.BlockSpec(memory_space=pltpu.VMEM)
    shapes = (kernel.shape, norm_gain.shape, w_expand.shape, w_reduce.shape, head_rows.shape)
    g_inputs, g_kernel, g_gain, g_expand, g_reduce, g_head = pl.pallas_call(
        finish,
        out_shape=tuple(jax.ShapeDtypeStruct(shape, F32) for shape in (inputs.shape, *shapes)),
        in_specs=[in_vmem] * 5 + [anywhere],
        out_specs=(anywhere,) * 6,
        scratch_shapes=[vmem(shape, F32) for shape in shapes] + [pltpu.SemaphoreType.DMA((11,))],
        compiler_params=pltpu.CompilerParams(vmem_limit_bytes=32 * 1024 * 1024),
        name="finish",
    )(*reduced, direct)
    return g_inputs, g_kernel, g_gain, g_expand, g_reduce, g_head.T


def solution(mesh):
    sizes = grid_of(mesh)
    return jax.shard_map(
        lambda *arrays: on_device(sizes, *arrays),
        mesh=mesh,
        in_specs=(
            P("ens", None, "tile", None),
            P(None, None, "tile"),
            P(None, "tile"),
            P(),
            P(),
            P(),
            P(),
            P(),
        ),
        out_specs=(P("ens", None, "tile", None), P(), P(), P(), P(), P()),
        check_vma=False,
    )
```

```python
import jax
import jax.numpy as jnp
from jax import lax
from jax.experimental import pallas as pl
from jax.experimental.pallas import tpu as pltpu
from jax.sharding import PartitionSpec as P

FAIR_WEIGHT = 0.95
SMOOTHING = 0.5
NORM_EPS = 1e-06
D = 384
FFN = 1536
LANES = 3
BLOCK = 512
BLOCKS = FFN // BLOCK
MEMBERS = 8
HALF = 2048
SHARD = 64
MAIN = 48
SLOTS = 48
THIRD = 1024
COUNT_BITS = 8
FEW = 128
F32 = jnp.float32
BF16 = jnp.bfloat16


def grid_of(mesh):
    tiles = mesh.shape["tile"]
    side = 4 if tiles == 64 else 2
    return side, side, tiles // (side * side)


def dot(a, b, dims):
    return lax.dot_general(a, b, (dims, ((), ())), preferred_element_type=F32)


NN = ((1,), (0,))
NT = ((1,), (1,))
TN = ((0,), (0,))


class Place:
    def __init__(self, sizes):
        self.nx, self.ny, self.nzh = sizes
        self.nz = 2 * self.nzh
        self.tiles = self.nx * self.ny * self.nzh
        self.ens = lax.axis_index("ens")
        self.tile = lax.axis_index("tile")
        self.core = lax.rem(self.ens, 2)
        self.zl = lax.div(self.ens, 2)
        self.zh = lax.rem(self.tile, self.nzh)
        self.x = lax.rem(lax.div(self.tile, self.nzh), self.nx)
        self.y = lax.div(self.tile, self.nzh * self.nx)
        self.z = self.zh * 2 + self.zl

    def at(self, x, y, z, core):
        return (lax.rem(z, 2) * 2 + core, (y * self.nx + x) * self.nzh + lax.div(z, 2))

    def along_x(self, d):
        return self.at(lax.rem(self.x + d, self.nx), self.y, self.z, self.core)

    def along_y(self, d):
        return self.at(self.x, lax.rem(self.y + d, self.ny), self.z, self.core)

    def along_z(self, d):
        return self.at(self.x, self.y, lax.rem(self.z + d, self.nz), self.core)

    def other_core(self):
        return self.at(self.x, self.y, self.z, 1 - self.core)

    def along_tile(self, d):
        return (self.ens, lax.rem(self.tile + d + self.tiles, self.tiles))

    def along_ens(self, d):
        return (lax.rem(self.ens + d, 4), self.tile)

    def everyone(self):
        peers = [self.along_tile(1), self.along_tile(-1)]
        peers += [self.along_ens(d) for d in range(1, 4)]
        peers += [self.along_x(d) for d in range(1, self.nx)]
        peers += [self.along_y(d) for d in range(1, self.ny)]
        peers += [self.along_z(d) for d in range(1, self.nz)]
        return peers


def remote(src, dst, send, recv, to):
    return pltpu.make_async_remote_copy(
        src_ref=src,
        dst_ref=dst,
        send_sem=send,
        recv_sem=recv,
        device_id=to,
        device_id_type=pl.DeviceIdType.MESH,
    )


def far_first(size):
    return sorted(range(1, size), key=lambda d: -min(d, size - d))


def summed(parts):
    value = None
    for part in parts:
        part = part.astype(F32)
        value = part if value is None else value + part
    return value.astype(BF16)


def from_row(start, count):
    return pl.ds(pl.multiple_of(start, 16), count)


class Group:
    def __init__(self, owner, whole, apart=False):
        self.owner, self.whole, self.apart = owner, whole, apart
        self.send, self.recv = owner.send.at[owner.slot()], owner.recv.at[owner.slot()]
        self.copies = []
        owner.groups.append(self)

    def start(self, src, dst, to):
        recv = self.owner.recv.at[self.owner.slot()] if self.apart else self.recv
        copy = remote(src, dst, self.send, recv, to)
        copy.start()
        self.copies.append(copy)
        self.to = to

    def all(self):
        return remote(self.whole, self.whole, self.send, self.recv, self.to)

    def received(self):
        self.all().wait_recv()

    def sent(self):
        self.all().wait_send()


class Copies:
    def __init__(self, send, recv):
        self.send, self.recv = send, recv
        self.slots = 0
        self.groups = []

    def slot(self):
        self.slots += 1
        return self.slots - 1

    def one(self, src, dst, to):
        group = Group(self, src)
        group.start(src, dst, to)
        return group

    def keep(self, src, dst):
        copy = pltpu.make_async_copy(src, dst, self.send.at[self.slot()])
        copy.start()
        return copy

    def settle(self):
        for group in self.groups:
            group.sent()
        self.groups = []


class Reduce(Copies):
    def __init__(self, place, refs, out, third):
        self.third = third
        self.p = place
        self.g, self.rc, self.s1, self.r1, self.s2, self.r2, self.sz, self.rz, self.oz, *sems = refs
        super().__init__(*sems)
        self.out = out
        self.n, self.nz = place.nx, place.nz
        self.c_rows = HALF // 2
        self.p_rows = self.c_rows // self.n
        self.q_rows = self.p_rows // self.n
        self.z_rows = 2 * self.q_rows // self.nz
        self.order, self.z_order = far_first(self.n), far_first(self.nz)
        self.core = [None, None]
        self.in_first = [None, None]
        self.in_second = [None, None]

    def first(self, h):
        return self.p.x if h == 0 else self.p.y

    def second(self, h):
        return self.p.y if h == 0 else self.p.x

    def to_first(self, h, d):
        return self.p.along_x(d) if h == 0 else self.p.along_y(d)

    def to_second(self, h, d):
        return self.p.along_y(d) if h == 0 else self.p.along_x(d)

    def start_core(self, halves=(0, 1)):
        other = from_row((1 - self.p.core) * self.c_rows, self.c_rows)
        for h in halves:
            self.core[h] = self.one(self.g.at[h, other], self.rc.at[h], self.p.other_core())

    def core_to_first(self, halves=(0, 1)):
        for h in halves:
            self.core[h].received()
            group = self.in_first[h] = Group(self, self.r1.at[h])
            for d in (*self.order, 0):
                at = lax.rem(self.first(h) + d, self.n) * self.p_rows
                piece = from_row(at, self.p_rows)
                mine = from_row(self.p.core * self.c_rows + at, self.p_rows)
                self.s1[h, piece, :] = summed([self.g[h, mine, :], self.rc[h, piece, :]])
                if d:
                    group.start(self.s1.at[h, piece], self.r1.at[h, d - 1], self.to_first(h, d))

    def first_to_second(self, halves=(0, 1)):
        for h in halves:
            self.in_first[h].received()
            mine = self.s1[h, from_row(self.first(h) * self.p_rows, self.p_rows), :]
            self.s2[h] = summed([mine, *(self.r1[h, d] for d in range(self.n - 1))])
            group = self.in_second[h] = Group(self, self.r2.at[h])
            for d in self.order:
                piece = from_row(lax.rem(self.second(h) + d, self.n) * self.q_rows, self.q_rows)
                group.start(self.s2.at[h, piece], self.r2.at[h, d - 1], self.to_second(h, d))

    def second_to_z(self):
        for h in range(2):
            self.in_second[h].received()
            mine = self.s2[h, from_row(self.second(h) * self.q_rows, self.q_rows), :]
            self.sz[h * self.q_rows : (h + 1) * self.q_rows, :] = summed(
                [mine, *(self.r2[h, d] for d in range(self.n - 1))]
            )
        self.in_z = Group(self, self.rz)
        for d in self.z_order:
            piece = from_row(lax.rem(self.p.z + d, self.nz) * self.z_rows, self.z_rows)
            self.in_z.start(self.sz.at[piece], self.rz.at[d - 1], self.p.along_z(d))

    def z_to_gather(self):
        self.in_z.received()
        mine = from_row(self.p.z * self.z_rows, self.z_rows)
        self.oz[mine, :] = summed([self.sz[mine, :], *(self.rz[d] for d in range(self.nz - 1))])
        self.out_z = Group(self, self.oz.at[pl.ds(0, (self.nz - 1) * self.z_rows)])
        for d in self.z_order:
            self.out_z.start(self.oz.at[mine], self.oz.at[mine], self.p.along_z(d))

    def shard(self, h):
        return self.p.core * self.c_rows + self.first(h) * self.p_rows + self.second(h) * self.q_rows

    def gather_to_second(self):
        self.out_z.received()
        self.out_second = []
        self.kept = []
        for h in range(2):
            at = from_row(self.shard(h), self.q_rows)
            mine = self.oz.at[pl.ds(h * self.q_rows, self.q_rows)]
            group = Group(self, self.out.at[h, pl.ds(0, (self.n - 1) * self.q_rows)])
            self.out_second.append(group)
            for d in self.order:
                group.start(mine, self.out.at[h, at], self.to_second(h, d))
            self.kept.append(self.keep(mine, self.out.at[h, at]))

    def piece(self, h, d):
        at = lax.rem(self.first(h) + d, self.n) * self.p_rows
        return self.out.at[h, from_row(self.p.core * self.c_rows + at, self.p_rows)]

    def second_to_first(self):
        self.out_first = []
        self.out_core = []
        for h in range(2):
            self.out_second[h].received()
            self.kept[h].wait()
            mine = self.piece(h, 0)
            group = Group(self, self.out.at[h, pl.ds(0, (self.n - 1) * self.p_rows)], apart=True)
            self.out_first.append(group)
            for d in self.order:
                group.start(mine, mine, self.to_first(h, d))
            group = Group(self, self.out.at[h, pl.ds(0, self.c_rows)])
            self.out_core.append(group)
            group.start(mine, mine, self.p.other_core())

    def first_to_core(self):
        for k, d in enumerate(self.order):
            for h in range(2):
                self.out_first[h].copies[k].wait_recv()
                came = self.piece(h, self.n - d)
                self.out_core[h].start(came, came, self.p.other_core())

    def finish(self):
        self.settle()
        for group in self.out_core:
            group.received()


class Few(Copies):
    def __init__(self, place, refs, out):
        self.p = p = place
        self.g, self.rc, self.s, self.rx, self.sy, self.sz, self.o, *sems = refs
        super().__init__(*sems)
        self.out = out
        self.x_rows = FEW // p.nx

    def piece(self, d):
        return from_row(lax.rem(self.p.x + d, self.p.nx) * self.x_rows, self.x_rows)

    def start(self):
        self.got = self.one(self.g.at[1 - self.p.core], self.rc, self.p.other_core())

    def to_x(self):
        p = self.p
        self.got.received()
        self.s[...] = summed([self.g[p.core], self.rc[...]])
        self.got = Group(self, self.rx)
        for d in far_first(p.nx):
            self.got.start(self.s.at[self.piece(d)], self.rx.at[d - 1], p.along_x(d))

    def to_y(self):
        p = self.p
        self.got.received()
        self.sy[p.y] = summed([self.s[self.piece(0), :], *(self.rx[d] for d in range(p.nx - 1))])
        self.got = Group(self, self.sy.at[pl.ds(0, p.ny - 1)])
        for d in far_first(p.ny):
            self.got.start(self.sy.at[p.y], self.sy.at[p.y], p.along_y(d))

    def to_z(self):
        p = self.p
        self.got.received()
        self.sz[p.z] = summed(self.sy[k] for k in range(p.ny))
        self.got = Group(self, self.sz.at[pl.ds(0, p.nz - 1)])
        for d in far_first(p.nz):
            self.got.start(self.sz.at[p.z], self.sz.at[p.z], p.along_z(d))

    def to_gather(self):
        p = self.p
        self.got.received()
        self.o[...] = summed(self.sz[k] for k in range(p.nz))
        mine = self.out.at[p.core, self.piece(0)]
        self.kept = self.keep(self.o, mine)
        self.got = Group(self, self.out.at[0, pl.ds(0, (p.nx - 1) * self.x_rows)])
        for d in far_first(p.nx):
            self.got.start(self.o, mine, p.along_x(d))
        self.last = Group(self, self.out.at[0])
        self.last.start(self.o, mine, p.other_core())

    def to_core(self):
        p = self.p
        self.got.received()
        for d in range(1, p.nx):
            came = self.out.at[p.core, self.piece(d)]
            self.last.start(came, came, p.other_core())

    def finish(self):
        self.settle()
        self.kept.wait()
        self.last.received()


class Third(Copies):
    def __init__(self, place, refs, out):
        self.p = p = place
        self.g, self.rc, self.s1, self.r1, self.s2, self.r2, self.sy, self.o, *sems = refs
        super().__init__(*sems)
        self.out = out
        self.z_rows = THIRD // 2 // p.nz
        self.x_rows = self.z_rows // p.nx
        self.order = far_first(p.nz)

    def piece(self, d):
        return from_row(lax.rem(self.p.z + d, self.p.nz) * self.z_rows, self.z_rows)

    def start_core(self):
        self.got = self.one(self.g.at[1 - self.p.core], self.rc, self.p.other_core())

    def core_to_first(self):
        p = self.p
        self.got.received()
        self.s1[...] = summed([self.g[p.core], self.rc[...]])
        self.got = Group(self, self.r1)
        for d in self.order:
            self.got.start(self.s1.at[self.piece(d)], self.r1.at[d - 1], p.along_z(d))

    def first_to_second(self):
        p = self.p
        self.got.received()
        self.s2[...] = summed([self.s1[self.piece(0), :], *(self.r1[k] for k in range(p.nz - 1))])
        self.got = Group(self, self.r2)
        for d in far_first(p.nx):
            piece = from_row(lax.rem(p.x + d, p.nx) * self.x_rows, self.x_rows)
            self.got.start(self.s2.at[piece], self.r2.at[d - 1], p.along_x(d))

    def second_to_y(self):
        p = self.p
        self.got.received()
        mine = self.s2[from_row(p.x * self.x_rows, self.x_rows), :]
        self.sy[p.y] = summed([mine, *(self.r2[d] for d in range(p.nx - 1))])
        self.got = Group(self, self.sy.at[pl.ds(0, p.ny - 1)])
        for d in far_first(p.ny):
            self.got.start(self.sy.at[p.y], self.sy.at[p.y], p.along_y(d))

    def y_to_second(self):
        p = self.p
        self.got.received()
        self.o[...] = summed(self.sy[k] for k in range(p.ny))
        mine = self.out.at[p.core, from_row(p.z * self.z_rows + p.x * self.x_rows, self.x_rows)]
        self.kept = self.keep(self.o, mine)
        self.got = Group(self, self.out.at[0, pl.ds(0, (p.nx - 1) * self.x_rows)])
        for d in far_first(p.nx):
            self.got.start(self.o, mine, p.along_x(d))

    def second_to_first(self):
        p = self.p
        self.got.received()
        self.kept.wait()
        mine = self.out.at[p.core, self.piece(0)]
        self.got = Group(self, self.out.at[0, pl.ds(0, (p.nz - 1) * self.z_rows)])
        for d in self.order:
            self.got.start(mine, mine, p.along_z(d))

    def first_to_core(self):
        p = self.p
        self.got.received()
        self.last = self.one(self.out.at[p.core], self.out.at[p.core], p.other_core())

    def finish(self):
        self.settle()
        self.last.received()


def third_scratch(sizes):
    nx, ny, nzh = sizes
    nz = 2 * nzh
    z_rows = THIRD // 2 // nz
    x_rows = z_rows // nx
    shapes = [
        (2, THIRD // 2, 128), (THIRD // 2, 128), (THIRD // 2, 128), (nz - 1, z_rows, 128), (z_rows, 128),
        (nx - 1, x_rows, 128), (ny, x_rows, 128), (x_rows, 128),
    ]
    return [pltpu.VMEM(shape, BF16) for shape in shapes] + [pltpu.SemaphoreType.DMA((SLOTS,))] * 2


def few_scratch(sizes):
    nx, ny, nzh = sizes
    x_rows = FEW // nx
    shapes = [
        (2, FEW, 128), (FEW, 128), (FEW, 128), (nx - 1, x_rows, 128), (ny, x_rows, 128), (2 * nzh, x_rows, 128),
        (x_rows, 128),
    ]
    return [pltpu.VMEM(shape, BF16) for shape in shapes] + [pltpu.SemaphoreType.DMA((SLOTS,))] * 2


def reduce_scratch(sizes):
    n, _, nzh = sizes
    nz = 2 * nzh
    c_rows = HALF // 2
    p_rows = c_rows // n
    q_rows = p_rows // n
    z_rows = 2 * q_rows // nz
    shapes = [
        (2, HALF, 128), (2, c_rows, 128), (2, c_rows, 128), (2, n - 1, p_rows, 128), (2, p_rows, 128),
        (2, n - 1, q_rows, 128), (2 * q_rows, 128), (nz - 1, z_rows, 128), (2 * q_rows, 128),
    ]
    return [pltpu.VMEM(shape, BF16) for shape in shapes] + [pltpu.SemaphoreType.DMA((SLOTS,))] * 2


def slope_of(offset):
    return offset * lax.rsqrt(offset * offset + SMOOTHING * SMOOTHING)


def places(flat, count):
    at = 0
    while at < count:
        here = flat + at
        if here < HALF:
            take, part, row = HALF - here, 0, here
        elif here < HALF + 32 * MAIN:
            shard, inner = divmod(here - HALF, MAIN)
            take, part, row = MAIN - inner, 1, shard * SHARD + inner
        else:
            row = here - HALF - 32 * MAIN
            part, row = 2 + row // (THIRD // 2), row % (THIRD // 2)
            take = THIRD // 2 - row
        take = min(take, count - at)
        yield at, part, row, take
        at += take


def part_of(halves, third, part):
    return halves.at[part] if part < 2 else third.at[part - 2]


def put_main(batch, flat, value):
    for at, part, row, take in places(flat, value.shape[0]):
        part_of(batch.g, batch.third.g, part)[row : row + take, :] = value[at : at + take].astype(BF16)


def put_small(batch, index, value):
    batch[1, index * SHARD + MAIN : (index + 1) * SHARD, :] = value.astype(BF16)


def put_few(batch, index, value):
    batch[index // 6, index % 6 * 16 : index % 6 * 16 + 16, :] = value.astype(BF16)


def work(sizes, *refs):
    (
        x_hbm, target_hbm, sea_hbm, kernel_hbm, gain_hbm, expand_hbm, reduce_hbm, head_hbm,
        out1, third1, out2, third2, out3, direct_out,
        xb, target, tall, tg, sea, taps, gain, we, wr, head,
        ext, dext, rim, hs, hr, hs2, hr2, mixed, standard, recip, normed, before, slope, hidden, hidden_t, normed_t,
        block, head_t, fall, d_block, d_block_b, d_before, d_norm, gk,
        in_sems, halo_send, halo_recv, ens_send, ens_recv,
        *rest,
    ) = refs
    place = Place(sizes)
    few = Few(place, rest[-9:], out3)
    pieces = (len(rest) - 9) // 2
    batch1, batch2 = (
        Reduce(place, mine[:-10], out, Third(place, mine[-10:], third))
        for mine, out, third in ((rest[:pieces], out1, third1), (rest[pieces : 2 * pieces], out2, third2))
    )

    loads = [
        pltpu.make_async_copy(x_hbm.at[0, 0:8], xb.at[0:8], in_sems.at[0]),
        pltpu.make_async_copy(x_hbm.at[1, 0:8], xb.at[8:16], in_sems.at[1]),
        pltpu.make_async_copy(x_hbm.at[0, 8:12], xb.at[16:20], in_sems.at[2]),
        pltpu.make_async_copy(x_hbm.at[1, 8:12], xb.at[20:24], in_sems.at[3]),
    ]
    tap_loads = [
        pltpu.make_async_copy(kernel_hbm.at[:, :, l * 128 : (l + 1) * 128], taps.at[l], in_sems.at[4 + l])
        for l in range(LANES)
    ]
    later = [
        pltpu.make_async_copy(gain_hbm, gain, in_sems.at[7]),
        pltpu.make_async_copy(head_hbm, head, in_sems.at[8]),
        pltpu.make_async_copy(expand_hbm, we, in_sems.at[9]),
        pltpu.make_async_copy(reduce_hbm, wr, in_sems.at[10]),
        pltpu.make_async_copy(target_hbm, target, in_sems.at[11]),
        pltpu.make_async_copy(sea_hbm, sea, in_sems.at[12]),
    ]
    for copy in loads:
        copy.start()

    barrier = pltpu.get_barrier_semaphore()
    peers = place.everyone()
    for peer in peers:
        pl.semaphore_signal(barrier, inc=1, device_id=peer, device_id_type=pl.DeviceIdType.MESH)

    for copy in tap_loads + later:
        copy.start()

    def clear(i, _):
        l, m = lax.div(i, 2), lax.rem(i, 2)
        ext[l, m, 0:3] = jnp.zeros((3, 32, 128), F32)
        ext[l, m, 15:18] = jnp.zeros((3, 32, 128), F32)
        ext[l, m, 3:15, 0:8] = jnp.zeros((12, 8, 128), F32)
        ext[l, m, 3:15, 24:32] = jnp.zeros((12, 8, 128), F32)
        return 0

    lax.fori_loop(0, 2 * LANES, clear, 0)
    rim[...] = jnp.zeros_like(rim)
    for copy in loads:
        copy.wait()
    for l in range(LANES):
        lanes = slice(l * 128, (l + 1) * 128)
        for m in range(2):
            ext[l, m, 3:11, 8:24, :] = xb[m * 8 : m * 8 + 8, :, lanes].astype(F32)
            ext[l, m, 11:15, 8:24, :] = xb[16 + m * 4 : 20 + m * 4, :, lanes].astype(F32)

    def rim_rows(m, j):
        return slice((m * 3 + j) * 12, (m * 3 + j) * 12 + 12)

    def pack(field, out):
        for side, col in ((0, 8), (1, 21)):
            for m in range(2):
                for j in range(3):
                    for l in range(LANES):
                        rim[side, l, rim_rows(m, j)] = field[l, m, 3:15, col + j, :]
        out[...] = rim[...].astype(BF16)

    def unpack(field, got, l):
        for side, col in ((0, 5), (1, 24)):
            rim[side, l] = got[side, l].astype(F32)
            for m in range(2):
                for j in range(3):
                    field[l, m, 3:15, col + j, :] = rim[side, l, rim_rows(m, j)]

    def halo(out, got, at):
        copies = [
            [
                remote(out.at[side, l], got.at[1 - side, l], halo_send.at[at + s], halo_recv.at[at + s], place.along_tile(to))
                for s, (side, to) in enumerate(((0, -1), (1, 1)), 2 * l)
            ]
            for l in range(LANES)
        ]
        for pair in copies:
            for copy in pair:
                copy.start()
        return copies

    pack(ext, hs)
    pl.semaphore_wait(barrier, len(peers))
    halo1 = halo(hs, hr, 0)

    for copy in tap_loads:
        copy.wait()
    def correlate(field, l, m, flip):
        total = jnp.zeros((12, 16, 128), F32)
        for j in range(7):
            shifted = field[l, m, :, 5 + j : 21 + j, :]
            for i in range(7):
                tap = taps[l, 6 - i, 6 - j : 7 - j, :] if flip else taps[l, i, j : j + 1, :]
                total = total + shifted[i : i + 12] * tap
        return total

    def mix(i, _):
        l, m = lax.div(i, 2), lax.rem(i, 2)
        total = correlate(ext, l, m, False)
        mixed[l, pl.ds(m * 8, 8)] = total[:8]
        mixed[l, pl.ds(16 + m * 4, 4)] = total[8:]
        return 0

    lax.fori_loop(0, 2 * LANES, mix, 0)
    sublane = lax.broadcasted_iota(jnp.int32, (18, 8, 128), 1)

    def edges(l, m):
        for first, taps_in in ((0, (0, 1, 2)), (8, (4, 5, 6))):
            total = jnp.zeros((12, 8, 128), F32)
            for j in taps_in:
                outside = sublane < 3 - j if first == 0 else sublane >= 11 - j
                shifted = jnp.where(outside, ext[l, m, :, 5 + first + j : 13 + first + j, :], 0.0)
                for i in range(7):
                    total = total + shifted[i : i + 12] * taps[l, i, j : j + 1, :]
            mixed[l, pl.ds(m * 8, 8), first : first + 8] += total[:8]
            mixed[l, pl.ds(16 + m * 4, 4), first : first + 8] += total[8:]

    for l in range(LANES):
        for copy in halo1[l]:
            copy.wait_recv()
        unpack(ext, hr, l)
        lax.fori_loop(0, 2, lambda m, _, l=l: (edges(l, m), 0)[1], 0, unroll=True)

    for copy in later:
        copy.wait()
    outputs = head.shape[0]
    head_t[...] = jnp.concatenate([head[...].astype(F32), jnp.zeros((80 - outputs, D), F32)], axis=0).astype(BF16)
    gain_row = gain[...].reshape(1, D)

    def norm(i, _):
        rows = pl.ds(pl.multiple_of(i * 64, 64), 64)
        parts = [mixed[l, pl.ds(i * 4, 4)].reshape(64, 128) for l in range(LANES)]
        mean = jnp.sum(parts[0] + parts[1] + parts[2], axis=-1, keepdims=True) / D
        centre = [part - mean for part in parts]
        square = centre[0] * centre[0] + centre[1] * centre[1] + centre[2] * centre[2]
        scale = lax.rsqrt(jnp.sum(square, axis=-1, keepdims=True) / D + NORM_EPS)
        recip[rows, :] = jnp.broadcast_to(scale, (64, 128))
        for l in range(LANES):
            lanes = slice(l * 128, (l + 1) * 128)
            value = centre[l] * scale
            standard[rows, lanes] = value
            normed[rows, lanes] = (value * gain_row[:, lanes]).astype(BF16)
        return 0

    lax.fori_loop(0, 6, norm, 0, unroll=True)

    total = xb[...].reshape(D, D).astype(F32)
    for b in range(BLOCKS):
        columns = slice(b * BLOCK, (b + 1) * BLOCK)
        before[b] = dot(normed[...], we[:, columns], NN)

        def gelu(i, _, b=b, columns=columns):
            rows = pl.ds(pl.multiple_of(i * 32, 32), 32)
            v = before[b, rows, :]
            square = v * v
            scale = 0.7978845608028654
            t = jnp.tanh(v * (scale + (scale * 0.044715) * square))
            half = 0.5 + 0.5 * t
            hidden[rows, columns] = (v * half).astype(BF16)
            slope[rows, columns] = half + (0.5 * v) * (1.0 - t * t) * (scale + (scale * 3 * 0.044715) * square)
            return 0

        lax.fori_loop(0, 12, gelu, 0, unroll=True)
        total = total + dot(hidden[:, columns], wr[columns, :], NN)
    block[...] = total.astype(BF16)

    own = dot(head_t[...], block[...], NT)
    fall[0] = own
    far = place.along_ens(2)
    far_copies = [
        remote(fall.at[0, pl.ds(r, 40)], fall.at[2, pl.ds(r, 40)], ens_send.at[k], ens_recv.at[k], far)
        for k, r in enumerate((0, 40))
    ]
    near_copy = remote(fall.at[0], fall.at[1], ens_send.at[2], ens_recv.at[2], place.other_core())
    relays = [
        remote(fall.at[2, pl.ds(r, 40)], fall.at[3, pl.ds(r, 40)], ens_send.at[3 + k], ens_recv.at[3 + k], place.other_core())
        for k, r in enumerate((0, 40))
    ]
    for copy in [*far_copies, near_copy]:
        copy.start()
    for index in range(32):
        put_small(batch1.g, index, jnp.zeros((16, 128), F32))
        if index >= 15:
            put_small(batch2.g, index, jnp.zeros((16, 128), F32))
    gk[...] = jnp.zeros_like(gk)
    few.g[...] = jnp.zeros_like(few.g)

    def clear_back(i, _):
        l, m = lax.div(i, 2), lax.rem(i, 2)
        dext[l, m, 0:3] = jnp.zeros((3, 32, 128), F32)
        dext[l, m, 15:18] = jnp.zeros((3, 32, 128), F32)
        return 0

    lax.fori_loop(0, 2 * LANES, clear_back, 0)
    diagonal = lax.broadcasted_iota(jnp.int32, (16, 16), 0) == lax.broadcasted_iota(jnp.int32, (16, 16), 1)
    tall[...] = jnp.zeros_like(tall)
    for a in range(12):
        water = jnp.broadcast_to(sea[a : a + 1, :].astype(F32), (16, 16))
        water = jnp.sum(jnp.where(diagonal, water, 0.0), axis=1, keepdims=True)
        for at in (a * 16,) if a < 8 else (a * 16, a * 16 + 64):
            tall[at : at + 16, 0:outputs] = target[a]
            tall[at : at + 16, outputs : outputs + 1] = water
    tg[...] = tall[...].T[0:80]
    normed_t[...] = normed[...].T
    for b in range(BLOCKS):
        hidden_t[b * BLOCK : (b + 1) * BLOCK, :] = hidden[:, b * BLOCK : (b + 1) * BLOCK].T
    for came, relay in zip(far_copies, relays):
        came.wait_recv()
        relay.start()
    near_copy.wait_recv()

    spread = jnp.zeros((80, D), F32)
    for s in range(4):
        if s == 3:
            for copy in relays:
                copy.wait_recv()
        theirs = fall[s]
        swapped = jnp.concatenate(
            [theirs[:, 128:256], theirs[:, 0:128], pltpu.roll(theirs[:, 256:384], 64, 1)], axis=1
        )
        spread = spread + slope_of(own - theirs) + slope_of(own - swapped)
    observed = jnp.concatenate([tg[:, 0:128], tg[:, 0:128], tg[:, 128:256]], axis=1)
    ocean = observed[outputs : outputs + 1]
    slopes = slope_of(own - observed) / MEMBERS - FAIR_WEIGHT / (MEMBERS * (MEMBERS - 1)) * spread
    slopes_b = (slopes * ocean).astype(BF16)

    back = dot(slopes_b, head_t[...], TN)
    d_block[...] = back
    d_block_b[...] = back.astype(BF16)
    grad_reduce = dot(hidden_t[...], d_block_b[...], NN)
    for l in range(LANES):
        put_main(batch1, l * FFN, grad_reduce[:, l * 128 : (l + 1) * 128])
    batch1.start_core()
    batch1.third.start_core()

    grad_head = dot(slopes_b, block[...], NN)
    for r in range(5):
        for l in range(LANES):
            put_small(batch2.g, r * 3 + l, grad_head[r * 16 : r * 16 + 16, l * 128 : (l + 1) * 128])

    for b in range(BLOCKS):
        columns = slice(b * BLOCK, (b + 1) * BLOCK)
        before[b] = dot(d_block_b[...], wr[columns, :], NT)

        def gate(i, _, b=b, columns=columns):
            rows = pl.ds(pl.multiple_of(i * 32, 32), 32)
            d_before[rows, columns] = (before[b, rows, :] * slope[rows, columns]).astype(BF16)
            return 0

        lax.fori_loop(0, 12, gate, 0, unroll=True)
        grad_expand = dot(normed_t[...], d_before[:, columns], NN)
        for l in range(BLOCK // 128):
            put_main(batch2, (b * (BLOCK // 128) + l) * D, grad_expand[:, l * 128 : (l + 1) * 128])
        if b == 1:
            batch2.start_core((0,))
            batch1.core_to_first()
            batch1.third.core_to_first()
    batch2.start_core((1,))
    batch2.third.start_core()
    batch2.core_to_first((0,))
    d_norm[...] = dot(d_before[...], we[...], NT)
    batch2.core_to_first((1,))
    batch2.third.core_to_first()

    gk[0, 7:8, :] = jnp.zeros((1, 128), F32)

    def unnorm(i, _):
        rows = pl.ds(pl.multiple_of(i * 64, 64), 64)
        value = [d_norm[rows, l * 128 : (l + 1) * 128] for l in range(LANES)]
        std = [standard[rows, l * 128 : (l + 1) * 128] for l in range(LANES)]
        for l in range(LANES):
            gk[l, 7:8, :] += jnp.sum(value[l] * std[l], axis=0, keepdims=True)
        scaled = [value[l] * gain_row[:, l * 128 : (l + 1) * 128] for l in range(LANES)]
        mean = jnp.sum(scaled[0] + scaled[1] + scaled[2], axis=-1, keepdims=True) / D
        along = jnp.sum(scaled[0] * std[0] + scaled[1] * std[1] + scaled[2] * std[2], axis=-1, keepdims=True) / D
        for l in range(LANES):
            mixed[l, pl.ds(i * 4, 4)] = (recip[rows, :] * (scaled[l] - mean - std[l] * along)).reshape(4, 16, 128)
        return 0

    lax.fori_loop(0, 6, unnorm, 0, unroll=True)
    for l in range(LANES):
        for m in range(2):
            dext[l, m, 3:11, 8:24, :] = mixed[l, m * 8 : m * 8 + 8]
            dext[l, m, 11:15, 8:24, :] = mixed[l, 16 + m * 4 : 20 + m * 4]
    pack(dext, hs2)
    halo2 = halo(hs2, hr2, 6)

    def kernel_grad(l, _):
        for j in range(7):
            near = [ext[l, m, :, 5 + j : 21 + j, :] for m in range(2)]
            for i in range(7):
                part = jnp.zeros((16, 128), F32)
                for m in range(2):
                    part = part + jnp.sum(dext[l, m, 3:15, 8:24, :] * near[m][i : i + 12], axis=0)
                gk[l, i * 8 + j : i * 8 + j + 1, :] = jnp.sum(part, axis=0, keepdims=True)
        return 0

    batch1.first_to_second()
    batch2.first_to_second((0,))
    lax.fori_loop(0, 1, kernel_grad, 0)
    batch1.third.first_to_second()
    batch2.first_to_second((1,))
    batch1.second_to_z()
    lax.fori_loop(1, 2, kernel_grad, 0)
    batch2.third.first_to_second()
    lax.fori_loop(2, 3, kernel_grad, 0)
    count = jnp.sum(sea[...].astype(F32)).astype(jnp.int32)
    lane = lax.broadcasted_iota(jnp.int32, (1, 128), 1)
    bits = lax.bitwise_and(lax.shift_right_logical(jnp.broadcast_to(count, (1, 128)), jnp.minimum(lane, 31)), 1)
    gk[0, 15:16, :] = jnp.where(lane < COUNT_BITS, bits, 0).astype(F32)
    for r in range(4):
        for l in range(LANES):
            put_few(few.g, r * 3 + l, gk[l, r * 16 : r * 16 + 16, :])
    few.start()
    batch2.second_to_z()
    batch1.third.second_to_y()
    for l in range(LANES):
        for copy in halo2[l]:
            copy.wait_recv()
        unpack(dext, hr2, l)

    def mix_back(i, _):
        l, m = lax.div(i, 2), lax.rem(i, 2)
        mixed_back = correlate(dext, l, m, True)
        mixed[l, pl.ds(m * 8, 8)] = mixed_back[:8]
        mixed[l, pl.ds(16 + m * 4, 4)] = mixed_back[8:]
        return 0

    lax.fori_loop(0, 2, mix_back, 0)
    few.to_x()
    batch1.z_to_gather()
    batch2.third.second_to_y()
    lax.fori_loop(2, 4, mix_back, 0)
    batch1.third.y_to_second()
    batch2.z_to_gather()
    few.to_y()
    lax.fori_loop(4, 6, mix_back, 0)
    for l in range(LANES):
        lanes = slice(l * 128, (l + 1) * 128)
        mixed[l] = mixed[l] + d_block[:, lanes].reshape(24, 16, 128)
    direct = []
    for l in range(LANES):
        for m in range(2):
            lanes = slice(l * 128, (l + 1) * 128)
            at = (l * 2 + m) * 2
            direct.append(
                pltpu.make_async_copy(
                    mixed.at[l, m * 8 : m * 8 + 8], direct_out.at[m, 0:8, :, lanes], in_sems.at[at]
                )
            )
            direct.append(
                pltpu.make_async_copy(
                    mixed.at[l, 16 + m * 4 : 20 + m * 4], direct_out.at[m, 8:12, :, lanes], in_sems.at[at + 1]
                )
            )
    for copy in direct:
        copy.start()
    batch2.third.y_to_second()
    batch1.gather_to_second()
    few.to_z()
    batch1.third.second_to_first()
    batch2.gather_to_second()
    batch2.third.second_to_first()
    batch1.second_to_first()
    few.to_gather()
    batch2.second_to_first()
    batch1.third.first_to_core()
    few.to_core()
    batch1.first_to_core()
    batch2.third.first_to_core()
    batch2.first_to_core()
    for copy in sum(halo1 + halo2, []) + far_copies + [near_copy] + relays:
        copy.wait_send()
    for copy in direct:
        copy.wait()
    few.finish()
    for batch in (batch1, batch2):
        batch.third.finish()
        batch.finish()


def finish(
    o1, t1, o2, t2, o3, direct, g_inputs, g_kernel, g_gain, g_expand, g_reduce, g_head, kernel, gain, expand, reduce, head, sems
):
    copies = []

    def write(src, dst):
        copy = pltpu.make_async_copy(src, dst, sems.at[len(copies)])
        copy.start()
        copies.append(copy)

    def few(index):
        return o3[index // 6, index % 6 * 16 : index % 6 * 16 + 16, :].astype(F32)

    write(direct, g_inputs)
    rows = [[few(r * 3 + l) for l in range(LANES)] for r in range(4)]
    weight = lax.broadcasted_iota(jnp.int32, (1, 128), 1)
    weight = jnp.where(weight < COUNT_BITS, lax.shift_left(1, jnp.minimum(weight, 15)), 0).astype(F32)
    total = jnp.sum(rows[0][0][15:16] * weight, axis=-1, keepdims=True) / 4
    scale = 1.0 / total

    def main(halves, third, flat, count):
        for at, part, row, take in places(flat, count):
            yield at, take, part_of(halves, third, part)[row : row + take, :].astype(F32) * scale

    for r in range(0, FFN, 512):
        for l in range(LANES):
            for at, take, part in main(o1, t1, l * FFN + r, 512):
                reduce[r + at : r + at + take, l * 128 : (l + 1) * 128] = part
        write(reduce.at[r : r + 512], g_reduce.at[r : r + 512])
    for r in range(0, D, 128):
        for l in range(FFN // 128):
            for at, take, part in main(o2, t2, l * D + r, 128):
                expand[r + at : r + at + take, l * 128 : (l + 1) * 128] = part
        write(expand.at[r : r + 128], g_expand.at[r : r + 128])
    for l in range(LANES):
        lanes = slice(l * 128, (l + 1) * 128)
        for i in range(7):
            at = (i % 2) * 8
            kernel[i, :, lanes] = rows[i // 2][l][at : at + 7] * scale
        gain[lanes] = (rows[0][l][7:8] * scale).reshape(128)
        for r in range(5):
            index = r * 3 + l
            part = o2[1, index * SHARD + MAIN : (index + 1) * SHARD, :].astype(F32) * scale
            count = min(16, head.shape[0] - r * 16)
            head[r * 16 : r * 16 + count, lanes] = part[:count]
    write(kernel, g_kernel)
    write(gain, g_gain)
    write(head, g_head)
    for copy in copies:
        copy.wait()


def on_device(sizes, inputs, target, land_sea, kernel, norm_gain, w_expand, w_reduce, head_weight):
    outputs = target.shape[0]
    by_cell = jnp.transpose(target, (1, 2, 0))
    head_rows = head_weight.T
    anywhere = pl.BlockSpec(memory_space=pl.ANY)
    in_hbm = pl.BlockSpec(memory_space=pltpu.HBM)
    vmem = pltpu.VMEM
    scratch = [
        vmem((24, 16, D), BF16),
        vmem((12, 16, outputs), F32),
        vmem((256, 128), F32),
        vmem((80, 256), F32),
        vmem((12, 16), jnp.int32),
        vmem((LANES, 7, 7, 128), F32),
        vmem((D,), F32),
        vmem((D, FFN), BF16),
        vmem((FFN, D), BF16),
        vmem((outputs, D), BF16),
        vmem((LANES, 2, 18, 32, 128), F32),
        vmem((LANES, 2, 18, 32, 128), F32),
        vmem((2, LANES, 80, 128), F32),
        vmem((2, LANES, 80, 128), BF16),
        vmem((2, LANES, 80, 128), BF16),
        vmem((2, LANES, 80, 128), BF16),
        vmem((2, LANES, 80, 128), BF16),
        vmem((LANES, 24, 16, 128), F32),
        vmem((D, D), F32),
        vmem((D, 128), F32),
        vmem((D, D), BF16),
        vmem((BLOCKS, D, BLOCK), F32),
        vmem((D, FFN), F32),
        vmem((D, FFN), BF16),
        vmem((FFN, D), BF16),
        vmem((D, D), BF16),
        vmem((D, D), BF16),
        vmem((80, D), BF16),
        vmem((4, 80, D), F32),
        vmem((D, D), F32),
        vmem((D, D), BF16),
        vmem((D, FFN), BF16),
        vmem((D, D), F32),
        vmem((LANES, 64, 128), F32),
        pltpu.SemaphoreType.DMA((13,)),
        pltpu.SemaphoreType.DMA((12,)),
        pltpu.SemaphoreType.DMA((12,)),
        pltpu.SemaphoreType.DMA((5,)),
        pltpu.SemaphoreType.DMA((5,)),
    ]
    batch = reduce_scratch(sizes)
    batch = [*batch, *third_scratch(sizes)]
    scratch += batch + batch + few_scratch(sizes)
    operands = [inputs, by_cell, land_sea, kernel, norm_gain, w_expand, w_reduce, head_rows]
    operands = [pltpu.with_memory_space_constraint(operand, pltpu.HBM) for operand in operands]
    *reduced, direct = pl.pallas_call(
        lambda *refs: work(sizes, *refs),
        out_shape=(
            *(jax.ShapeDtypeStruct((2, rows, 128), BF16) for rows in (HALF, THIRD // 2, HALF, THIRD // 2, FEW)),
            jax.ShapeDtypeStruct(inputs.shape, F32),
        ),
        in_specs=[in_hbm] * 8,
        out_specs=(anywhere,) * 6,
        scratch_shapes=scratch,
        compiler_params=pltpu.CompilerParams(
            collective_id=0, has_side_effects=True, vmem_limit_bytes=48 * 1024 * 1024
        ),
        name="block_pass",
    )(*operands)
    in_vmem = pl.BlockSpec(memory_space=pltpu.VMEM)
    shapes = (kernel.shape, norm_gain.shape, w_expand.shape, w_reduce.shape, head_rows.shape)
    g_inputs, g_kernel, g_gain, g_expand, g_reduce, g_head = pl.pallas_call(
        finish,
        out_shape=tuple(jax.ShapeDtypeStruct(shape, F32) for shape in (inputs.shape, *shapes)),
        in_specs=[in_vmem] * 5 + [anywhere],
        out_specs=(anywhere,) * 6,
        scratch_shapes=[vmem(shape, F32) for shape in shapes] + [pltpu.SemaphoreType.DMA((11,))],
        compiler_params=pltpu.CompilerParams(vmem_limit_bytes=32 * 1024 * 1024),
        name="finish",
    )(*reduced, direct)
    return g_inputs, g_kernel, g_gain, g_expand, g_reduce, g_head.T


def solution(mesh):
    sizes = grid_of(mesh)
    return jax.shard_map(
        lambda *arrays: on_device(sizes, *arrays),
        mesh=mesh,
        in_specs=(
            P("ens", None, "tile", None),
            P(None, None, "tile"),
            P(None, "tile"),
            P(),
            P(),
            P(),
            P(),
            P(),
        ),
        out_specs=(P("ens", None, "tile", None), P(), P(), P(), P(), P()),
        check_vma=False,
    )
```
